256 devices in a mesh: tm: 16 (over x, y), space: 16 (over z, core).
Axes of the slice: x: 4, y: 4, z: 8, core: 2. Of those that a mesh axis runs over, the one named last changes fastest.
Arguments:
- courant_x: float32 [16, 4, 128, 3072], P('tm', None, 'space'), may hold values from -0.45 to 0.45
- courant_y: float32 [16, 4, 128, 3072], P('tm', None, 'space'), may hold values from -0.45 to 0.45
- model_var: float32 [16, 4, 128, 3072], P('tm', None, 'space'), may hold values from 0.2 to 2
- obs_var: float32 [16, 16384], P('tm', 'space'), may hold values from 0.25 to 4
- obs_brick: int32 [16, 16384], P('tm'), may hold values from 0 to 15
- obs_cell: int32 [16, 16384], P('tm'), may hold values from 0 to 98303
- obs_step: int32 [16, 16384], P('tm'), may hold values from 0 to 1
- dual_state: float32 [16, 4, 128, 3072], P('tm', None, 'space'), may hold values from -6 to 6
- dual_obs: float32 [16, 16384], P('tm', 'space'), may hold values from -6 to 6
- increment: float32 [16, 4, 128, 3072], P('tm', None, 'space'), may hold values from -6 to 6
- resid_model: float32 [16, 4, 128, 3072], P('tm', None, 'space'), may hold values from -6 to 6
- resid_obs: float32 [16, 16384], P('tm', 'space'), may hold values from -6 to 6
- resid_state: float32 [16, 4, 128, 3072], P('tm', None, 'space'), may hold values from -6 to 6
Outputs:
- new_dual_state: float32 [16, 4, 128, 3072], P('tm', None, 'space')
- new_dual_obs: float32 [16, 16384], P('tm', 'space')
- new_increment: float32 [16, 4, 128, 3072], P('tm', None, 'space')
- new_resid_model: float32 [16, 4, 128, 3072], P('tm', None, 'space')
- new_resid_obs: float32 [16, 16384], P('tm', 'space')
- new_resid_state: float32 [16, 4, 128, 3072], P('tm', None, 'space')
The draws below stay inside these ranges and needn't reach their ends.
Inputs may be any that keep to these rules, and one draw needn't show every extreme that they name: `obs_brick`: index of the brick of 8 rows that holds the observation. `obs_cell`: cell within the brick, levels slowest, then rows, then columns. `obs_step`: 0: taken at the sub-window's start; 1: after its first advection step.
All inputs are finite; a program needn't handle non-finite values.
Results may differ from the reference program's by a relative error of at most 0.00005.
Values sent between devices are 32-bit elements; how exact they have to be, the bound alone decides.
No kernel may reach another device: no remote copies, remote signals or barrier semaphores. Data moves between devices by JAX's collectives and lax.ppermute only.
A program may use at most 128 MiB of HBM per device.

```python
import math
import jax
import jax.numpy as jnp

LEV = 4
NX = 3072
ROWS_DEV = 8
NT = 16
BRICKS = 16
NY = 128
NOBS = 16384
BRICK_CELLS = 98304


def place_ends(drawn, stream_key, least, top_value):
    index_at = [jax.random.randint(jax.random.fold_in(stream_key, axis), (), 0, length) for axis, length in enumerate(drawn.shape)]
    widest = drawn.shape.index(max(drawn.shape))
    neighbour = index_at[:widest] + [(index_at[widest] + 1) % drawn.shape[widest]] + index_at[widest + 1:]
    return drawn.at[tuple(index_at)].set(least).at[tuple(neighbour)].set(top_value)


def steps_of(stream_key, extent, split, least, top_value):
    gain, own = 1.0, jax.random.fold_in(stream_key, 6)
    for position, blocks in split:
        heights = jnp.exp(jax.random.uniform(jax.random.fold_in(own, position), (blocks,), jnp.float32, least / len(split), top_value / len(split)))
        gain = gain * jnp.repeat(heights, extent[position] // blocks).reshape([-1 if axis == position else 1 for axis in range(len(extent))])
    return gain


def normal_values(key, extent, spread, reach, shards=(), kind=jnp.bfloat16):
    result = jax.random.normal(key, extent, jnp.float32) * spread
    if len(shards) > 0:
        result = steps_of(key, extent, shards, -0.22, 0.18) * result
    return jnp.clip(result, min=-reach, max=reach).astype(kind)


def setup_inputs(seed: int = 0) -> dict:
    seeds = jax.random.split(jax.random.key(seed), 14)
    courant_x = jnp.clip(jax.random.uniform(seeds[0], (NT, LEV, NY, NX), jnp.float32, -0.45, 0.45) * steps_of(seeds[0], (NT, LEV, NY, NX), ((0, 16), (2, 16)), -0.4, 0.0), -0.45, 0.45)
    courant_y = jnp.clip(jax.random.uniform(seeds[1], (NT, LEV, NY, NX), jnp.float32, -0.45, 0.45) * steps_of(seeds[1], (NT, LEV, NY, NX), ((0, 16), (2, 16)), -0.4, 0.0), -0.45, 0.45)
    model_var = jnp.clip(jnp.exp(math.log(2.0) - 2.3025851 * jax.random.uniform(seeds[2], (NT, LEV, NY, NX), jnp.float32) ** steps_of(seeds[2], (NT, LEV, NY, NX), ((0, 16), (2, 16)), -0.2, 0.2)), 0.2, 2.0)
    obs_var = jnp.clip(jnp.exp(math.log(4.0) - 2.7725887 * jax.random.uniform(seeds[3], (NT, NOBS), jnp.float32) ** steps_of(seeds[3], (NT, NOBS), ((0, 16), (1, 16)), -0.2, 0.2)), 0.25, 4.0)
    obs_brick = place_ends(jax.random.randint(seeds[4], (NT, NOBS), 0, BRICKS), jax.random.fold_in(seeds[4], 1), 0, BRICKS - 1).astype(jnp.int32)
    obs_cell = place_ends(jax.random.randint(seeds[5], (NT, NOBS), 0, BRICK_CELLS), jax.random.fold_in(seeds[5], 1), 0, BRICK_CELLS - 1).astype(jnp.int32)
    obs_step = place_ends(jax.random.randint(seeds[6], (NT, NOBS), 0, 2), jax.random.fold_in(seeds[6], 1), 0, 1).astype(jnp.int32)
    dual_state = normal_values(seeds[7], (NT, LEV, NY, NX), 1.0, 6.0, ((0, 16), (2, 16)), jnp.float32)
    dual_obs = normal_values(seeds[8], (NT, NOBS), 1.0, 6.0, ((0, 16), (1, 16)), jnp.float32)
    increment = normal_values(seeds[9], (NT, LEV, NY, NX), 1.0, 6.0, ((0, 16), (2, 16)), jnp.float32)
    resid_model = normal_values(seeds[10], (NT, LEV, NY, NX), 1.0, 6.0, ((0, 16), (2, 16)), jnp.float32)
    resid_obs = normal_values(seeds[11], (NT, NOBS), 1.0, 6.0, ((0, 16), (1, 16)), jnp.float32)
    resid_state = normal_values(seeds[12], (NT, LEV, NY, NX), 1.0, 6.0, ((0, 16), (2, 16)), jnp.float32)
    return dict(courant_x=courant_x, courant_y=courant_y, model_var=model_var, obs_var=obs_var, obs_brick=obs_brick, obs_cell=obs_cell, obs_step=obs_step, dual_state=dual_state, dual_obs=dual_obs, increment=increment, resid_model=resid_model, resid_obs=resid_obs, resid_state=resid_state)


def weights_of(courant_x, courant_y):
    coef_west = jnp.maximum(courant_x, 0.0)
    coef_east = jnp.maximum(-courant_x, 0.0)
    coef_south = jnp.maximum(courant_y, 0.0)
    coef_north = jnp.maximum(-courant_y, 0.0)
    coef_self = 1.0 - jnp.abs(courant_x) - jnp.abs(courant_y)
    return coef_self, coef_west, coef_east, coef_south, coef_north


def advect(state_field, coeffs):
    coef_self, coef_west, coef_east, coef_south, coef_north = coeffs
    zero_row = jnp.zeros_like(state_field[..., :1, :])
    from_south = jnp.concatenate([zero_row, state_field[..., :-1, :]], axis=-2)
    from_north = jnp.concatenate([state_field[..., 1:, :], zero_row], axis=-2)
    return (coef_self * state_field + coef_west * jnp.roll(state_field, 1, axis=-1)
            + coef_east * jnp.roll(state_field, -1, axis=-1)
            + coef_south * from_south + coef_north * from_north)


def advect_adjoint(state_field, coeffs):
    coef_self, coef_west, coef_east, coef_south, coef_north = coeffs
    south_part = coef_south * state_field
    north_part = coef_north * state_field
    zero_row = jnp.zeros_like(state_field[..., :1, :])
    up_part = jnp.concatenate([south_part[..., 1:, :], zero_row], axis=-2)
    down_part = jnp.concatenate([zero_row, north_part[..., :-1, :]], axis=-2)
    return (coef_self * state_field + jnp.roll(coef_west * state_field, -1, axis=-1)
            + jnp.roll(coef_east * state_field, 1, axis=-1) + up_part + down_part)


def reference(courant_x, courant_y, model_var, obs_var, obs_brick, obs_cell, obs_step, dual_state, dual_obs,
              increment, resid_model, resid_obs, resid_state):
    coeffs = weights_of(courant_x, courant_y)
    dual_step = jnp.cumsum(resid_state[::-1], axis=0)[::-1]
    dual_obs_step = resid_obs / obs_var
    source = resid_model - model_var * dual_step
    incr_step = jnp.cumsum(source, axis=0)
    after_one = advect(incr_step, coeffs)
    after_two = advect(after_one, coeffs)
    carried = jnp.concatenate([jnp.zeros_like(after_two[:1]), after_two[:-1]], axis=0)
    image_model = model_var * dual_step + incr_step - carried
    obs_level = (obs_cell // (ROWS_DEV * NX)).astype(jnp.int32)
    grid_row = (obs_brick * ROWS_DEV + (obs_cell // NX) % ROWS_DEV).astype(jnp.int32)
    column = (obs_cell % NX).astype(jnp.int32)
    sub_index = (jnp.arange(NT, dtype=jnp.int32)[:, None] + jnp.zeros_like(obs_cell)).astype(jnp.int32)
    at_start = incr_step[sub_index, obs_level, grid_row, column]
    at_middle = after_one[sub_index, obs_level, grid_row, column]
    image_obs = obs_var * dual_obs_step + jnp.where(obs_step == 0, at_start, at_middle)
    blank_field = jnp.zeros_like(dual_step)
    start_dual = jnp.where(obs_step == 0, dual_obs_step, jnp.zeros_like(dual_obs_step))
    middle_dual = jnp.where(obs_step == 1, dual_obs_step, jnp.zeros_like(dual_obs_step))
    spread_start = blank_field.at[sub_index, obs_level, grid_row, column].add(start_dual)
    spread_middle = blank_field.at[sub_index, obs_level, grid_row, column].add(middle_dual)
    next_dual = jnp.concatenate([dual_step[1:], blank_field[:1]], axis=0)
    carried_back = advect_adjoint(next_dual, coeffs)
    image_state = dual_step + spread_start + advect_adjoint(spread_middle - carried_back, coeffs)
    projected = (jnp.sum(resid_model * image_model) + jnp.sum(resid_obs * image_obs)
                 + jnp.sum(resid_state * image_state))
    curvature = (jnp.sum(image_model * image_model) + jnp.sum(image_obs * image_obs)
                 + jnp.sum(image_state * image_state))
    step_length = projected / curvature
    return (dual_state + step_length * dual_step,
            dual_obs + step_length * dual_obs_step,
            increment + step_length * incr_step,
            resid_model - step_length * image_model,
            resid_obs - step_length * image_obs,
            resid_state - step_length * image_state)
```

```python
import functools

import jax
import jax.numpy as jnp
from jax import lax
from jax.experimental import pallas as pl
from jax.experimental.pallas import tpu as pltpu
from jax.sharding import PartitionSpec as P

LANES = 128
SLOTS = 128
BLOCK = 1024
MIB = 1024 * 1024


def params(mib):
    return pltpu.CompilerParams(vmem_limit_bytes=mib * MIB)


def cost(flops, touched):
    return pl.CostEstimate(flops=flops, bytes_accessed=touched, transcendentals=0)


VMEM = pl.BlockSpec(memory_space=pltpu.VMEM)
SMEM = pl.BlockSpec(memory_space=pltpu.SMEM)


def f32(*shape):
    return jax.ShapeDtypeStruct(shape, jnp.float32)


def i32(*shape):
    return jax.ShapeDtypeStruct(shape, jnp.int32)


def pack_kernel(parts, rs_ref, rm_ref, mv_ref, out_ref):
    levels, rows, columns = rs_ref.shape
    per_level = parts // levels
    width = columns // per_level
    for level in range(levels):
        for piece in range(per_level):
            part = level * per_level + piece
            cols = slice(piece * width, (piece + 1) * width)
            for place, ref in enumerate((rs_ref, rm_ref, mv_ref)):
                out_ref[part, rows * place : rows * (place + 1), :] = ref[level, :, cols]


def scan_kernel(in_ref, out_ref):
    steps = in_ref.shape[0]
    rows = in_ref.shape[1] // 3
    later = jnp.zeros((rows, in_ref.shape[2]), jnp.float32)
    for t in reversed(range(steps)):
        out_ref[t, rows : 2 * rows, :] = later
        later = later + in_ref[t, 0:rows, :]
        out_ref[t, 0:rows, :] = (
            in_ref[t, rows : 2 * rows, :] - in_ref[t, 2 * rows : 3 * rows, :] * later
        )
    total = jnp.zeros((rows, in_ref.shape[2]), jnp.float32)
    for t in range(steps):
        total = total + out_ref[t, 0:rows, :]
        out_ref[t, 0:rows, :] = total


def edge_kernel(levels, back_ref, up_ref, down_ref):
    parts, _, width = back_ref.shape
    per_level = parts // levels
    for part in range(parts):
        level, piece = part // per_level, part % per_level
        cols = slice(piece * width, (piece + 1) * width)
        for field in range(2):
            base = 8 * field
            for out_ref, rows in ((up_ref, (7, 6)), (down_ref, (0, 1))):
                for place, row in enumerate(rows):
                    at = base + 4 * place + level
                    out_ref[at : at + 1, cols] = back_ref[part, base + row : base + row + 1, :]


def courant_edge_kernel(cx_ref, cy_ref, up_ref, down_ref):
    levels = cx_ref.shape[0]
    for level in range(levels):
        for out_ref, rows in ((up_ref, (7, 6)), (down_ref, (0, 1))):
            first, second = rows
            out_ref[level : level + 1, :] = cx_ref[level, first : first + 1, :]
            out_ref[4 + level : 5 + level, :] = cy_ref[level, first : first + 1, :]
            out_ref[8 + level : 9 + level, :] = cy_ref[level, second : second + 1, :]
            out_ref[12 + level : 13 + level, :] = cy_ref[level, second : second + 1, :]


def place_kernel(columns, at_ref, brick_ref, cell_ref, step_ref, rank_ref, code_ref, passes_ref,
                 brick_s, cell_s, step_s):
    blocks = rank_ref.shape[0]
    here = at_ref[0]
    lane_groups = columns // LANES
    for k in range(blocks):
        cols = slice(k * BLOCK, (k + 1) * BLOCK)
        brick_s[k : k + 1, :] = brick_ref[0:1, cols]
        cell_s[k : k + 1, :] = cell_ref[0:1, cols]
        step_s[k : k + 1, :] = step_ref[0:1, cols]
    brick, cell, step = brick_s[...], cell_s[...], step_s[...]
    line = ((cell >> 10) * 171) >> 9
    level, row = line >> 3, line & 7
    column = cell - line * columns
    group, lane = column >> 7, column & 127
    own = brick == here
    below = (brick == here - 1) & (row == 7) & (step == 1)
    above = (brick == here + 1) & (row == 0) & (step == 1)
    halo_base = 4 * lane_groups * 8
    own_group = (level * lane_groups + group) * 8 + row
    halo_group = halo_base + group * 8 + level + jnp.where(above, 4, 0)
    code_ref[...] = jnp.where(own, own_group, halo_group) * 256 + step * LANES + lane
    inside = own | below | above
    count = inside.astype(jnp.int32)
    lanes = lax.broadcasted_iota(jnp.int32, count.shape, 1)
    shift = 1
    while shift < BLOCK:
        count = count + jnp.where(lanes >= shift, pltpu.roll(count, shift, 1), 0)
        shift *= 2
    rank_ref[...] = jnp.where(inside, count - 1, -1)
    passes_ref[0] = (jnp.max(count) + SLOTS - 1) // SLOTS


def slot_codes(rank_row, code_row, first):
    slot = lax.broadcasted_iota(jnp.int32, (SLOTS, BLOCK), 0) + first
    held = jnp.broadcast_to(rank_row, (SLOTS, BLOCK)) == slot
    code = jnp.max(
        jnp.where(held, jnp.broadcast_to(code_row, (SLOTS, BLOCK)), -1), axis=1, keepdims=True
    )
    return held, code


def split_two(x):
    high = x.astype(jnp.bfloat16)
    low = (x - high.astype(jnp.float32)).astype(jnp.bfloat16)
    return high, low


def spread_kernel(at_ref, passes_ref, rank_ref, code_ref, duals_ref, start_ref, middle_ref, edge_ref,
                  total, hot_s, high_s, low_s):
    blocks = rank_ref.shape[0]
    groups = total.shape[0]
    here = at_ref[0]
    levels, _, columns = start_ref.shape
    lane_groups = columns // LANES
    together = min(4, blocks)
    total[...] = jnp.zeros_like(total)
    eye = (lax.broadcasted_iota(jnp.int32, (SLOTS, SLOTS), 0)
           == lax.broadcasted_iota(jnp.int32, (SLOTS, SLOTS), 1))
    group_id = lax.broadcasted_iota(jnp.int32, (groups, SLOTS), 0)
    column_id = lax.broadcasted_iota(jnp.int32, (SLOTS, 2 * LANES), 1)

    def one_pass(number, carry):
        first = number * SLOTS

        def some_blocks(q, carry):
            for j in range(together):
                k = q * together + j
                held, code = slot_codes(rank_ref[pl.ds(k, 1), :], code_ref[pl.ds(k, 1), :], first)
                dual_row = duals_ref[pl.ds(lax.bitwise_xor(k, here), 1), BLOCK : 2 * BLOCK]
                dual = jnp.sum(
                    jnp.where(held, jnp.broadcast_to(dual_row, (SLOTS, BLOCK)), 0.0),
                    axis=1, keepdims=True,
                )
                group = jnp.max(
                    jnp.where(eye, jnp.broadcast_to(code >> 8, (SLOTS, SLOTS)), -1),
                    axis=0, keepdims=True,
                )
                hot_s[:, j * SLOTS : (j + 1) * SLOTS] = (
                    (group_id == jnp.broadcast_to(group, (groups, SLOTS)))
                    .astype(jnp.float32).astype(jnp.bfloat16)
                )
                placed = jnp.where(
                    column_id == jnp.broadcast_to(code & 255, (SLOTS, 2 * LANES)),
                    jnp.broadcast_to(dual, (SLOTS, 2 * LANES)), 0.0,
                )
                high, low = split_two(placed)
                high_s[j * SLOTS : (j + 1) * SLOTS, :] = high
                low_s[j * SLOTS : (j + 1) * SLOTS, :] = low
            total[...] += jnp.dot(
                hot_s[...], high_s[...], preferred_element_type=jnp.float32
            ) + jnp.dot(hot_s[...], low_s[...], preferred_element_type=jnp.float32)
            return carry

        return lax.fori_loop(0, blocks // together, some_blocks, carry)

    lax.fori_loop(0, passes_ref[0], one_pass, 0)
    for level in range(levels):
        for g in range(lane_groups):
            at = (level * lane_groups + g) * 8
            cols = slice(g * LANES, (g + 1) * LANES)
            start_ref[level, :, cols] = total[at : at + 8, 0:LANES]
            middle_ref[level, :, cols] = total[at : at + 8, LANES : 2 * LANES]
    base = levels * lane_groups * 8
    for g in range(lane_groups):
        edge_ref[:, g * LANES : (g + 1) * LANES] = total[
            base + 8 * g : base + 8 * g + 8, LANES : 2 * LANES
        ]


def west_of(v):
    return pltpu.roll(v, 1, 1)


def east_of(v):
    return pltpu.roll(v, v.shape[1] - 1, 1)


def weights_of(cx, cy):
    west, east = jnp.maximum(cx, 0.0), jnp.maximum(-cx, 0.0)
    south, north = jnp.maximum(cy, 0.0), jnp.maximum(-cy, 0.0)
    return 1.0 - jnp.abs(cx) - jnp.abs(cy), west, east, south, north


def forward(v, below, above, coeffs):
    own, west, east, south, north = coeffs
    return own * v + west * west_of(v) + east * east_of(v) + south * below + north * above


def adjoint(v, from_above, from_below, coeffs):
    own, west, east, _, _ = coeffs
    return own * v + east_of(west * v) + west_of(east * v) + from_above + from_below


def row_below(v, edge, first):
    return jnp.where(first, jnp.broadcast_to(edge, v.shape), pltpu.roll(v, 1, 0))


def row_above(v, edge, last):
    return jnp.where(last, jnp.broadcast_to(edge, v.shape), pltpu.roll(v, v.shape[0] - 1, 0))


def stacked(low, high):
    return jnp.concatenate([low, high], axis=0)


def image_kernel(where_ref, passes_ref, back_ref, up_ref, down_ref, below_ref, above_ref, cx_ref, cy_ref,
                 cup_ref, cdown_ref, cbelow_ref, cabove_ref, start_ref, middle_ref, edge_ref,
                 rs_ref, rm_ref, rm_next_ref, rank_ref, code_ref, obs_ref,
                 next_ref, state_ref, sent_ref, fields, hot_s, found):
    levels, rows, columns = cx_ref.shape
    parts, _, width = back_ref.shape
    per_level = parts // levels
    blocks = rank_ref.shape[0]
    lane_groups = columns // LANES
    window, windows, here = where_ref[0], where_ref[1], where_ref[2]

    cx_edge = stacked(cbelow_ref[0:4, :], cabove_ref[0:4, :])
    cy_edge = stacked(cbelow_ref[4:8, :], cabove_ref[4:8, :])
    cy_edge_below = stacked(cbelow_ref[8:12, :], cup_ref[4:8, :])
    cy_edge_above = stacked(cdown_ref[4:8, :], cabove_ref[8:12, :])
    edge_coeffs = weights_of(cx_edge, cy_edge)
    incr_edge = stacked(below_ref[0:4, :], above_ref[0:4, :])
    one_edge = forward(
        incr_edge,
        stacked(below_ref[4:8, :], up_ref[0:4, :]),
        stacked(down_ref[0:4, :], above_ref[4:8, :]),
        edge_coeffs,
    )
    dual_edge = stacked(below_ref[8:12, :], above_ref[8:12, :])
    dual_below = stacked(below_ref[12:16, :], up_ref[8:12, :])
    dual_above = stacked(down_ref[8:12, :], above_ref[12:16, :])
    kept_edge = edge_ref[...] - adjoint(
        dual_edge,
        jnp.maximum(cy_edge_above, 0.0) * dual_above,
        jnp.maximum(-cy_edge_below, 0.0) * dual_below,
        edge_coeffs,
    )
    edge_north, edge_south = edge_coeffs[4], edge_coeffs[3]
    dual_flux = jnp.where(
        lax.broadcasted_iota(jnp.int32, cx_edge.shape, 0) < 4, edge_north, edge_south
    )
    kept_flux = dual_flux * kept_edge
    dual_flux = dual_flux * dual_edge

    row_id = lax.broadcasted_iota(jnp.int32, (rows, columns), 0)
    first, last = row_id == 0, row_id == rows - 1
    projected = jnp.zeros((rows, columns), jnp.float32)
    curvature = jnp.zeros((rows, columns), jnp.float32)
    has_next = jnp.where(window < windows - 1, 1.0, 0.0)
    is_first = jnp.where(window == 0, 1.0, 0.0)
    for level in range(levels):
        pieces = range(level * per_level, (level + 1) * per_level)
        incr = jnp.concatenate([back_ref[p, 0:rows, :] for p in pieces], axis=1)
        next_dual = jnp.concatenate([back_ref[p, rows : 2 * rows, :] for p in pieces], axis=1)
        coeffs = weights_of(cx_ref[level], cy_ref[level])
        south, north = coeffs[3], coeffs[4]
        low, high = slice(level, level + 1), slice(4 + level, 5 + level)
        after_one = forward(
            incr,
            row_below(incr, incr_edge[low], first),
            row_above(incr, incr_edge[high], last),
            coeffs,
        )
        after_two = forward(
            after_one,
            row_below(after_one, one_edge[low], first),
            row_above(after_one, one_edge[high], last),
            coeffs,
        )
        rm_next = rm_next_ref[level]
        image_next = (rm_next + incr - after_two) * has_next
        next_ref[level] = image_next
        back_one = adjoint(
            next_dual,
            row_above(south * next_dual, dual_flux[high], last),
            row_below(north * next_dual, dual_flux[low], first),
            coeffs,
        )
        kept = middle_ref[level] - back_one
        rs, rm = rs_ref[level], rm_ref[level]
        image_state = (next_dual + rs) + start_ref[level] + adjoint(
            kept,
            row_above(south * kept, kept_flux[high], last),
            row_below(north * kept, kept_flux[low], first),
            coeffs,
        )
        state_ref[level] = image_state
        at_first = is_first * rm * rm
        projected += rm_next * image_next + rs * image_state + at_first
        curvature += image_next * image_next + image_state * image_state + at_first
        for g in range(lane_groups):
            at = (level * lane_groups + g) * 8
            cols = slice(g * LANES, (g + 1) * LANES)
            fields[at : at + 8, 0:LANES] = incr[:, cols]
            fields[at : at + 8, LANES : 2 * LANES] = after_one[:, cols]

    high_fields, low_fields = split_two(fields[...])
    groups = levels * lane_groups * 8
    group_id = lax.broadcasted_iota(jnp.int32, (SLOTS, groups), 1)
    column_id = lax.broadcasted_iota(jnp.int32, (SLOTS, 2 * LANES), 1)
    together = min(4, blocks)
    found[...] = jnp.zeros_like(found)

    def one_pass(number, carry):
        first_slot = number * SLOTS

        def some_blocks(q, carry):
            columns_of, helds = [], []
            for j in range(together):
                k = q * together + j
                held, code = slot_codes(
                    rank_ref[pl.ds(k, 1), :], code_ref[pl.ds(k, 1), :], first_slot
                )
                hot_s[j * SLOTS : (j + 1) * SLOTS, :] = (
                    (group_id == jnp.broadcast_to(code >> 8, (SLOTS, groups)))
                    .astype(jnp.float32).astype(jnp.bfloat16)
                )
                columns_of.append(code & 255)
                helds.append(held)
            picked = jnp.dot(
                hot_s[...], high_fields, preferred_element_type=jnp.float32
            ) + jnp.dot(hot_s[...], low_fields, preferred_element_type=jnp.float32)
            for j in range(together):
                k = q * together + j
                value = jnp.sum(
                    jnp.where(
                        column_id == jnp.broadcast_to(columns_of[j], (SLOTS, 2 * LANES)),
                        picked[j * SLOTS : (j + 1) * SLOTS, :], 0.0,
                    ),
                    axis=1, keepdims=True,
                )
                found[pl.ds(k, 1), :] += jnp.sum(
                    jnp.where(helds[j], jnp.broadcast_to(value, (SLOTS, BLOCK)), 0.0),
                    axis=0, keepdims=True,
                )
            return carry

        return lax.fori_loop(0, blocks // together, some_blocks, carry)

    lax.fori_loop(0, passes_ref[0], one_pass, 0)

    observed = found[...]
    sent_ref[:, 0:BLOCK] = observed
    resid = jnp.concatenate(
        [obs_ref[pl.ds(lax.bitwise_xor(k, here), 1), 0:BLOCK] for k in range(blocks)], axis=0
    )
    own = (rank_ref[...] >= 0) & (code_ref[...] < groups * 256)
    image_obs = jnp.where(own, resid + observed, 0.0)
    all_projected = jnp.sum(projected) + jnp.sum(resid * image_obs)
    all_curvature = jnp.sum(curvature) + jnp.sum(image_obs * image_obs)
    lane = lax.broadcasted_iota(jnp.int32, (blocks, LANES), 1)
    sent_ref[:, BLOCK : BLOCK + LANES] = jnp.where(
        lane == 0, all_projected, jnp.where(lane == 1, all_curvature, 0.0)
    )


def gather_kernel(got_ref, observed_ref, sums_ref):
    total = jnp.sum(got_ref[...], axis=0, keepdims=True)
    observed_ref[...] = total[:, 0:BLOCK]
    sums_ref[...] = jnp.broadcast_to(total[:, BLOCK : BLOCK + LANES], sums_ref.shape)


def update_kernel(where_ref, sums_ref, ds_ref, inc_ref, rm_ref, rs_ref, back_ref, image_ref, state_ref,
                  do_ref, ro_ref, ov_ref, observed_ref,
                  ds_out, do_out, inc_out, rm_out, ro_out, rs_out):
    sums = jnp.sum(sums_ref[...], axis=0, keepdims=True)
    lane = lax.broadcasted_iota(jnp.int32, sums.shape, 1)
    projected = jnp.sum(jnp.where(lane == 0, sums, 0.0), axis=1, keepdims=True)
    curvature = jnp.sum(jnp.where(lane == 1, sums, 0.0), axis=1, keepdims=True)
    step = projected / curvature
    rows = rs_ref.shape[1]
    parts, _, width = back_ref.shape
    wide = jnp.broadcast_to(step, (rows, width))
    starts = where_ref[0] == 0
    for piece in range(parts):
        cols = slice(piece * width, (piece + 1) * width)
        dual = back_ref[piece, rows : 2 * rows, :] + rs_ref[0, :, cols]
        ds_out[0, :, cols] = ds_ref[0, :, cols] + wide * dual
        inc_out[0, :, cols] = inc_ref[0, :, cols] + wide * back_ref[piece, 0:rows, :]
        rm = rm_ref[0, :, cols]
        image = jnp.where(starts, rm, image_ref[0, :, cols])
        rm_out[0, :, cols] = rm - wide * image
        rs_out[0, :, cols] = rs_ref[0, :, cols] - wide * state_ref[0, :, cols]

    @pl.when(pl.program_id(0) == 0)
    def _():
        narrow = jnp.broadcast_to(step, ro_ref.shape)
        ro, ov = ro_ref[...], ov_ref[...]
        dual = ro / ov
        do_out[...] = do_ref[...] + narrow * dual
        ro_out[...] = ro - narrow * (ov * dual + observed_ref[...])


def body(windows, bricks, courant_x, courant_y, model_var, obs_var, obs_brick, obs_cell, obs_step,
         dual_state, dual_obs, increment, resid_model, resid_obs, resid_state):
    cx, cy, mv = courant_x[0], courant_y[0], model_var[0]
    ds, inc, rm, rs = dual_state[0], increment[0], resid_model[0], resid_state[0]
    levels, rows, columns = rs.shape
    per_level = windows // levels
    width = columns // per_level
    blocks = bricks
    groups = levels * (columns // LANES) * 8
    halo_groups = groups + (columns // LANES) * 8
    field_bytes = 4 * levels * rows * columns
    here = lax.axis_index("space").astype(jnp.int32)
    window = lax.axis_index("tm").astype(jnp.int32)
    where = jnp.stack([window, jnp.int32(windows), here])
    at = here[None]

    upward = [(i, i + 1) for i in range(bricks - 1)]
    downward = [(i + 1, i) for i in range(bricks - 1)]

    packed = pl.pallas_call(
        functools.partial(pack_kernel, windows),
        out_shape=f32(windows, 3 * rows, width),
        in_specs=[VMEM] * 3,
        out_specs=VMEM,
        compiler_params=params(32),
        cost_estimate=cost(0, 6 * field_bytes),
        name="pack",
    )(rs, rm, mv)
    windows_of = lax.all_to_all(packed, "tm", 0, 0)

    rm_next = lax.ppermute(rm, "tm", [(i + 1, i) for i in range(windows - 1)])
    obs_all = jnp.concatenate([resid_obs, resid_obs / obs_var], axis=1)
    distance = 1
    while distance < bricks:
        other = lax.ppermute(obs_all, "space", [(i, i ^ distance) for i in range(bricks)])
        obs_all = jnp.concatenate([obs_all, other], axis=0)
        distance *= 2
    cup, cdown = pl.pallas_call(
        courant_edge_kernel,
        out_shape=(f32(16, columns), f32(16, columns)),
        in_specs=[VMEM] * 2,
        out_specs=(VMEM, VMEM),
        compiler_params=params(32),
        cost_estimate=cost(0, 3 * field_bytes),
        name="courant_edges",
    )(cx, cy)
    cbelow = lax.ppermute(cup, "space", upward)
    cabove = lax.ppermute(cdown, "space", downward)
    rank, code, passes = pl.pallas_call(
        functools.partial(place_kernel, columns),
        out_shape=(i32(blocks, BLOCK), i32(blocks, BLOCK), i32(1)),
        in_specs=[SMEM, VMEM, VMEM, VMEM],
        out_specs=(VMEM, VMEM, SMEM),
        scratch_shapes=[pltpu.VMEM((blocks, BLOCK), jnp.int32)] * 3,
        compiler_params=params(32),
        cost_estimate=cost(0, 2 * field_bytes),
        name="places",
    )(at, obs_brick, obs_cell, obs_step)
    together = min(4, blocks)
    spread_start, spread_middle, spread_edge = pl.pallas_call(
        spread_kernel,
        out_shape=(f32(levels, rows, columns), f32(levels, rows, columns), f32(8, columns)),
        in_specs=[SMEM, SMEM, VMEM, VMEM, VMEM],
        out_specs=(VMEM, VMEM, VMEM),
        scratch_shapes=[
            pltpu.VMEM((halo_groups, 2 * LANES), jnp.float32),
            pltpu.VMEM((halo_groups, together * SLOTS), jnp.bfloat16),
            pltpu.VMEM((together * SLOTS, 2 * LANES), jnp.bfloat16),
            pltpu.VMEM((together * SLOTS, 2 * LANES), jnp.bfloat16),
        ],
        compiler_params=params(40),
        cost_estimate=cost(4 * blocks * SLOTS * halo_groups * 2 * LANES, 3 * field_bytes),
        name="spread",
    )(at, passes, rank, code, obs_all)

    summed = pl.pallas_call(
        scan_kernel,
        out_shape=f32(windows, 2 * rows, width),
        in_specs=[VMEM],
        out_specs=VMEM,
        compiler_params=params(32),
        cost_estimate=cost(0, 5 * field_bytes),
        name="scan",
    )(windows_of)
    back = lax.all_to_all(summed, "tm", 0, 0)
    up, down = pl.pallas_call(
        functools.partial(edge_kernel, levels),
        out_shape=(f32(16, columns), f32(16, columns)),
        in_specs=[VMEM],
        out_specs=(VMEM, VMEM),
        compiler_params=params(32),
        cost_estimate=cost(0, 3 * field_bytes),
        name="edges",
    )(back)
    below = lax.ppermute(up, "space", upward)
    above = lax.ppermute(down, "space", downward)

    image_next, image_state, sent = pl.pallas_call(
        image_kernel,
        out_shape=(
            f32(levels, rows, columns), f32(levels, rows, columns), f32(blocks, BLOCK + LANES),
        ),
        in_specs=[SMEM, SMEM] + [VMEM] * 20,
        out_specs=(VMEM, VMEM, VMEM),
        scratch_shapes=[
            pltpu.VMEM((groups, 2 * LANES), jnp.float32),
            pltpu.VMEM((together * SLOTS, groups), jnp.bfloat16),
            pltpu.VMEM((blocks, BLOCK), jnp.float32),
        ],
        compiler_params=params(40),
        cost_estimate=cost(4 * blocks * SLOTS * groups * 2 * LANES, 14 * field_bytes),
        name="images",
    )(where, passes, back, up, down, below, above, cx, cy, cup, cdown, cbelow, cabove,
      spread_start, spread_middle, spread_edge, rs, rm, rm_next, rank, code, obs_all)

    image_model = lax.ppermute(image_next, "tm", [(i, i + 1) for i in range(windows - 1)])
    got = lax.all_to_all(sent, "space", 0, 0, tiled=True)
    observed, sums = pl.pallas_call(
        gather_kernel,
        out_shape=(f32(1, BLOCK), f32(windows, LANES)),
        in_specs=[VMEM],
        out_specs=(VMEM, VMEM),
        cost_estimate=cost(0, 200000),
        name="first_sums",
    )(got)
    all_sums = lax.all_to_all(sums, "tm", 0, 0, tiled=True)

    field = pl.BlockSpec((1, rows, columns), lambda l: (l, 0, 0))
    whole = lambda *shape: pl.BlockSpec(shape, lambda l: (0,) * len(shape))
    count = resid_obs.shape[1]
    new_ds, new_do, new_inc, new_rm, new_ro, new_rs = pl.pallas_call(
        update_kernel,
        grid=(levels,),
        out_shape=(
            f32(levels, rows, columns), f32(1, count), f32(levels, rows, columns),
            f32(levels, rows, columns), f32(1, count), f32(levels, rows, columns),
        ),
        in_specs=[
            SMEM, whole(windows, LANES), field, field, field, field,
            pl.BlockSpec((per_level, 2 * rows, width), lambda l: (l, 0, 0)), field, field,
            whole(1, count), whole(1, count), whole(1, count), whole(1, count),
        ],
        out_specs=(field, whole(1, count), field, field, whole(1, count), field),
        compiler_params=params(32),
        cost_estimate=cost(0, 12 * field_bytes),
        name="updates",
    )(where, all_sums, ds, inc, rm, rs, back, image_model, image_state,
      dual_obs, resid_obs, obs_var, observed)
    return new_ds[None], new_do, new_inc[None], new_rm[None], new_ro, new_rs[None]


def solution(mesh):
    field = P("tm", None, "space", None)
    obs = P("tm", "space")
    shared = P("tm", None)
    return jax.shard_map(
        functools.partial(body, mesh.shape["tm"], mesh.shape["space"]),
        mesh=mesh,
        in_specs=(
            field, field, field, obs, shared, shared, shared,
            field, obs, field, field, obs, field,
        ),
        out_specs=(field, obs, field, field, obs, field),
        check_vma=False,
    )
```

```python
import functools

import jax
import jax.numpy as jnp
from jax import lax
from jax.experimental import pallas as pl
from jax.experimental.pallas import tpu as pltpu
from jax.sharding import PartitionSpec as P

LANES = 128
SLOTS = 64
BLOCK = 512
CHUNK = 1024
MIB = 1024 * 1024


def params(mib):
    return pltpu.CompilerParams(vmem_limit_bytes=mib * MIB)


def cost(flops, touched):
    return pl.CostEstimate(flops=flops, bytes_accessed=touched, transcendentals=0)


VMEM = pl.BlockSpec(memory_space=pltpu.VMEM)
SMEM = pl.BlockSpec(memory_space=pltpu.SMEM)
ANY = pl.BlockSpec(memory_space=pl.ANY)
HBM = pl.BlockSpec(memory_space=pltpu.HBM)


def f32(*shape):
    return jax.ShapeDtypeStruct(shape, jnp.float32)


def i32(*shape):
    return jax.ShapeDtypeStruct(shape, jnp.int32)


def b16(*shape):
    return jax.ShapeDtypeStruct(shape, jnp.bfloat16)


def pack_kernel(parts, rs_ref, rm_ref, mv_ref, out_ref):
    levels, rows, columns = rs_ref.shape
    per_level = parts // levels
    width = columns // per_level
    for part in range(parts):
        level, piece = part // per_level, part % per_level
        cols = slice(piece * width, (piece + 1) * width)
        for place, ref in enumerate((rs_ref, rm_ref, mv_ref)):
            out_ref[part, rows * place : rows * (place + 1), :] = ref[level, :, cols]


def scan_kernel(in_ref, *rest):
    out_ref = rest[-1]
    steps = in_ref.shape[0]
    rows = in_ref.shape[1] // 3
    later = jnp.zeros((rows, in_ref.shape[2]), jnp.float32)
    for t in reversed(range(steps)):
        out_ref[t, rows : 2 * rows, :] = later
        later = later + in_ref[t, 0:rows, :]
        out_ref[t, 0:rows, :] = (
            in_ref[t, rows : 2 * rows, :] - in_ref[t, 2 * rows : 3 * rows, :] * later
        )
    total = jnp.zeros((rows, in_ref.shape[2]), jnp.float32)
    for t in range(steps):
        total = total + out_ref[t, 0:rows, :]
        out_ref[t, 0:rows, :] = total


def edge_kernel(levels, back_ref, rows_ref, up_ref, down_ref, rows_s):
    parts, both, width = back_ref.shape
    rows = both // 2
    per_level = parts // levels
    for part in range(parts):
        level, piece = part // per_level, part % per_level
        cols = slice(piece * width, (piece + 1) * width)
        for place, row in enumerate((rows - 1, 0, rows - 2, 1)):
            for field in range(2):
                at = 16 * field + 4 * place + level
                row_at = rows * field + row
                rows_s[at : at + 1, cols] = back_ref[part, row_at : row_at + 1, :]
    incr, incr_in, dual, dual_in = (rows_s[8 * i : 8 * i + 8, :] for i in range(4))
    cx, cy, cy_in, middle = (rows_ref[8 * i : 8 * i + 8, :] for i in range(4))
    own, west, east, south, north = weights_of(cx, cy)
    is_up = lax.broadcasted_iota(jnp.int32, cx.shape, 0) < 4
    inner, outer = jnp.where(is_up, south, north), jnp.where(is_up, north, south)
    one = own * incr + west * west_of(incr) + east * east_of(incr) + inner * incr_in
    from_in = jnp.maximum(jnp.where(is_up, -cy_in, cy_in), 0.0) * dual_in
    kept = middle - (own * dual + east_of(west * dual) + west_of(east * dual) + from_in)
    for place, value in enumerate((incr, one, outer, outer * kept, outer * dual)):
        up_ref[4 * place : 4 * place + 4, :] = value[0:4]
        down_ref[4 * place : 4 * place + 4, :] = value[4:8]


def slots_held(rank_ref, k, half, first):
    slot = lax.broadcasted_iota(jnp.int32, (SLOTS, BLOCK), 0) + first
    row = rank_ref[pl.ds(k, 1), half * BLOCK : (half + 1) * BLOCK]
    return jnp.broadcast_to(row, (SLOTS, BLOCK)) == slot


def build_slots(rank_ref, code_ref, first, hot_ref, cols_ref, finish=None):
    groups = hot_ref.shape[1]
    group_id = lax.broadcasted_iota(jnp.int32, (SLOTS, groups), 1)

    def one_chunk(k, carry):
        for half in range(CHUNK // BLOCK):
            held = slots_held(rank_ref, k, half, first)
            row = code_ref[pl.ds(k, 1), half * BLOCK : (half + 1) * BLOCK]
            code = jnp.max(
                jnp.where(held, jnp.broadcast_to(row, (SLOTS, BLOCK)), -1), axis=1, keepdims=True
            )
            at = pl.ds(pl.multiple_of(k * (CHUNK // BLOCK * SLOTS) + half * SLOTS, SLOTS), SLOTS)
            hot_ref[at, :] = (
                (group_id == jnp.broadcast_to(code >> 8, (SLOTS, groups)))
                .astype(jnp.float32).astype(jnp.bfloat16)
            )
            cols_ref[at, :] = jnp.broadcast_to(code & 255, (SLOTS, LANES))
        if finish is not None:
            finish(k)
        return carry

    lax.fori_loop(0, rank_ref.shape[0], one_chunk, 0)


def place_kernel(columns, at_ref, brick_ref, cell_ref, step_ref,
                 rank_ref, code_ref, hot_ref, cols_ref, passes_ref,
                 brick_s, cell_s, step_s, hot_s, cols_s, sems):
    chunks = rank_ref.shape[0]
    here = at_ref[0]
    lane_groups = columns // LANES
    for k in range(chunks):
        cols = slice(k * CHUNK, (k + 1) * CHUNK)
        brick_s[k : k + 1, :] = brick_ref[0:1, cols]
        cell_s[k : k + 1, :] = cell_ref[0:1, cols]
        step_s[k : k + 1, :] = step_ref[0:1, cols]
    brick, cell, step = brick_s[...], cell_s[...], step_s[...]
    line = ((cell >> 10) * 171) >> 9
    level, row = line >> 3, line & 7
    column = cell - line * columns
    group, lane = column >> 7, column & 127
    code_ref[...] = ((level * lane_groups + group) * 8 + row) * 256 + step * LANES + lane
    inside = brick == here
    count = inside.astype(jnp.int32)
    lanes = lax.broadcasted_iota(jnp.int32, count.shape, 1) & (BLOCK - 1)
    shift = 1
    while shift < BLOCK:
        count = count + jnp.where(lanes >= shift, pltpu.roll(count, shift, 1), 0)
        shift *= 2
    rank_ref[...] = jnp.where(inside, count - 1, -1)
    passes_ref[0] = (jnp.max(count) + SLOTS - 1) // SLOTS
    per_chunk = CHUNK // BLOCK * SLOTS

    def copies(k):
        at = pl.ds(pl.multiple_of(k * per_chunk, per_chunk), per_chunk)
        return (
            pltpu.make_async_copy(hot_s.at[at, :], hot_ref.at[at, :], sems.at[k, 0]),
            pltpu.make_async_copy(cols_s.at[at, :], cols_ref.at[at, :], sems.at[k, 1]),
        )

    def finish(k):
        for copy in copies(k):
            copy.start()

    build_slots(rank_ref, code_ref, 0, hot_s, cols_s, finish)
    for k in range(chunks):
        for copy in copies(k):
            copy.wait()


def in_column(cols, values, which):
    lane = lax.broadcasted_iota(jnp.int32, cols.shape, 1) + which * LANES
    return jnp.where(cols == lane, values, 0.0)


def split_two(x):
    high = x.astype(jnp.bfloat16)
    low = (x - high.astype(jnp.float32)).astype(jnp.bfloat16)
    return high, low


def spread_kernel(at_ref, passes_ref, rank_ref, code_ref, hot_hbm, cols_hbm, near_ref, far_ref, cx_ref, cy_ref,
                  start_ref, middle_ref, rows_ref, resid_ref,
                  total, hot_ref, cols_ref, again_hot, again_cols, high_s, low_s, duals_s, sems):
    chunks = rank_ref.shape[0]
    here = at_ref[0]
    levels, rows, columns = start_ref.shape
    lane_groups = columns // LANES
    cols_copy = pltpu.make_async_copy(cols_hbm, cols_ref, sems.at[0])
    hot_copy = pltpu.make_async_copy(hot_hbm, hot_ref, sems.at[1])
    cols_copy.start()
    hot_copy.start()
    for i in range(chunks):
        half = chunks // 2
        row = near_ref[i : i + 1, :] if i < half else far_ref[i - half : i - half + 1, :]
        at = pl.ds(lax.bitwise_xor(jnp.int32(i), here), 1)
        resid_ref[at, :] = row[:, 0:CHUNK]
        duals_s[at, :] = row[:, CHUNK : 2 * CHUNK]
    for level in range(levels):
        for place, row in enumerate((rows - 1, 0)):
            at = 4 * place + level
            rows_ref[at : at + 1, :] = cx_ref[level, row : row + 1, :]
            rows_ref[8 + at : 9 + at, :] = cy_ref[level, row : row + 1, :]
            inner = row - 1 if place == 0 else row + 1
            rows_ref[16 + at : 17 + at, :] = cy_ref[level, inner : inner + 1, :]
    cols_copy.wait()

    def add_up(first, hot, cols_ref, ready):
        def one_chunk(k, carry):
            for half in range(CHUNK // BLOCK):
                held = slots_held(rank_ref, k, half, first)
                row = duals_s[pl.ds(k, 1), half * BLOCK : (half + 1) * BLOCK]
                dual = jnp.sum(
                    jnp.where(held, jnp.broadcast_to(row, (SLOTS, BLOCK)), 0.0),
                    axis=1, keepdims=True,
                )
                at = pl.ds(pl.multiple_of(k * (CHUNK // BLOCK * SLOTS) + half * SLOTS, SLOTS), SLOTS)
                wide = jnp.broadcast_to(dual, (SLOTS, LANES))
                for which in range(2):
                    high, low = split_two(in_column(cols_ref[at, :], wide, which))
                    high_s[at, which * LANES : (which + 1) * LANES] = high
                    low_s[at, which * LANES : (which + 1) * LANES] = low
            return carry

        lax.fori_loop(0, chunks, one_chunk, 0)
        if ready is not None:
            ready.wait()
        over_slots = (((0,), (0,)), ((), ()))
        both = lax.dot_general(
            high_s[...], hot[...], over_slots, preferred_element_type=jnp.float32
        ) + lax.dot_general(
            low_s[...], hot[...], over_slots, preferred_element_type=jnp.float32
        )
        return both.T

    total[...] = add_up(0, hot_ref, cols_ref, hot_copy)

    def one_more(number, carry):
        build_slots(rank_ref, code_ref, number * SLOTS, again_hot, again_cols)
        total[...] += add_up(number * SLOTS, again_hot, again_cols, None)
        return carry

    lax.fori_loop(1, passes_ref[0], one_more, 0)
    for level in range(levels):
        for g in range(lane_groups):
            at = (level * lane_groups + g) * 8
            cols = slice(g * LANES, (g + 1) * LANES)
            start_ref[level, :, cols] = total[at : at + 8, 0:LANES]
            middle_ref[level, :, cols] = total[at : at + 8, LANES : 2 * LANES]
    for level in range(levels):
        for place, row in enumerate((rows - 1, 0)):
            at = 24 + 4 * place + level
            rows_ref[at : at + 1, :] = middle_ref[level, row : row + 1, :]


def west_of(v):
    return pltpu.roll(v, 1, 1)


def east_of(v):
    return pltpu.roll(v, v.shape[1] - 1, 1)


def weights_of(cx, cy):
    west, east = jnp.maximum(cx, 0.0), jnp.maximum(-cx, 0.0)
    south, north = jnp.maximum(cy, 0.0), jnp.maximum(-cy, 0.0)
    return 1.0 - jnp.abs(cx) - jnp.abs(cy), west, east, south, north


def forward(v, below, above, coeffs):
    own, west, east, south, north = coeffs
    return own * v + west * west_of(v) + east * east_of(v) + south * below + north * above


def adjoint(v, from_above, from_below, coeffs):
    own, west, east, _, _ = coeffs
    return own * v + east_of(west * v) + west_of(east * v) + from_above + from_below


def row_below(v, edge, first):
    return jnp.where(first, jnp.broadcast_to(edge, v.shape), pltpu.roll(v, 1, 0))


def row_above(v, edge, last):
    return jnp.where(last, jnp.broadcast_to(edge, v.shape), pltpu.roll(v, v.shape[0] - 1, 0))


def image_kernel(where_ref, passes_ref, back_hbm, below_hbm, above_hbm, cx_hbm, cy_hbm,
                 start_hbm, middle_hbm, rs_hbm, rm_hbm, rm_next_hbm, hot_hbm, cols_hbm,
                 rank_ref, code_ref, resid_ref, next_ref, state_ref, sent_ref,
                 back_ref, below_ref, above_ref, cx_ref, cy_ref, start_ref, middle_ref, rs_ref, rm_ref, rm_next_ref,
                 hot_ref, cols_ref, fields, again_hot, again_cols, found, sems, hot_sems):
    levels, rows, columns = cx_ref.shape
    parts, _, width = back_ref.shape
    per_level = parts // levels
    chunks = rank_ref.shape[0]
    lane_groups = columns // LANES
    window, windows = where_ref[0], where_ref[1]

    edges = [
        pltpu.make_async_copy(below_hbm, below_ref, hot_sems.at[0]),
        pltpu.make_async_copy(above_hbm, above_ref, hot_sems.at[1]),
    ]
    loads = []
    for level in range(levels):
        pieces = pl.ds(level * per_level, per_level)
        pairs = [(back_hbm.at[pieces], back_ref.at[pieces])] + [
            (a.at[level], b.at[level])
            for a, b in (
                (cx_hbm, cx_ref), (cy_hbm, cy_ref), (rm_next_hbm, rm_next_ref), (start_hbm, start_ref),
                (middle_hbm, middle_ref), (rs_hbm, rs_ref), (rm_hbm, rm_ref),
            )
        ]
        loads.append([
            pltpu.make_async_copy(a, b, sems.at[level, i]) for i, (a, b) in enumerate(pairs)
        ])
    look = [
        pltpu.make_async_copy(hot_hbm, hot_ref, hot_sems.at[2]),
        pltpu.make_async_copy(cols_hbm, cols_ref, hot_sems.at[3]),
    ]
    for copy in loads[0] + edges + loads[1] + loads[2] + loads[3] + look:
        copy.start()
    for copy in edges:
        copy.wait()

    row_id = lax.broadcasted_iota(jnp.int32, (rows, columns), 0)
    first, last = row_id == 0, row_id == rows - 1
    projected = jnp.zeros((rows, columns), jnp.float32)
    curvature = jnp.zeros((rows, columns), jnp.float32)
    has_next = jnp.where(window < windows - 1, 1.0, 0.0)
    is_first = jnp.where(window == 0, 1.0, 0.0)
    for level in range(levels):
        for copy in loads[level]:
            copy.wait()
        pieces = range(level * per_level, (level + 1) * per_level)
        incr = jnp.concatenate([back_ref[p, 0:rows, :] for p in pieces], axis=1)
        next_dual = jnp.concatenate([back_ref[p, rows : 2 * rows, :] for p in pieces], axis=1)
        coeffs = weights_of(cx_ref[level], cy_ref[level])
        south, north = coeffs[3], coeffs[4]
        low, high = (
            [ref[4 * i + level : 4 * i + level + 1, :] for i in range(5)] for ref in (below_ref, above_ref)
        )
        after_one = forward(
            incr,
            row_below(incr, low[0], first),
            row_above(incr, high[0], last),
            coeffs,
        )
        after_two = forward(
            after_one,
            row_below(after_one, low[1] + low[2] * incr[0:1], first),
            row_above(after_one, high[1] + high[2] * incr[rows - 1 :], last),
            coeffs,
        )
        rm_next = rm_next_ref[level]
        image_next = (rm_next + incr - after_two) * has_next
        next_ref[level] = image_next
        south_dual, north_dual = south * next_dual, north * next_dual
        back_one = adjoint(
            next_dual,
            row_above(south_dual, high[4], last),
            row_below(north_dual, low[4], first),
            coeffs,
        )
        kept = middle_ref[level] - back_one
        rs, rm = rs_ref[level], rm_ref[level]
        image_state = (next_dual + rs) + start_ref[level] + adjoint(
            kept,
            row_above(south * kept, high[3] - high[2] * north_dual[rows - 1 :], last),
            row_below(north * kept, low[3] - low[2] * south_dual[0:1], first),
            coeffs,
        )
        state_ref[level] = image_state
        at_first = is_first * rm * rm
        projected += rm_next * image_next + rs * image_state + at_first
        curvature += image_next * image_next + image_state * image_state + at_first
        for g in range(lane_groups):
            at = (level * lane_groups + g) * 8
            cols = slice(g * LANES, (g + 1) * LANES)
            fields[at : at + 8, 0:LANES] = incr[:, cols]
            fields[at : at + 8, LANES : 2 * LANES] = after_one[:, cols]

    high_fields, low_fields = split_two(fields[...])
    groups = levels * lane_groups * 8
    per_chunk = CHUNK // BLOCK * SLOTS

    def look_up(first, hot, cols_ref, fresh):
        def some_chunks(q, carry):
            rows_at = pl.ds(pl.multiple_of(q * 4 * per_chunk, 4 * per_chunk), 4 * per_chunk)
            picks = hot[rows_at, :]
            picked = jnp.dot(
                picks, high_fields, preferred_element_type=jnp.float32
            ) + jnp.dot(picks, low_fields, preferred_element_type=jnp.float32)
            cols = cols_ref[rows_at, :]
            value = jnp.sum(
                in_column(cols, picked[:, 0:LANES], 0)
                + in_column(cols, picked[:, LANES : 2 * LANES], 1),
                axis=1, keepdims=True,
            )
            for j in range(4):
                k = q * 4 + j
                for half in range(CHUNK // BLOCK):
                    at = j * per_chunk + half * SLOTS
                    held = slots_held(rank_ref, k, half, first)
                    line = jnp.sum(
                        jnp.where(
                            held, jnp.broadcast_to(value[at : at + SLOTS], (SLOTS, BLOCK)), 0.0
                        ),
                        axis=0, keepdims=True,
                    )
                    lanes = slice(half * BLOCK, (half + 1) * BLOCK)
                    if fresh:
                        found[pl.ds(k, 1), lanes] = line
                    else:
                        found[pl.ds(k, 1), lanes] += line
            return carry

        lax.fori_loop(0, chunks // 4, some_chunks, 0)

    for copy in look:
        copy.wait()
    look_up(0, hot_ref, cols_ref, True)

    def one_more(number, carry):
        build_slots(rank_ref, code_ref, number * SLOTS, again_hot, again_cols)
        look_up(number * SLOTS, again_hot, again_cols, False)
        return carry

    lax.fori_loop(1, passes_ref[0], one_more, 0)

    observed = found[...]
    resid = resid_ref[...]
    image_obs = jnp.where(rank_ref[...] >= 0, resid + observed, 0.0)
    all_projected = jnp.sum(projected) + jnp.sum(resid * image_obs)
    all_curvature = jnp.sum(curvature) + jnp.sum(image_obs * image_obs)
    lane = lax.broadcasted_iota(jnp.int32, (1, LANES), 1)
    sums = jnp.where(lane == 0, all_projected, jnp.where(lane == 1, all_curvature, 0.0))
    for k in range(chunks):
        sent_ref[k, :, 0:CHUNK] = found[k : k + 1, :]
        sent_ref[k, :, CHUNK : CHUNK + LANES] = sums


def gather_kernel(got_ref, observed_ref, sums_ref):
    total = got_ref[0]
    for k in range(1, got_ref.shape[0]):
        total = total + got_ref[k]
    observed_ref[...] = total[:, 0:CHUNK]
    for k in range(sums_ref.shape[0]):
        sums_ref[k] = total[:, CHUNK : CHUNK + LANES]


def update_kernel(where_ref, sums_ref, ds_ref, inc_ref, rm_ref, rs_ref, back_ref, image_ref, state_ref,
                  do_ref, ro_ref, ov_ref, observed_ref,
                  ds_out, do_out, inc_out, rm_out, ro_out, rs_out, ds_s, inc_s, rm_s, rs_s, sems):
    sums = sums_ref[0]
    for k in range(1, sums_ref.shape[0]):
        sums = sums + sums_ref[k]
    lane = lax.broadcasted_iota(jnp.int32, sums.shape, 1)
    projected = jnp.sum(jnp.where(lane == 0, sums, 0.0), axis=1, keepdims=True)
    curvature = jnp.sum(jnp.where(lane == 1, sums, 0.0), axis=1, keepdims=True)
    step = projected / curvature
    levels, rows, columns = rs_ref.shape
    parts, _, width = back_ref.shape
    per_level = parts // levels
    wide = jnp.broadcast_to(step, (rows, width))
    starts = where_ref[0] == 0
    copies = []
    for level in range(levels):
        for piece in range(per_level):
            part = level * per_level + piece
            cols = slice(piece * width, (piece + 1) * width)
            rs, rm = rs_ref[level, :, cols], rm_ref[level, :, cols]
            dual = back_ref[part, rows : 2 * rows, :] + rs
            ds_s[level, :, cols] = ds_ref[level, :, cols] + wide * dual
            inc_s[level, :, cols] = inc_ref[level, :, cols] + wide * back_ref[part, 0:rows, :]
            image = jnp.where(starts, rm, image_ref[level, :, cols])
            rm_s[level, :, cols] = rm - wide * image
            rs_s[level, :, cols] = rs - wide * state_ref[level, :, cols]
        pairs = ((ds_s, ds_out), (inc_s, inc_out), (rm_s, rm_out), (rs_s, rs_out))
        for place, (held, out) in enumerate(pairs):
            copies.append(pltpu.make_async_copy(held.at[level], out.at[level], sems.at[level, place]))
            copies[-1].start()
    narrow = jnp.broadcast_to(step, ro_ref.shape)
    ro, ov = ro_ref[...], ov_ref[...]
    dual = ro / ov
    do_out[...] = do_ref[...] + narrow * dual
    ro_out[...] = ro - narrow * (ov * dual + observed_ref[...])
    for copy in copies:
        copy.wait()


def body(windows, bricks, courant_x, courant_y, model_var, obs_var, obs_brick, obs_cell, obs_step,
         dual_state, dual_obs, increment, resid_model, resid_obs, resid_state):
    cx, cy, mv = courant_x[0], courant_y[0], model_var[0]
    ds, inc, rm, rs = dual_state[0], increment[0], resid_model[0], resid_state[0]
    levels, rows, columns = rs.shape
    per_level = windows // levels
    width = columns // per_level
    blocks = bricks
    groups = levels * (columns // LANES) * 8
    field_bytes = 4 * levels * rows * columns
    here = lax.axis_index("space").astype(jnp.int32)
    window = lax.axis_index("tm").astype(jnp.int32)
    where = jnp.stack([window, jnp.int32(windows), here])
    at = here[None]

    upward = [(i, i + 1) for i in range(bricks - 1)]
    downward = [(i + 1, i) for i in range(bricks - 1)]

    packed = pl.pallas_call(
        functools.partial(pack_kernel, windows),
        out_shape=f32(windows, 3 * rows, width),
        in_specs=[VMEM] * 3,
        out_specs=VMEM,
        compiler_params=params(60),
        cost_estimate=cost(0, 6 * field_bytes),
        name="pack",
    )(rs, rm, mv)
    windows_of = lax.all_to_all(packed, "tm", 0, 0)

    rm_next = lax.ppermute(rm, "tm", [(i + 1, i) for i in range(windows - 1)])
    near = jnp.concatenate([resid_obs, resid_obs / obs_var], axis=1)
    distance = 1
    while distance < bricks // 2:
        other = lax.ppermute(near, "space", [(i, i ^ distance) for i in range(bricks)])
        near = jnp.concatenate([near, other], axis=0)
        distance *= 2
    far = lax.ppermute(near, "space", [(i, i ^ distance) for i in range(bricks)])
    slots = blocks * (CHUNK // BLOCK) * SLOTS
    rank, code, hot, slot_cols, passes = pl.pallas_call(
        functools.partial(place_kernel, columns),
        out_shape=(
            i32(blocks, CHUNK), i32(blocks, CHUNK), b16(slots, groups), i32(slots, LANES), i32(1),
        ),
        in_specs=[SMEM, VMEM, VMEM, VMEM],
        out_specs=(VMEM, VMEM, HBM, HBM, SMEM),
        scratch_shapes=[pltpu.VMEM((blocks, CHUNK), jnp.int32)] * 3
        + [
            pltpu.VMEM((slots, groups), jnp.bfloat16), pltpu.VMEM((slots, LANES), jnp.int32),
            pltpu.SemaphoreType.DMA((blocks, 2)),
        ],
        compiler_params=params(60),
        cost_estimate=cost(0, 8 * field_bytes),
        name="places",
    )(at, obs_brick, obs_cell, obs_step)
    slot_scratch = [
        pltpu.VMEM((slots, groups), jnp.bfloat16), pltpu.VMEM((slots, LANES), jnp.int32),
    ]
    spread_start, spread_middle, edge_rows, resid_all = pl.pallas_call(
        spread_kernel,
        out_shape=(
            f32(levels, rows, columns), f32(levels, rows, columns), f32(32, columns),
            f32(blocks, CHUNK),
        ),
        in_specs=[SMEM, SMEM, VMEM, VMEM, HBM, HBM] + [VMEM] * 4,
        out_specs=(VMEM,) * 4,
        scratch_shapes=[
            pltpu.VMEM((groups, 2 * LANES), jnp.float32),
            *slot_scratch,
            *slot_scratch,
            pltpu.VMEM((slots, 2 * LANES), jnp.bfloat16),
            pltpu.VMEM((slots, 2 * LANES), jnp.bfloat16),
            pltpu.VMEM((blocks, CHUNK), jnp.float32),
            pltpu.SemaphoreType.DMA((2,)),
        ],
        compiler_params=params(60),
        cost_estimate=cost(4 * slots * groups * 2 * LANES, 16 * field_bytes),
        name="spread",
    )(at, passes, rank, code, hot, slot_cols, near, far, cx, cy)

    summed = pl.pallas_call(
        scan_kernel,
        out_shape=f32(windows, 2 * rows, width),
        in_specs=[VMEM, ANY, ANY],
        out_specs=VMEM,
        compiler_params=params(4),
        cost_estimate=cost(0, 5 * field_bytes),
        name="scan",
    )(windows_of, code, near)
    back = lax.all_to_all(summed, "tm", 0, 0)
    up, down = pl.pallas_call(
        functools.partial(edge_kernel, levels),
        out_shape=(f32(24, columns), f32(24, columns)),
        in_specs=[VMEM, VMEM],
        out_specs=(VMEM, VMEM),
        scratch_shapes=[pltpu.VMEM((32, columns), jnp.float32)],
        compiler_params=params(6),
        cost_estimate=cost(0, 3 * field_bytes),
        name="edges",
    )(back, edge_rows)
    below = lax.ppermute(up, "space", upward)
    above = lax.ppermute(down, "space", downward)

    image_next, image_state, sent = pl.pallas_call(
        image_kernel,
        out_shape=(
            f32(levels, rows, columns), f32(levels, rows, columns), f32(blocks, 1, CHUNK + LANES),
        ),
        in_specs=[SMEM, SMEM] + [HBM] * 12 + [VMEM] * 3,
        out_specs=(VMEM, VMEM, VMEM),
        scratch_shapes=[
            pltpu.VMEM((windows, 2 * rows, width), jnp.float32),
            pltpu.VMEM((24, columns), jnp.float32),
            pltpu.VMEM((24, columns), jnp.float32),
            *[pltpu.VMEM((levels, rows, columns), jnp.float32)] * 7,
            *slot_scratch,
            pltpu.VMEM((groups, 2 * LANES), jnp.float32),
            *slot_scratch,
            pltpu.VMEM((blocks, CHUNK), jnp.float32),
            pltpu.SemaphoreType.DMA((levels, 8)),
            pltpu.SemaphoreType.DMA((4,)),
        ],
        compiler_params=params(60),
        cost_estimate=cost(4 * slots * groups * 2 * LANES, 24 * field_bytes),
        name="images",
    )(where, passes, back, below, above, cx, cy, spread_start, spread_middle, rs, rm, rm_next,
      hot, slot_cols, rank, code, resid_all)

    image_model = lax.ppermute(image_next, "tm", [(i, i + 1) for i in range(windows - 1)])
    got = lax.all_to_all(sent, "space", 0, 0)
    observed, sums = pl.pallas_call(
        gather_kernel,
        out_shape=(f32(1, CHUNK), f32(windows, 1, LANES)),
        in_specs=[VMEM],
        out_specs=(VMEM, VMEM),
        compiler_params=params(4),
        cost_estimate=cost(0, 200000),
        name="first_sums",
    )(got)
    all_sums = lax.all_to_all(sums, "tm", 0, 0)

    count = resid_obs.shape[1]
    held = pltpu.VMEM((levels, rows, columns), jnp.float32)
    new_ds, new_do, new_inc, new_rm, new_ro, new_rs = pl.pallas_call(
        update_kernel,
        out_shape=(
            f32(levels, rows, columns), f32(1, count), f32(levels, rows, columns),
            f32(levels, rows, columns), f32(1, count), f32(levels, rows, columns),
        ),
        in_specs=[SMEM] + [VMEM] * 12,
        out_specs=(ANY, VMEM, ANY, ANY, VMEM, ANY),
        scratch_shapes=[held] * 4 + [pltpu.SemaphoreType.DMA((levels, 4))],
        compiler_params=params(8),
        cost_estimate=cost(0, 12 * field_bytes),
        name="updates",
    )(where, all_sums, ds, inc, rm, rs, back, image_model, image_state,
      dual_obs, resid_obs, obs_var, observed)
    return new_ds[None], new_do, new_inc[None], new_rm[None], new_ro, new_rs[None]


def solution(mesh):
    field = P("tm", None, "space", None)
    obs = P("tm", "space")
    shared = P("tm", None)
    return jax.shard_map(
        functools.partial(body, mesh.shape["tm"], mesh.shape["space"]),
        mesh=mesh,
        in_specs=(
            field, field, field, obs, shared, shared, shared,
            field, obs, field, field, obs, field,
        ),
        out_specs=(field, obs, field, field, obs, field),
        check_vma=False,
    )
```

```python
import functools

import jax
import jax.numpy as jnp
from jax import lax
from jax.experimental import pallas as pl
from jax.experimental.pallas import tpu as pltpu
from jax.sharding import PartitionSpec as P

LANES = 128
SLOTS = 64
BLOCK = 512
CHUNK = 1024
MIB = 1024 * 1024


def params(mib):
    return pltpu.CompilerParams(vmem_limit_bytes=mib * MIB)


def cost(flops, touched):
    return pl.CostEstimate(flops=flops, bytes_accessed=touched, transcendentals=0)


VMEM = pl.BlockSpec(memory_space=pltpu.VMEM)
SMEM = pl.BlockSpec(memory_space=pltpu.SMEM)
ANY = pl.BlockSpec(memory_space=pl.ANY)
HBM = pl.BlockSpec(memory_space=pltpu.HBM)


def f32(*shape):
    return jax.ShapeDtypeStruct(shape, jnp.float32)


def i32(*shape):
    return jax.ShapeDtypeStruct(shape, jnp.int32)


def b16(*shape):
    return jax.ShapeDtypeStruct(shape, jnp.bfloat16)


def duals_kernel(ro_ref, ov_ref, out_ref):
    count = ro_ref.shape[1]
    out_ref[:, 0:count] = ro_ref[...]
    out_ref[:, count : 2 * count] = ro_ref[...] / ov_ref[...]


def join_kernel(*refs):
    out_ref = refs[-1]
    rows = refs[0].shape[0]
    for place, ref in enumerate(refs[:-1]):
        out_ref[place * rows : (place + 1) * rows, :] = ref[...]


def gather_fields_kernel(cx_ref, cy_ref, rs_ref, after_ref, out_ref):
    levels = cx_ref.shape[0]
    for place, ref in enumerate((cx_ref, cy_ref, rs_ref)):
        out_ref[place * levels : (place + 1) * levels] = ref[...]


def pack_kernel(parts, rs_ref, rm_ref, mv_ref, out_ref):
    levels, rows, columns = rs_ref.shape
    per_level = parts // levels
    width = columns // per_level
    for part in range(parts):
        level, piece = part // per_level, part % per_level
        cols = slice(piece * width, (piece + 1) * width)
        for place, ref in enumerate((rs_ref, rm_ref, mv_ref)):
            out_ref[part, rows * place : rows * (place + 1), :] = ref[level, :, cols]


def scan_kernel(in_ref, *rest):
    out_ref = rest[-1]
    steps = in_ref.shape[0]
    rows = in_ref.shape[1] // 3
    later = jnp.zeros((rows, in_ref.shape[2]), jnp.float32)
    for t in reversed(range(steps)):
        out_ref[t, rows : 2 * rows, :] = later
        later = later + in_ref[t, 0:rows, :]
        out_ref[t, 0:rows, :] = (
            in_ref[t, rows : 2 * rows, :] - in_ref[t, 2 * rows : 3 * rows, :] * later
        )
    total = jnp.zeros((rows, in_ref.shape[2]), jnp.float32)
    for t in range(steps):
        total = total + out_ref[t, 0:rows, :]
        out_ref[t, 0:rows, :] = total


def collect_kernel(at_ref, *refs):
    out_ref = refs[-1]
    here = at_ref[0]
    rows = refs[0].shape[0]
    for place, ref in enumerate(refs[:-1]):
        for i in range(rows):
            at = lax.bitwise_xor(jnp.int32(place * rows + i), here)
            out_ref[pl.ds(at, 1), :] = ref[i : i + 1, :]


def edge_kernel(levels, back_ref, bundle_ref, up_ref, down_ref, rows_s):
    parts, both, width = back_ref.shape
    rows = both // 2
    per_level = parts // levels
    for part in range(parts):
        level, piece = part // per_level, part % per_level
        cols = slice(piece * width, (piece + 1) * width)
        for place, row in enumerate((rows - 1, 0, rows - 2, 1)):
            for field in range(2):
                at = 16 * field + 4 * place + level
                row_at = rows * field + row
                rows_s[at : at + 1, cols] = back_ref[part, row_at : row_at + 1, :]
    incr, incr_in, dual, dual_in = (rows_s[8 * i : 8 * i + 8, :] for i in range(4))
    cx, cy, cy_in, middle = (bundle_ref[2 * levels + i] for i in range(4))
    own, west, east, south, north = weights_of(cx, cy)
    is_up = lax.broadcasted_iota(jnp.int32, cx.shape, 0) < 4
    inner, outer = jnp.where(is_up, south, north), jnp.where(is_up, north, south)
    one = own * incr + west * west_of(incr) + east * east_of(incr) + inner * incr_in
    from_in = jnp.maximum(jnp.where(is_up, -cy_in, cy_in), 0.0) * dual_in
    kept = middle - (own * dual + east_of(west * dual) + west_of(east * dual) + from_in)
    for place, value in enumerate((incr, one, outer, outer * kept, outer * dual)):
        up_ref[4 * place : 4 * place + 4, :] = value[0:4]
        down_ref[4 * place : 4 * place + 4, :] = value[4:8]


def slots_held(rank_ref, k, half, first):
    slot = lax.broadcasted_iota(jnp.int32, (SLOTS, BLOCK), 0) + first
    row = rank_ref[pl.ds(k, 1), half * BLOCK : (half + 1) * BLOCK]
    return jnp.broadcast_to(row, (SLOTS, BLOCK)) == slot


def build_slots(rank_ref, code_ref, first, codes_ref, groups_ref):
    eye = (lax.broadcasted_iota(jnp.int32, (LANES, LANES), 0)
           == lax.broadcasted_iota(jnp.int32, (LANES, LANES), 1))

    def one_chunk(k, carry):
        parts = []
        for half in range(CHUNK // BLOCK):
            held = slots_held(rank_ref, k, half, first)
            row = (code_ref[pl.ds(k, 1), half * BLOCK : (half + 1) * BLOCK] + 1).astype(jnp.float32)
            code = jnp.sum(
                jnp.where(held, jnp.broadcast_to(row, (SLOTS, BLOCK)), 0.0), axis=1, keepdims=True
            )
            parts.append(jnp.broadcast_to(code, (SLOTS, LANES)))
        codes = jnp.concatenate(parts, axis=0) - 1.0
        codes_ref[pl.ds(pl.multiple_of(k * LANES, LANES), LANES), :] = codes
        groups_ref[pl.ds(k, 1), :] = jnp.sum(
            jnp.where(eye, codes.astype(jnp.int32) >> 8, 0), axis=0, keepdims=True
        )
        return carry

    lax.fori_loop(0, rank_ref.shape[0], one_chunk, 0, unroll=4)


def sections(chunks):
    tall = CHUNK // LANES
    sizes = dict(
        codes=chunks * LANES, rank=chunks * tall, code=chunks * tall, groups=chunks,
        square=8,
    )
    places, at = {}, 0
    for name, size in sizes.items():
        places[name] = at
        at += size
    return places, at


def fold(table_ref, first, lines):
    tall = lines.shape[1] // LANES
    for i in range(lines.shape[0] // 8):
        for j in range(tall):
            at = first + (i * tall + j) * 8
            table_ref[at : at + 8, :] = lines[8 * i : 8 * i + 8, j * LANES : (j + 1) * LANES]


def unfold(table_ref, first, count):
    tall = CHUNK // LANES
    return jnp.concatenate([
        jnp.concatenate(
            [table_ref[first + (i * tall + j) * 8 : first + (i * tall + j) * 8 + 8, :] for j in range(tall)],
            axis=1,
        )
        for i in range(count // 8)
    ], axis=0)


def place_kernel(columns, at_ref, brick_ref, cell_ref, step_ref, rm_ref,
                 table_ref, passes_ref, brick_s, cell_s, step_s, groups_s):
    chunks = brick_s.shape[0]
    rank_ref, code_ref = brick_s, cell_s
    places, _ = sections(chunks)
    here = at_ref[0]
    lane_groups = columns // LANES
    for k in range(chunks):
        cols = slice(k * CHUNK, (k + 1) * CHUNK)
        brick_s[k : k + 1, :] = brick_ref[0:1, cols]
        cell_s[k : k + 1, :] = cell_ref[0:1, cols]
        step_s[k : k + 1, :] = step_ref[0:1, cols]
    brick, cell, step = brick_s[...], cell_s[...], step_s[...]
    line = ((cell >> 10) * 171) >> 9
    level, row = line >> 3, line & 7
    column = cell - line * columns
    group, lane = column >> 7, column & 127
    code_ref[...] = ((level * lane_groups + group) * 8 + row) * 256 + step * LANES + lane
    inside = brick == here
    count = inside.astype(jnp.int32)
    lanes = lax.broadcasted_iota(jnp.int32, count.shape, 1) & (BLOCK - 1)
    shift = 1
    while shift < BLOCK:
        count = count + jnp.where(lanes >= shift, pltpu.roll(count, shift, 1), 0)
        shift *= 2
    rank_ref[...] = jnp.where(inside, count - 1, -1)
    build_slots(rank_ref, code_ref, 0, table_ref, groups_s)
    fold(table_ref, places["rank"], rank_ref[...].astype(jnp.float32))
    fold(table_ref, places["code"], code_ref[...].astype(jnp.float32))
    table_ref[places["groups"] : places["groups"] + chunks, :] = groups_s[...].astype(jnp.float32)
    passes_ref[0] = (jnp.max(count.astype(jnp.float32)).astype(jnp.int32) + SLOTS - 1) // SLOTS
    square = jnp.zeros(rm_ref.shape[1:], jnp.float32)
    for level in range(rm_ref.shape[0]):
        square += rm_ref[level] * rm_ref[level]
    table_ref[places["square"] : places["square"] + 8, :] = jnp.broadcast_to(
        jnp.sum(square), (8, LANES)
    )


def in_column(codes, values, which):
    codes = codes.astype(jnp.int32)
    lane = lax.broadcasted_iota(jnp.int32, codes.shape, 1) + which * LANES
    return jnp.where((codes & 255) == lane, values, 0.0)


def split_two(x):
    high = x.astype(jnp.bfloat16)
    low = (x - high.astype(jnp.float32)).astype(jnp.bfloat16)
    return high, low


def spread_kernel(passes_ref, table_ref, lines_ref, cx_ref, cy_ref, bundle_ref,
                  rank_ref, code_ref, again_codes, groups_ref, hot_s, high_s, low_s, total):
    chunks = rank_ref.shape[0]
    places, _ = sections(chunks)
    rank_ref[...] = unfold(table_ref, places["rank"], chunks).astype(jnp.int32)
    groups_ref[...] = table_ref[places["groups"] : places["groups"] + chunks, :].astype(jnp.int32)
    levels, rows, columns = cx_ref.shape
    lane_groups = columns // LANES
    groups = total.shape[0]
    for k in range(chunks // 8):
        bundle_ref[3 * levels, :, k * CHUNK : (k + 1) * CHUNK] = lines_ref[8 * k : 8 * k + 8, 0:CHUNK]
    rows_ref = bundle_ref.at[2 * levels : 3 * levels]
    for level in range(levels):
        for place, row in enumerate((rows - 1, 0)):
            at = 4 * place + level
            rows_ref[0, at : at + 1, :] = cx_ref[level, row : row + 1, :]
            rows_ref[1, at : at + 1, :] = cy_ref[level, row : row + 1, :]
            inner = row - 1 if place == 0 else row + 1
            rows_ref[2, at : at + 1, :] = cy_ref[level, inner : inner + 1, :]
    group_id = lax.broadcasted_iota(jnp.int32, (groups, LANES), 0)

    def add_up(first, codes_ref):
        def one_chunk(k, carry):
            at = pl.ds(pl.multiple_of(k * LANES, LANES), LANES)
            parts = []
            for half in range(CHUNK // BLOCK):
                held = slots_held(rank_ref, k, half, first)
                row = lines_ref[pl.ds(k, 1), CHUNK + half * BLOCK : CHUNK + (half + 1) * BLOCK]
                dual = jnp.sum(
                    jnp.where(held, jnp.broadcast_to(row, (SLOTS, BLOCK)), 0.0),
                    axis=1, keepdims=True,
                )
                parts.append(jnp.broadcast_to(dual, (SLOTS, LANES)))
            dual = jnp.concatenate(parts, axis=0)
            codes = codes_ref[at, :]
            for which in range(2):
                high, low = split_two(in_column(codes, dual, which))
                high_s[at, which * LANES : (which + 1) * LANES] = high
                low_s[at, which * LANES : (which + 1) * LANES] = low
            row = jnp.broadcast_to(groups_ref[pl.ds(k, 1), :], (groups, LANES))
            hot_s[:, at] = (row == group_id).astype(jnp.float32).astype(jnp.bfloat16)
            return carry

        lax.fori_loop(0, chunks, one_chunk, 0, unroll=4)
        return jnp.dot(
            hot_s[...], high_s[...], preferred_element_type=jnp.float32
        ) + jnp.dot(hot_s[...], low_s[...], preferred_element_type=jnp.float32)

    total[...] = add_up(0, table_ref)

    def one_more(number, carry):
        code_ref[...] = unfold(table_ref, places["code"], chunks).astype(jnp.int32)
        build_slots(rank_ref, code_ref, number * SLOTS, again_codes, groups_ref)
        total[...] += add_up(number * SLOTS, again_codes)
        return carry

    lax.fori_loop(1, passes_ref[0], one_more, 0)

    for g in range(lane_groups):
        cols = slice(g * LANES, (g + 1) * LANES)
        for level in range(levels):
            at = (level * lane_groups + g) * 8
            bundle_ref[level, :, cols] = total[at : at + 8, 0:LANES]
            bundle_ref[levels + level, :, cols] = total[at : at + 8, LANES : 2 * LANES]
    for level in range(levels):
        for place, row in enumerate((rows - 1, 0)):
            at = 4 * place + level
            rows_ref[3, at : at + 1, :] = bundle_ref[levels + level, row : row + 1, :]


def west_of(v):
    return pltpu.roll(v, 1, 1)


def east_of(v):
    return pltpu.roll(v, v.shape[1] - 1, 1)


def weights_of(cx, cy):
    west, east = jnp.maximum(cx, 0.0), jnp.maximum(-cx, 0.0)
    south, north = jnp.maximum(cy, 0.0), jnp.maximum(-cy, 0.0)
    return 1.0 - jnp.abs(cx) - jnp.abs(cy), west, east, south, north


def forward(v, below, above, coeffs):
    own, west, east, south, north = coeffs
    return own * v + west * west_of(v) + east * east_of(v) + south * below + north * above


def adjoint(v, from_above, from_below, coeffs):
    own, west, east, _, _ = coeffs
    return own * v + east_of(west * v) + west_of(east * v) + from_above + from_below


def row_below(v, edge, first):
    return jnp.where(first, jnp.broadcast_to(edge, v.shape), pltpu.roll(v, 1, 0))


def row_above(v, edge, last):
    return jnp.where(last, jnp.broadcast_to(edge, v.shape), pltpu.roll(v, v.shape[0] - 1, 0))


def image_kernel(windows, window_ref, passes_ref, back_ref, below_ref, above_ref, args_ref,
                 bundle_ref, rm_next_ref, table_ref, next_ref, state_ref, sent_ref,
                 fields, rank_ref, code_ref, again_codes, again_groups, hot_s, found):
    levels, rows, columns = rm_next_ref.shape
    parts, _, width = back_ref.shape
    per_level = parts // levels
    chunks = found.shape[0]
    places, _ = sections(chunks)
    rank_ref[...] = unfold(table_ref, places["rank"], chunks).astype(jnp.int32)
    lane_groups = columns // LANES
    window = window_ref[0]

    row_id = lax.broadcasted_iota(jnp.int32, (rows, columns), 0)
    first, last = row_id == 0, row_id == rows - 1
    projected = jnp.zeros((rows, columns), jnp.float32)
    curvature = jnp.zeros((rows, columns), jnp.float32)
    has_next = jnp.where(window < windows - 1, 1.0, 0.0)
    for level in range(levels):
        pieces = range(level * per_level, (level + 1) * per_level)
        incr = jnp.concatenate([back_ref[p, 0:rows, :] for p in pieces], axis=1)
        next_dual = jnp.concatenate([back_ref[p, rows : 2 * rows, :] for p in pieces], axis=1)
        coeffs = weights_of(args_ref[level], args_ref[levels + level])
        south, north = coeffs[3], coeffs[4]
        low, high = (
            [ref[4 * i + level : 4 * i + level + 1, :] for i in range(5)] for ref in (below_ref, above_ref)
        )
        after_one = forward(
            incr,
            row_below(incr, low[0], first),
            row_above(incr, high[0], last),
            coeffs,
        )
        after_two = forward(
            after_one,
            row_below(after_one, low[1] + low[2] * incr[0:1], first),
            row_above(after_one, high[1] + high[2] * incr[rows - 1 :], last),
            coeffs,
        )
        rm_next = rm_next_ref[level]
        image_next = (rm_next + incr - after_two) * has_next
        next_ref[level] = image_next
        south_dual, north_dual = south * next_dual, north * next_dual
        back_one = adjoint(
            next_dual,
            row_above(south_dual, high[4], last),
            row_below(north_dual, low[4], first),
            coeffs,
        )
        kept = bundle_ref[levels + level] - back_one
        rs = args_ref[2 * levels + level]
        image_state = (next_dual + rs) + bundle_ref[level] + adjoint(
            kept,
            row_above(south * kept, high[3] - high[2] * north_dual[rows - 1 :], last),
            row_below(north * kept, low[3] - low[2] * south_dual[0:1], first),
            coeffs,
        )
        state_ref[level] = image_state
        projected += rm_next * image_next + rs * image_state
        curvature += image_next * image_next + image_state * image_state
        for g in range(lane_groups):
            at = (level * lane_groups + g) * 8
            cols = slice(g * LANES, (g + 1) * LANES)
            fields[at : at + 8, 0:LANES] = incr[:, cols]
            fields[at : at + 8, LANES : 2 * LANES] = after_one[:, cols]

    high_fields, low_fields = split_two(fields[...])
    groups = levels * lane_groups * 8
    together = hot_s.shape[0] // LANES
    group_id = lax.broadcasted_iota(jnp.int32, (LANES, groups), 1)

    def look_up(first, fresh, codes_ref):
        def some_chunks(q, carry):
            codes = []
            for j in range(together):
                k = q * together + j
                code = codes_ref[pl.ds(pl.multiple_of(k * LANES, LANES), LANES), :]
                wide = jnp.concatenate([code.astype(jnp.int32) >> 8] * (groups // LANES), axis=1)
                hot_s[j * LANES : (j + 1) * LANES, :] = (
                    (wide == group_id).astype(jnp.float32).astype(jnp.bfloat16)
                )
                codes.append(code)
            picks = hot_s[...]
            picked = jnp.dot(
                picks, high_fields, preferred_element_type=jnp.float32
            ) + jnp.dot(picks, low_fields, preferred_element_type=jnp.float32)
            for j in range(together):
                k = q * together + j
                at = slice(j * LANES, (j + 1) * LANES)
                value = jnp.sum(
                    in_column(codes[j], picked[at, 0:LANES], 0)
                    + in_column(codes[j], picked[at, LANES : 2 * LANES], 1),
                    axis=1, keepdims=True,
                )
                for half in range(CHUNK // BLOCK):
                    held = slots_held(rank_ref, k, half, first)
                    part = value[half * SLOTS : (half + 1) * SLOTS]
                    line = jnp.sum(
                        jnp.where(held, jnp.broadcast_to(part, (SLOTS, BLOCK)), 0.0),
                        axis=0, keepdims=True,
                    )
                    lanes = slice(half * BLOCK, (half + 1) * BLOCK)
                    if fresh:
                        found[pl.ds(k, 1), lanes] = line
                    else:
                        found[pl.ds(k, 1), lanes] += line
            return carry

        lax.fori_loop(0, chunks // together, some_chunks, 0, unroll=fresh)

    look_up(0, True, table_ref)

    def one_more(number, carry):
        code_ref[...] = unfold(table_ref, places["code"], chunks).astype(jnp.int32)
        build_slots(rank_ref, code_ref, number * SLOTS, again_codes, again_groups)
        look_up(number * SLOTS, False, again_codes)
        return carry

    lax.fori_loop(1, passes_ref[0], one_more, 0)

    observed = found[...]
    resid = jnp.concatenate(
        [bundle_ref[3 * levels, :, k * CHUNK : (k + 1) * CHUNK] for k in range(chunks // 8)], axis=0
    )
    image_obs = jnp.where(rank_ref[...] >= 0, resid + observed, 0.0)
    square = jnp.where(window == 0, table_ref[places["square"] : places["square"] + 1, :], 0.0)
    all_projected = jnp.sum(projected) + jnp.sum(resid * image_obs) + square
    all_curvature = jnp.sum(curvature) + jnp.sum(image_obs * image_obs) + square
    lane = lax.broadcasted_iota(jnp.int32, (1, LANES), 1)
    sums = jnp.where(lane == 0, all_projected, jnp.where(lane == 1, all_curvature, 0.0))
    for k in range(chunks):
        sent_ref[k, :, 0:CHUNK] = found[k : k + 1, :]
        sent_ref[k, :, CHUNK : CHUNK + LANES] = sums


def gather_kernel(got_ref, observed_ref, sums_ref):
    total = got_ref[0]
    for k in range(1, got_ref.shape[0]):
        total = total + got_ref[k]
    observed_ref[...] = total[:, 0:CHUNK]
    for k in range(sums_ref.shape[0]):
        sums_ref[k] = total[:, CHUNK : CHUNK + LANES]


def update_kernel(window_ref, sums_ref, ds_ref, inc_ref, rm_ref, rs_ref, back_ref, image_ref, state_ref,
                  do_ref, ro_ref, ov_ref, observed_ref,
                  ds_out, do_out, inc_out, rm_out, ro_out, rs_out, ds_s, inc_s, rm_s, rs_s, sems):
    sums = sums_ref[0]
    for k in range(1, sums_ref.shape[0]):
        sums = sums + sums_ref[k]
    lane = lax.broadcasted_iota(jnp.int32, sums.shape, 1)
    projected = jnp.sum(jnp.where(lane == 0, sums, 0.0), axis=1, keepdims=True)
    curvature = jnp.sum(jnp.where(lane == 1, sums, 0.0), axis=1, keepdims=True)
    step = projected / curvature
    levels, rows, columns = rs_ref.shape
    parts, _, width = back_ref.shape
    per_level = parts // levels
    wide = jnp.broadcast_to(step, (rows, width))
    starts = window_ref[0] == 0
    copies = []
    for level in range(levels):
        for piece in range(per_level):
            part = level * per_level + piece
            cols = slice(piece * width, (piece + 1) * width)
            rs, rm = rs_ref[level, :, cols], rm_ref[level, :, cols]
            dual = back_ref[part, rows : 2 * rows, :] + rs
            ds_s[level, :, cols] = ds_ref[level, :, cols] + wide * dual
            inc_s[level, :, cols] = inc_ref[level, :, cols] + wide * back_ref[part, 0:rows, :]
            image = jnp.where(starts, rm, image_ref[level, :, cols])
            rm_s[level, :, cols] = rm - wide * image
            rs_s[level, :, cols] = rs - wide * state_ref[level, :, cols]
        pairs = ((ds_s, ds_out), (inc_s, inc_out), (rm_s, rm_out), (rs_s, rs_out))
        for place, (held, out) in enumerate(pairs):
            copies.append(pltpu.make_async_copy(held.at[level], out.at[level], sems.at[level, place]))
            copies[-1].start()
    narrow = jnp.broadcast_to(step, ro_ref.shape)
    ro, ov = ro_ref[...], ov_ref[...]
    dual = ro / ov
    do_out[...] = do_ref[...] + narrow * dual
    ro_out[...] = ro - narrow * (ov * dual + observed_ref[...])
    for copy in copies:
        copy.wait()


def body(windows, bricks, courant_x, courant_y, model_var, obs_var, obs_brick, obs_cell, obs_step,
         dual_state, dual_obs, increment, resid_model, resid_obs, resid_state):
    cx, cy, mv = courant_x[0], courant_y[0], model_var[0]
    ds, inc, rm, rs = dual_state[0], increment[0], resid_model[0], resid_state[0]
    levels, rows, columns = rs.shape
    per_level = windows // levels
    width = columns // per_level
    blocks = bricks
    groups = levels * (columns // LANES) * 8
    field_bytes = 4 * levels * rows * columns
    here = lax.axis_index("space").astype(jnp.int32)
    window = lax.axis_index("tm").astype(jnp.int32)
    at, window_at = here[None], window[None]

    upward = [(i, i + 1) for i in range(bricks - 1)]
    downward = [(i + 1, i) for i in range(bricks - 1)]

    packed = pl.pallas_call(
        functools.partial(pack_kernel, windows),
        out_shape=f32(windows, 3 * rows, width),
        in_specs=[VMEM] * 3,
        out_specs=VMEM,
        compiler_params=params(60),
        cost_estimate=cost(1, 1),
        name="pack",
    )(rs, rm, mv)
    windows_of = lax.all_to_all(packed, "tm", 0, 0)

    rm_next = lax.ppermute(rm, "tm", [(i + 1, i) for i in range(windows - 1)])
    near = pl.pallas_call(
        duals_kernel,
        out_shape=f32(1, 2 * CHUNK),
        in_specs=[VMEM] * 2,
        out_specs=VMEM,
        compiler_params=params(2),
        cost_estimate=cost(1, 1),
        name="duals",
    )(resid_obs, obs_var)
    distance = 1
    while 4 * distance < bricks:
        others = [
            lax.ppermute(near, "space", [(i, i ^ (distance * k)) for i in range(bricks)]) for k in (1, 2, 3)
        ]
        near = pl.pallas_call(
            join_kernel,
            out_shape=f32(4 * distance, 2 * CHUNK),
            in_specs=[VMEM] * 4,
            out_specs=VMEM,
            compiler_params=params(2),
            cost_estimate=cost(1, 1),
            name="join",
        )(near, *others)
        distance *= 4
    far = [
        lax.ppermute(near, "space", [(i, i ^ (distance * k)) for i in range(bricks)])
        for k in range(1, bricks // distance)
    ]
    slots = blocks * LANES
    field_s = pltpu.VMEM((levels, rows, columns), jnp.float32)
    table_s = pltpu.VMEM((blocks, CHUNK), jnp.int32)
    line_s = pltpu.VMEM((blocks, CHUNK), jnp.float32)
    codes_s = pltpu.VMEM((slots, LANES), jnp.float32)
    groups_s = pltpu.VMEM((blocks, LANES), jnp.int32)
    table, passes = pl.pallas_call(
        functools.partial(place_kernel, columns),
        out_shape=(f32(sections(blocks)[1], LANES), i32(1)),
        in_specs=[SMEM] + [VMEM] * 4,
        out_specs=(VMEM, SMEM),
        scratch_shapes=[table_s, table_s, table_s, groups_s],
        compiler_params=params(8),
        cost_estimate=cost(1, 1),
        name="places",
    )(at, obs_brick, obs_cell, obs_step, rm)
    lines = pl.pallas_call(
        collect_kernel,
        out_shape=f32(blocks, 2 * CHUNK),
        in_specs=[SMEM] + [VMEM] * (1 + len(far)),
        out_specs=VMEM,
        compiler_params=params(2),
        cost_estimate=cost(1, 1),
        name="collect",
    )(at, near, *far)
    bundle = pl.pallas_call(
        spread_kernel,
        out_shape=f32(3 * levels + 1, rows, columns),
        in_specs=[SMEM] + [VMEM] * 4,
        out_specs=VMEM,
        scratch_shapes=[
            table_s, table_s, codes_s, groups_s,
            pltpu.VMEM((groups, slots), jnp.bfloat16),
            pltpu.VMEM((slots, 2 * LANES), jnp.bfloat16),
            pltpu.VMEM((slots, 2 * LANES), jnp.bfloat16),
            pltpu.VMEM((groups, 2 * LANES), jnp.float32),
        ],
        compiler_params=params(24),
        cost_estimate=cost(1, 1),
        name="spread",
    )(passes, table, lines, cx, cy)

    summed = pl.pallas_call(
        scan_kernel,
        out_shape=f32(windows, 2 * rows, width),
        in_specs=[VMEM, ANY, ANY],
        out_specs=VMEM,
        compiler_params=params(4),
        cost_estimate=cost(1, 1),
        name="scan",
    )(windows_of, table, lines)
    back = lax.all_to_all(summed, "tm", 0, 0)
    up, down = pl.pallas_call(
        functools.partial(edge_kernel, levels),
        out_shape=(f32(24, columns), f32(24, columns)),
        in_specs=[VMEM, VMEM],
        out_specs=(VMEM, VMEM),
        scratch_shapes=[pltpu.VMEM((32, columns), jnp.float32)],
        compiler_params=params(6),
        cost_estimate=cost(1, 1),
        name="edges",
    )(back, bundle)
    below = lax.ppermute(up, "space", upward)
    above = lax.ppermute(down, "space", downward)

    fields = pl.pallas_call(
        gather_fields_kernel,
        out_shape=f32(3 * levels, rows, columns),
        in_specs=[VMEM] * 3 + [ANY],
        out_specs=VMEM,
        compiler_params=params(6),
        cost_estimate=cost(1, 1),
        name="fields",
    )(cx, cy, rs, up)

    image_next, image_state, sent = pl.pallas_call(
        functools.partial(image_kernel, windows),
        out_shape=(
            f32(levels, rows, columns), f32(levels, rows, columns), f32(blocks, 1, CHUNK + LANES),
        ),
        in_specs=[SMEM, SMEM] + [VMEM] * 7,
        out_specs=(VMEM, VMEM, VMEM),
        scratch_shapes=[
            pltpu.VMEM((groups, 2 * LANES), jnp.float32),
            table_s, table_s, codes_s, groups_s,
            pltpu.VMEM((min(4, blocks) * LANES, groups), jnp.bfloat16),
            line_s,
        ],
        compiler_params=params(24),
        cost_estimate=cost(1, 1),
        name="images",
    )(window_at, passes, back, below, above, fields, bundle, rm_next, table)

    image_model = lax.ppermute(image_next, "tm", [(i, i + 1) for i in range(windows - 1)])
    got = lax.all_to_all(sent, "space", 0, 0)
    observed, sums = pl.pallas_call(
        gather_kernel,
        out_shape=(f32(1, CHUNK), f32(windows, 1, LANES)),
        in_specs=[VMEM],
        out_specs=(VMEM, VMEM),
        compiler_params=params(4),
        cost_estimate=cost(1, 1),
        name="first_sums",
    )(got)
    all_sums = lax.all_to_all(sums, "tm", 0, 0)

    count = resid_obs.shape[1]
    new_ds, new_do, new_inc, new_rm, new_ro, new_rs = pl.pallas_call(
        update_kernel,
        out_shape=(
            f32(levels, rows, columns), f32(1, count), f32(levels, rows, columns),
            f32(levels, rows, columns), f32(1, count), f32(levels, rows, columns),
        ),
        in_specs=[SMEM] + [VMEM] * 12,
        out_specs=(HBM, VMEM, HBM, HBM, VMEM, HBM),
        scratch_shapes=[field_s] * 4 + [pltpu.SemaphoreType.DMA((levels, 4))],
        compiler_params=params(8),
        cost_estimate=cost(1, 1),
        name="updates",
    )(window_at, all_sums, ds, inc, rm, rs, back, image_model, image_state,
      dual_obs, resid_obs, obs_var, observed)
    return new_ds[None], new_do, new_inc[None], new_rm[None], new_ro, new_rs[None]


def solution(mesh):
    field = P("tm", None, "space", None)
    obs = P("tm", "space")
    shared = P("tm", None)
    return jax.shard_map(
        functools.partial(body, mesh.shape["tm"], mesh.shape["space"]),
        mesh=mesh,
        in_specs=(
            field, field, field, obs, shared, shared, shared,
            field, obs, field, field, obs, field,
        ),
        out_specs=(field, obs, field, field, obs, field),
        check_vma=False,
    )
```

```python
import functools

import jax
import jax.numpy as jnp
from jax import lax
from jax.experimental import pallas as pl
from jax.experimental.pallas import tpu as pltpu
from jax.sharding import PartitionSpec as P

LANES = 128
SLOTS = 64
BLOCK = 512
CHUNK = 1024
MIB = 1024 * 1024


def params(mib):
    return pltpu.CompilerParams(vmem_limit_bytes=mib * MIB)


def cost(flops, touched):
    return pl.CostEstimate(flops=flops, bytes_accessed=touched, transcendentals=0)


VMEM = pl.BlockSpec(memory_space=pltpu.VMEM)
SMEM = pl.BlockSpec(memory_space=pltpu.SMEM)
ANY = pl.BlockSpec(memory_space=pl.ANY)
HBM = pl.BlockSpec(memory_space=pltpu.HBM)


def f32(*shape):
    return jax.ShapeDtypeStruct(shape, jnp.float32)


def i32(*shape):
    return jax.ShapeDtypeStruct(shape, jnp.int32)


def b16(*shape):
    return jax.ShapeDtypeStruct(shape, jnp.bfloat16)


def duals_kernel(ro_ref, ov_ref, out_ref):
    count = ro_ref.shape[1]
    out_ref[:, 0:count] = ro_ref[...]
    out_ref[:, count : 2 * count] = ro_ref[...] / ov_ref[...]


def join_kernel(*refs):
    out_ref = refs[-1]
    rows = refs[0].shape[0]
    for place, ref in enumerate(refs[:-1]):
        out_ref[place * rows : (place + 1) * rows, :] = ref[...]


def gather_fields_kernel(cx_ref, cy_ref, rs_ref, after_ref, out_ref):
    levels = cx_ref.shape[0]
    for place, ref in enumerate((cx_ref, cy_ref, rs_ref)):
        out_ref[place * levels : (place + 1) * levels] = ref[...]


def pack_kernel(parts, rs_ref, rm_ref, mv_ref, out_ref, square_ref):
    levels, rows, columns = rs_ref.shape
    per_level = parts // levels
    width = columns // per_level
    for part in range(parts):
        level, piece = part // per_level, part % per_level
        cols = slice(piece * width, (piece + 1) * width)
        for place, ref in enumerate((rs_ref, rm_ref, mv_ref)):
            out_ref[part, rows * place : rows * (place + 1), :] = ref[level, :, cols]
    square = jnp.zeros((rows, columns), jnp.float32)
    for level in range(levels):
        square += rm_ref[level] * rm_ref[level]
    square_ref[...] = jnp.broadcast_to(jnp.sum(square), square_ref.shape)


def scan_kernel(in_ref, *rest):
    out_ref = rest[-1]
    steps = in_ref.shape[0]
    rows = in_ref.shape[1] // 3
    later = jnp.zeros((rows, in_ref.shape[2]), jnp.float32)
    for t in reversed(range(steps)):
        out_ref[t, rows : 2 * rows, :] = later
        later = later + in_ref[t, 0:rows, :]
        out_ref[t, 0:rows, :] = (
            in_ref[t, rows : 2 * rows, :] - in_ref[t, 2 * rows : 3 * rows, :] * later
        )
    total = jnp.zeros((rows, in_ref.shape[2]), jnp.float32)
    for t in range(steps):
        total = total + out_ref[t, 0:rows, :]
        out_ref[t, 0:rows, :] = total


def collect_kernel(at_ref, *refs):
    out_ref = refs[-1]
    here = at_ref[0]
    rows = refs[0].shape[0]
    for place, ref in enumerate(refs[:-1]):
        for i in range(rows):
            at = lax.bitwise_xor(jnp.int32(place * rows + i), here)
            out_ref[pl.ds(at, 1), :] = ref[i : i + 1, :]


def edge_kernel(levels, first_row, back_ref, bundle_ref, table_ref, up_ref, down_ref, rows_s):
    parts, both, width = back_ref.shape
    rows = both // 2
    per_level = parts // levels
    for part in range(parts):
        level, piece = part // per_level, part % per_level
        cols = slice(piece * width, (piece + 1) * width)
        for place, row in enumerate((rows - 1, 0, rows - 2, 1)):
            for field in range(2):
                at = 16 * field + 4 * place + level
                row_at = rows * field + row
                rows_s[at : at + 1, cols] = back_ref[part, row_at : row_at + 1, :]
    incr, incr_in, dual, dual_in = (rows_s[8 * i : 8 * i + 8, :] for i in range(4))
    lane_groups = rows_s.shape[1] // LANES
    cx, cy, cy_in = (
        jnp.concatenate(
            [
                table_ref[at : at + 8, :]
                for at in range(first_row + i * lane_groups * 8, first_row + (i + 1) * lane_groups * 8, 8)
            ],
            axis=1,
        )
        for i in range(3)
    )
    middle = bundle_ref[2 * levels]
    own, west, east, south, north = weights_of(cx, cy)
    is_up = lax.broadcasted_iota(jnp.int32, cx.shape, 0) < 4
    inner, outer = jnp.where(is_up, south, north), jnp.where(is_up, north, south)
    one = own * incr + west * west_of(incr) + east * east_of(incr) + inner * incr_in
    from_in = jnp.maximum(jnp.where(is_up, -cy_in, cy_in), 0.0) * dual_in
    kept = middle - (own * dual + east_of(west * dual) + west_of(east * dual) + from_in)
    for place, value in enumerate((incr, one, outer, outer * kept, outer * dual)):
        up_ref[4 * place : 4 * place + 4, :] = value[0:4]
        down_ref[4 * place : 4 * place + 4, :] = value[4:8]


def slots_held(rank_ref, k, half, first):
    slot = lax.broadcasted_iota(jnp.int32, (SLOTS, BLOCK), 0) + first
    row = rank_ref[pl.ds(k, 1), half * BLOCK : (half + 1) * BLOCK]
    return jnp.broadcast_to(row, (SLOTS, BLOCK)) == slot


def build_slots(rank_ref, code_ref, first, codes_ref, groups_ref):
    eye = (lax.broadcasted_iota(jnp.int32, (LANES, LANES), 0)
           == lax.broadcasted_iota(jnp.int32, (LANES, LANES), 1))

    def one_chunk(k, carry):
        parts = []
        for half in range(CHUNK // BLOCK):
            held = slots_held(rank_ref, k, half, first)
            row = (code_ref[pl.ds(k, 1), half * BLOCK : (half + 1) * BLOCK] + 1).astype(jnp.float32)
            code = jnp.sum(
                jnp.where(held, jnp.broadcast_to(row, (SLOTS, BLOCK)), 0.0), axis=1, keepdims=True
            )
            parts.append(jnp.broadcast_to(code, (SLOTS, LANES)))
        codes = jnp.concatenate(parts, axis=0) - 1.0
        codes_ref[pl.ds(pl.multiple_of(k * LANES, LANES), LANES), :] = codes
        groups_ref[pl.ds(k, 1), :] = jnp.sum(
            jnp.where(eye, codes.astype(jnp.int32) >> 8, 0), axis=0, keepdims=True
        )
        return carry

    lax.fori_loop(0, rank_ref.shape[0], one_chunk, 0, unroll=4)


def sections(chunks, lane_groups):
    tall = CHUNK // LANES
    sizes = dict(
        codes=chunks * LANES, rank=chunks * tall, code=chunks * tall, groups=chunks,
        edges=3 * lane_groups * 8,
    )
    places, at = {}, 0
    for name, size in sizes.items():
        places[name] = at
        at += size
    return places, at


def fold(table_ref, first, lines):
    tall = lines.shape[1] // LANES
    for i in range(lines.shape[0] // 8):
        for j in range(tall):
            at = first + (i * tall + j) * 8
            table_ref[at : at + 8, :] = lines[8 * i : 8 * i + 8, j * LANES : (j + 1) * LANES]


def unfold(table_ref, first, count):
    tall = CHUNK // LANES
    return jnp.concatenate([
        jnp.concatenate(
            [table_ref[first + (i * tall + j) * 8 : first + (i * tall + j) * 8 + 8, :] for j in range(tall)],
            axis=1,
        )
        for i in range(count // 8)
    ], axis=0)


def place_kernel(columns, at_ref, brick_ref, cell_ref, step_ref, cx_ref, cy_ref,
                 table_ref, passes_ref, brick_s, cell_s, step_s, groups_s):
    chunks = brick_s.shape[0]
    rank_ref, code_ref = brick_s, cell_s
    here = at_ref[0]
    lane_groups = columns // LANES
    places, _ = sections(chunks, lane_groups)
    for k in range(chunks):
        cols = slice(k * CHUNK, (k + 1) * CHUNK)
        brick_s[k : k + 1, :] = brick_ref[0:1, cols]
        cell_s[k : k + 1, :] = cell_ref[0:1, cols]
        step_s[k : k + 1, :] = step_ref[0:1, cols]
    brick, cell, step = brick_s[...], cell_s[...], step_s[...]
    line = ((cell >> 10) * 171) >> 9
    level, row = line >> 3, line & 7
    column = cell - line * columns
    group, lane = column >> 7, column & 127
    code_ref[...] = ((level * lane_groups + group) * 8 + row) * 256 + step * LANES + lane
    inside = brick == here
    count = inside.astype(jnp.int32)
    lanes = lax.broadcasted_iota(jnp.int32, count.shape, 1) & (BLOCK - 1)
    shift = 1
    while shift < BLOCK:
        count = count + jnp.where(lanes >= shift, pltpu.roll(count, shift, 1), 0)
        shift *= 2
    rank_ref[...] = jnp.where(inside, count - 1, -1)
    build_slots(rank_ref, code_ref, 0, table_ref, groups_s)
    fold(table_ref, places["rank"], rank_ref[...].astype(jnp.float32))
    fold(table_ref, places["code"], code_ref[...].astype(jnp.float32))
    table_ref[places["groups"] : places["groups"] + chunks, :] = groups_s[...].astype(jnp.float32)
    passes_ref[0] = (jnp.max(count.astype(jnp.float32)).astype(jnp.int32) + SLOTS - 1) // SLOTS
    rows = cx_ref.shape[1]
    for place, (ref, pair) in enumerate((
        (cx_ref, (rows - 1, 0)), (cy_ref, (rows - 1, 0)), (cy_ref, (rows - 2, 1)),
    )):
        edge = jnp.concatenate(
            [ref[level, row : row + 1, :] for row in pair for level in range(cx_ref.shape[0])], axis=0
        )
        for g in range(lane_groups):
            at = places["edges"] + (place * lane_groups + g) * 8
            table_ref[at : at + 8, :] = edge[:, g * LANES : (g + 1) * LANES]


def in_column(columns, values, which):
    lane = lax.broadcasted_iota(jnp.int32, columns.shape, 1) + which * LANES
    return jnp.where(columns == lane, values, 0.0)


def split_two(x):
    high = x.astype(jnp.bfloat16)
    low = (x - high.astype(jnp.float32)).astype(jnp.bfloat16)
    return high, low


def spread_kernel(passes_ref, table_ref, lines_ref, bundle_ref,
                  rank_ref, code_ref, again_codes, groups_ref, hot_s, high_s, low_s, total):
    chunks = rank_ref.shape[0]
    _, rows, columns = bundle_ref.shape
    lane_groups = columns // LANES
    groups = total.shape[0]
    levels = groups // (lane_groups * rows)
    places, _ = sections(chunks, lane_groups)
    rank_ref[...] = unfold(table_ref, places["rank"], chunks).astype(jnp.int32)
    groups_ref[...] = table_ref[places["groups"] : places["groups"] + chunks, :].astype(jnp.int32)
    for k in range(chunks // 8):
        bundle_ref[2 * levels + 1, :, k * CHUNK : (k + 1) * CHUNK] = lines_ref[8 * k : 8 * k + 8, 0:CHUNK]
    rows_ref = bundle_ref.at[2 * levels]
    group_id = lax.broadcasted_iota(jnp.int32, (groups, LANES), 0).astype(jnp.int16)
    one, zero = jnp.ones((), jnp.bfloat16), jnp.zeros((), jnp.bfloat16)

    def add_up(first, codes_ref):
        def one_chunk(k, carry):
            at = pl.ds(pl.multiple_of(k * LANES, LANES), LANES)
            parts = []
            for half in range(CHUNK // BLOCK):
                held = slots_held(rank_ref, k, half, first)
                row = lines_ref[pl.ds(k, 1), CHUNK + half * BLOCK : CHUNK + (half + 1) * BLOCK]
                dual = jnp.sum(
                    jnp.where(held, jnp.broadcast_to(row, (SLOTS, BLOCK)), 0.0),
                    axis=1, keepdims=True,
                )
                parts.append(jnp.broadcast_to(dual, (SLOTS, LANES)))
            dual = jnp.concatenate(parts, axis=0)
            columns = codes_ref[at, :].astype(jnp.int32) & 255
            high = dual.astype(jnp.bfloat16).astype(jnp.float32)
            for which in range(2):
                cols = slice(which * LANES, (which + 1) * LANES)
                high_s[at, cols] = in_column(columns, high, which).astype(jnp.bfloat16)
                low_s[at, cols] = in_column(columns, dual - high, which).astype(jnp.bfloat16)
            row = jnp.broadcast_to(groups_ref[pl.ds(k, 1), :], (16, LANES)).astype(jnp.int16)
            row = jnp.concatenate([row] * (groups // 16), axis=0)
            hot_s[:, at] = jnp.where(row == group_id, one, zero)
            return carry

        lax.fori_loop(0, chunks, one_chunk, 0, unroll=4)
        return jnp.dot(
            hot_s[...], high_s[...], preferred_element_type=jnp.float32
        ) + jnp.dot(hot_s[...], low_s[...], preferred_element_type=jnp.float32)

    total[...] = add_up(0, table_ref)

    def one_more(number, carry):
        code_ref[...] = unfold(table_ref, places["code"], chunks).astype(jnp.int32)
        build_slots(rank_ref, code_ref, number * SLOTS, again_codes, groups_ref)
        total[...] += add_up(number * SLOTS, again_codes)
        return carry

    lax.fori_loop(1, passes_ref[0], one_more, 0)

    for g in range(lane_groups):
        cols = slice(g * LANES, (g + 1) * LANES)
        for level in range(levels):
            at = (level * lane_groups + g) * 8
            bundle_ref[level, :, cols] = total[at : at + 8, 0:LANES]
            bundle_ref[levels + level, :, cols] = total[at : at + 8, LANES : 2 * LANES]
    for level in range(levels):
        for place, row in enumerate((rows - 1, 0)):
            at = 4 * place + level
            rows_ref[at : at + 1, :] = bundle_ref[levels + level, row : row + 1, :]


def west_of(v):
    return pltpu.roll(v, 1, 1)


def east_of(v):
    return pltpu.roll(v, v.shape[1] - 1, 1)


def weights_of(cx, cy):
    west, east = jnp.maximum(cx, 0.0), jnp.maximum(-cx, 0.0)
    south, north = jnp.maximum(cy, 0.0), jnp.maximum(-cy, 0.0)
    return 1.0 - jnp.abs(cx) - jnp.abs(cy), west, east, south, north


def forward(v, below, above, coeffs):
    own, west, east, south, north = coeffs
    return own * v + west * west_of(v) + east * east_of(v) + south * below + north * above


def adjoint(v, from_above, from_below, coeffs):
    own, west, east, _, _ = coeffs
    return own * v + east_of(west * v) + west_of(east * v) + from_above + from_below


def row_below(v, edge, first):
    return jnp.where(first, jnp.broadcast_to(edge, v.shape), pltpu.roll(v, 1, 0))


def row_above(v, edge, last):
    return jnp.where(last, jnp.broadcast_to(edge, v.shape), pltpu.roll(v, v.shape[0] - 1, 0))


def image_kernel(windows, bricks, window_ref, at_ref, passes_ref, back_ref, below_ref, above_ref, args_ref,
                 bundle_ref, rm_next_ref, square_ref, table_ref, next_ref, state_ref, sent_ref,
                 fields, rank_ref, code_ref, again_codes, again_groups, hot_s, found):
    levels, rows, columns = rm_next_ref.shape
    parts, _, width = back_ref.shape
    per_level = parts // levels
    chunks = found.shape[0]
    lane_groups = columns // LANES
    places, _ = sections(chunks, lane_groups)
    rank_ref[...] = unfold(table_ref, places["rank"], chunks).astype(jnp.int32)
    window, here = window_ref[0], at_ref[0]
    has_below = jnp.where(here > 0, 1.0, 0.0)
    has_above = jnp.where(here < bricks - 1, 1.0, 0.0)

    row_id = lax.broadcasted_iota(jnp.int32, (rows, columns), 0)
    first, last = row_id == 0, row_id == rows - 1
    projected = jnp.zeros((rows, columns), jnp.float32)
    curvature = jnp.zeros((rows, columns), jnp.float32)
    has_next = jnp.where(window < windows - 1, 1.0, 0.0)
    for level in range(levels):
        pieces = range(level * per_level, (level + 1) * per_level)
        incr = jnp.concatenate([back_ref[p, 0:rows, :] for p in pieces], axis=1)
        next_dual = jnp.concatenate([back_ref[p, rows : 2 * rows, :] for p in pieces], axis=1)
        coeffs = weights_of(args_ref[level], args_ref[levels + level])
        south, north = coeffs[3], coeffs[4]
        low, high = (
            [held * ref[4 * i + level : 4 * i + level + 1, :] for i in range(5)]
            for ref, held in ((below_ref, has_below), (above_ref, has_above))
        )
        after_one = forward(
            incr,
            row_below(incr, low[0], first),
            row_above(incr, high[0], last),
            coeffs,
        )
        after_two = forward(
            after_one,
            row_below(after_one, low[1] + low[2] * incr[0:1], first),
            row_above(after_one, high[1] + high[2] * incr[rows - 1 :], last),
            coeffs,
        )
        rm_next = rm_next_ref[level]
        image_next = (rm_next + incr - after_two) * has_next
        next_ref[level] = image_next
        south_dual, north_dual = south * next_dual, north * next_dual
        back_one = adjoint(
            next_dual,
            row_above(south_dual, high[4], last),
            row_below(north_dual, low[4], first),
            coeffs,
        )
        kept = bundle_ref[levels + level] - back_one
        rs = args_ref[2 * levels + level]
        image_state = (next_dual + rs) + bundle_ref[level] + adjoint(
            kept,
            row_above(south * kept, high[3] - high[2] * north_dual[rows - 1 :], last),
            row_below(north * kept, low[3] - low[2] * south_dual[0:1], first),
            coeffs,
        )
        state_ref[level] = image_state
        projected += rm_next * image_next + rs * image_state
        curvature += image_next * image_next + image_state * image_state
        for g in range(lane_groups):
            at = (level * lane_groups + g) * 8
            cols = slice(g * LANES, (g + 1) * LANES)
            fields[at : at + 8, 0:LANES] = incr[:, cols]
            fields[at : at + 8, LANES : 2 * LANES] = after_one[:, cols]

    high_fields, low_fields = split_two(fields[...])
    groups = levels * lane_groups * 8
    together = hot_s.shape[0] // LANES
    group_id = lax.broadcasted_iota(jnp.int32, (LANES, groups), 1).astype(jnp.int16)
    one, zero = jnp.ones((), jnp.bfloat16), jnp.zeros((), jnp.bfloat16)

    def look_up(first, fresh, codes_ref):
        def some_chunks(q, carry):
            codes = []
            for j in range(together):
                k = q * together + j
                code = codes_ref[pl.ds(pl.multiple_of(k * LANES, LANES), LANES), :].astype(jnp.int32)
                wide = jnp.concatenate([(code >> 8).astype(jnp.int16)] * (groups // LANES), axis=1)
                hot_s[j * LANES : (j + 1) * LANES, :] = jnp.where(wide == group_id, one, zero)
                codes.append(code & 255)
            picks = hot_s[...]
            picked = jnp.dot(
                picks, high_fields, preferred_element_type=jnp.float32
            ) + jnp.dot(picks, low_fields, preferred_element_type=jnp.float32)
            for j in range(together):
                k = q * together + j
                at = slice(j * LANES, (j + 1) * LANES)
                value = jnp.sum(
                    in_column(codes[j], picked[at, 0:LANES], 0)
                    + in_column(codes[j], picked[at, LANES : 2 * LANES], 1),
                    axis=1, keepdims=True,
                )
                for half in range(CHUNK // BLOCK):
                    held = slots_held(rank_ref, k, half, first)
                    part = value[half * SLOTS : (half + 1) * SLOTS]
                    line = jnp.sum(
                        jnp.where(held, jnp.broadcast_to(part, (SLOTS, BLOCK)), 0.0),
                        axis=0, keepdims=True,
                    )
                    lanes = slice(half * BLOCK, (half + 1) * BLOCK)
                    if fresh:
                        found[pl.ds(k, 1), lanes] = line
                    else:
                        found[pl.ds(k, 1), lanes] += line
            return carry

        lax.fori_loop(0, chunks // together, some_chunks, 0, unroll=fresh)

    look_up(0, True, table_ref)

    def one_more(number, carry):
        code_ref[...] = unfold(table_ref, places["code"], chunks).astype(jnp.int32)
        build_slots(rank_ref, code_ref, number * SLOTS, again_codes, again_groups)
        look_up(number * SLOTS, False, again_codes)
        return carry

    lax.fori_loop(1, passes_ref[0], one_more, 0)

    observed = found[...]
    resid = jnp.concatenate(
        [bundle_ref[2 * levels + 1, :, k * CHUNK : (k + 1) * CHUNK] for k in range(chunks // 8)], axis=0
    )
    image_obs = jnp.where(rank_ref[...] >= 0, resid + observed, 0.0)
    square = jnp.where(window == 0, square_ref[...], 0.0)
    all_projected = jnp.sum(projected) + jnp.sum(resid * image_obs) + square
    all_curvature = jnp.sum(curvature) + jnp.sum(image_obs * image_obs) + square
    lane = lax.broadcasted_iota(jnp.int32, (1, LANES), 1)
    sums = jnp.where(lane == 0, all_projected, jnp.where(lane == 1, all_curvature, 0.0))
    for k in range(chunks):
        sent_ref[k, :, 0:CHUNK] = found[k : k + 1, :]
        sent_ref[k, :, CHUNK : CHUNK + LANES] = sums


def gather_kernel(got_ref, observed_ref, sums_ref):
    total = got_ref[0]
    for k in range(1, got_ref.shape[0]):
        total = total + got_ref[k]
    observed_ref[...] = total[:, 0:CHUNK]
    for k in range(sums_ref.shape[0]):
        sums_ref[k] = total[:, CHUNK : CHUNK + LANES]


def update_kernel(window_ref, sums_ref, ds_ref, inc_ref, rm_hbm, rs_ref, back_ref, image_ref, state_ref,
                  do_ref, ro_ref, ov_ref, observed_ref,
                  ds_out, do_out, inc_out, rm_out, ro_out, rs_out, ds_s, inc_s, rm_s, rs_s,
                  rm_ref, sems, rm_sem):
    rm_copy = pltpu.make_async_copy(rm_hbm, rm_ref, rm_sem)
    rm_copy.start()
    sums = sums_ref[0]
    for k in range(1, sums_ref.shape[0]):
        sums = sums + sums_ref[k]
    lane = lax.broadcasted_iota(jnp.int32, sums.shape, 1)
    projected = jnp.sum(jnp.where(lane == 0, sums, 0.0), axis=1, keepdims=True)
    curvature = jnp.sum(jnp.where(lane == 1, sums, 0.0), axis=1, keepdims=True)
    step = projected / curvature
    levels, rows, columns = rs_ref.shape
    parts, _, width = back_ref.shape
    per_level = parts // levels
    wide = jnp.broadcast_to(step, (rows, width))
    starts = window_ref[0] == 0
    copies = []

    def store(place, level, held, out):
        copies.append(pltpu.make_async_copy(held.at[level], out.at[level], sems.at[level, place]))
        copies[-1].start()

    for level in range(levels):
        for piece in range(per_level):
            part = level * per_level + piece
            cols = slice(piece * width, (piece + 1) * width)
            rs = rs_ref[level, :, cols]
            dual = back_ref[part, rows : 2 * rows, :] + rs
            ds_s[level, :, cols] = ds_ref[level, :, cols] + wide * dual
            inc_s[level, :, cols] = inc_ref[level, :, cols] + wide * back_ref[part, 0:rows, :]
            rs_s[level, :, cols] = rs - wide * state_ref[level, :, cols]
        store(0, level, ds_s, ds_out)
        store(1, level, inc_s, inc_out)
        store(2, level, rs_s, rs_out)
    rm_copy.wait()
    whole_step = jnp.broadcast_to(step, (rows, columns))
    for level in range(levels):
        rm = rm_ref[level]
        rm_s[level] = rm - whole_step * jnp.where(starts, rm, image_ref[level])
        store(3, level, rm_s, rm_out)
    narrow = jnp.broadcast_to(step, ro_ref.shape)
    ro, ov = ro_ref[...], ov_ref[...]
    dual = ro / ov
    do_out[...] = do_ref[...] + narrow * dual
    ro_out[...] = ro - narrow * (ov * dual + observed_ref[...])
    for copy in copies:
        copy.wait()


def body(windows, bricks, courant_x, courant_y, model_var, obs_var, obs_brick, obs_cell, obs_step,
         dual_state, dual_obs, increment, resid_model, resid_obs, resid_state):
    cx, cy, mv = courant_x[0], courant_y[0], model_var[0]
    ds, inc, rm, rs = dual_state[0], increment[0], resid_model[0], resid_state[0]
    levels, rows, columns = rs.shape
    per_level = windows // levels
    width = columns // per_level
    blocks = bricks
    groups = levels * (columns // LANES) * 8
    field_bytes = 4 * levels * rows * columns
    here = lax.axis_index("space").astype(jnp.int32)
    window = lax.axis_index("tm").astype(jnp.int32)
    at, window_at = here[None], window[None]

    upward = [(i, (i + 1) % bricks) for i in range(bricks)]
    downward = [((i + 1) % bricks, i) for i in range(bricks)]
    later = [(i, (i + 1) % windows) for i in range(windows)]

    packed, square = pl.pallas_call(
        functools.partial(pack_kernel, windows),
        out_shape=(f32(windows, 3 * rows, width), f32(1, LANES)),
        in_specs=[VMEM] * 3,
        out_specs=(VMEM, VMEM),
        compiler_params=params(60),
        cost_estimate=cost(1, 1),
        name="pack",
    )(rs, rm, mv)
    windows_of = lax.all_to_all(packed, "tm", 0, 0)

    rm_next = lax.ppermute(rm, "tm", [(i + 1, i) for i in range(windows - 1)])
    near = pl.pallas_call(
        duals_kernel,
        out_shape=f32(1, 2 * CHUNK),
        in_specs=[VMEM] * 2,
        out_specs=VMEM,
        compiler_params=params(2),
        cost_estimate=cost(1, 1),
        name="duals",
    )(resid_obs, obs_var)
    distance = 1
    while 4 * distance < bricks:
        others = [
            lax.ppermute(near, "space", [(i, i ^ (distance * k)) for i in range(bricks)]) for k in (1, 2, 3)
        ]
        near = pl.pallas_call(
            join_kernel,
            out_shape=f32(4 * distance, 2 * CHUNK),
            in_specs=[VMEM] * 4,
            out_specs=VMEM,
            compiler_params=params(2),
            cost_estimate=cost(1, 1),
            name="join",
        )(near, *others)
        distance *= 4
    far = [
        lax.ppermute(near, "space", [(i, i ^ (distance * k)) for i in range(bricks)])
        for k in range(1, bricks // distance)
    ]
    slots = blocks * LANES
    places, table_rows = sections(blocks, columns // LANES)
    field_s = pltpu.VMEM((levels, rows, columns), jnp.float32)
    table_s = pltpu.VMEM((blocks, CHUNK), jnp.int32)
    line_s = pltpu.VMEM((blocks, CHUNK), jnp.float32)
    codes_s = pltpu.VMEM((slots, LANES), jnp.float32)
    groups_s = pltpu.VMEM((blocks, LANES), jnp.int32)
    table, passes = pl.pallas_call(
        functools.partial(place_kernel, columns),
        out_shape=(f32(table_rows, LANES), i32(1)),
        in_specs=[SMEM] + [VMEM] * 5,
        out_specs=(VMEM, SMEM),
        scratch_shapes=[table_s, table_s, table_s, groups_s],
        compiler_params=params(8),
        cost_estimate=cost(1, 1),
        name="places",
    )(at, obs_brick, obs_cell, obs_step, cx, cy)
    lines = pl.pallas_call(
        collect_kernel,
        out_shape=f32(blocks, 2 * CHUNK),
        in_specs=[SMEM] + [VMEM] * (1 + len(far)),
        out_specs=VMEM,
        compiler_params=params(2),
        cost_estimate=cost(1, 1),
        name="collect",
    )(at, near, *far)
    bundle = pl.pallas_call(
        spread_kernel,
        out_shape=f32(2 * levels + 2, rows, columns),
        in_specs=[SMEM] + [VMEM] * 2,
        out_specs=VMEM,
        scratch_shapes=[
            table_s, table_s, codes_s, groups_s,
            pltpu.VMEM((groups, slots), jnp.bfloat16),
            pltpu.VMEM((slots, 2 * LANES), jnp.bfloat16),
            pltpu.VMEM((slots, 2 * LANES), jnp.bfloat16),
            pltpu.VMEM((groups, 2 * LANES), jnp.float32),
        ],
        compiler_params=params(24),
        cost_estimate=cost(1, 1),
        name="spread",
    )(passes, table, lines)

    summed = pl.pallas_call(
        scan_kernel,
        out_shape=f32(windows, 2 * rows, width),
        in_specs=[VMEM, ANY, ANY],
        out_specs=VMEM,
        compiler_params=params(4),
        cost_estimate=cost(1, 1),
        name="scan",
    )(windows_of, table, lines)
    back = lax.all_to_all(summed, "tm", 0, 0)
    up, down = pl.pallas_call(
        functools.partial(edge_kernel, levels, places["edges"]),
        out_shape=(f32(24, columns), f32(24, columns)),
        in_specs=[VMEM, VMEM, VMEM],
        out_specs=(VMEM, VMEM),
        scratch_shapes=[pltpu.VMEM((32, columns), jnp.float32)],
        compiler_params=params(6),
        cost_estimate=cost(1, 1),
        name="edges",
    )(back, bundle, table)
    below = lax.ppermute(up, "space", upward)
    above = lax.ppermute(down, "space", downward)

    fields = pl.pallas_call(
        gather_fields_kernel,
        out_shape=f32(3 * levels, rows, columns),
        in_specs=[VMEM] * 3 + [ANY],
        out_specs=VMEM,
        compiler_params=params(6),
        cost_estimate=cost(1, 1),
        name="fields",
    )(cx, cy, rs, up)

    image_next, image_state, sent = pl.pallas_call(
        functools.partial(image_kernel, windows, bricks),
        out_shape=(
            f32(levels, rows, columns), f32(levels, rows, columns), f32(blocks, 1, CHUNK + LANES),
        ),
        in_specs=[SMEM, SMEM, SMEM] + [VMEM] * 8,
        out_specs=(VMEM, VMEM, VMEM),
        scratch_shapes=[
            pltpu.VMEM((groups, 2 * LANES), jnp.float32),
            table_s, table_s, codes_s, groups_s,
            pltpu.VMEM((min(4, blocks) * LANES, groups), jnp.bfloat16),
            line_s,
        ],
        compiler_params=params(24),
        cost_estimate=cost(1, 1),
        name="images",
    )(window_at, at, passes, back, below, above, fields, bundle, rm_next, square, table)

    image_model = lax.ppermute(image_next, "tm", later)
    got = lax.all_to_all(sent, "space", 0, 0)
    observed, sums = pl.pallas_call(
        gather_kernel,
        out_shape=(f32(1, CHUNK), f32(windows, 1, LANES)),
        in_specs=[VMEM],
        out_specs=(VMEM, VMEM),
        compiler_params=params(4),
        cost_estimate=cost(1, 1),
        name="first_sums",
    )(got)
    all_sums = lax.all_to_all(sums, "tm", 0, 0)

    count = resid_obs.shape[1]
    new_ds, new_do, new_inc, new_rm, new_ro, new_rs = pl.pallas_call(
        update_kernel,
        out_shape=(
            f32(levels, rows, columns), f32(1, count), f32(levels, rows, columns),
            f32(levels, rows, columns), f32(1, count), f32(levels, rows, columns),
        ),
        in_specs=[SMEM] + [VMEM] * 3 + [HBM] + [VMEM] * 8,
        out_specs=(HBM, VMEM, HBM, HBM, VMEM, HBM),
        scratch_shapes=[field_s] * 5
        + [pltpu.SemaphoreType.DMA((levels, 4)), pltpu.SemaphoreType.DMA(())],
        compiler_params=params(8),
        cost_estimate=cost(1, 1),
        name="updates",
    )(window_at, all_sums, ds, inc, rm, rs, back, image_model, image_state,
      dual_obs, resid_obs, obs_var, observed)
    return new_ds[None], new_do, new_inc[None], new_rm[None], new_ro, new_rs[None]


def solution(mesh):
    field = P("tm", None, "space", None)
    obs = P("tm", "space")
    shared = P("tm", None)
    return jax.shard_map(
        functools.partial(body, mesh.shape["tm"], mesh.shape["space"]),
        mesh=mesh,
        in_specs=(
            field, field, field, obs, shared, shared, shared,
            field, obs, field, field, obs, field,
        ),
        out_specs=(field, obs, field, field, obs, field),
        check_vma=False,
    )
```

```python
import functools

import jax
import jax.numpy as jnp
from jax import lax
from jax.experimental import pallas as pl
from jax.experimental.pallas import tpu as pltpu
from jax.sharding import PartitionSpec as P

LANES = 128
SLOTS = 64
BLOCK = 512
CHUNK = 1024
MIB = 1024 * 1024


def params(mib):
    return pltpu.CompilerParams(vmem_limit_bytes=mib * MIB)


def cost(flops, touched):
    return pl.CostEstimate(flops=flops, bytes_accessed=touched, transcendentals=0)


VMEM = pl.BlockSpec(memory_space=pltpu.VMEM)
SMEM = pl.BlockSpec(memory_space=pltpu.SMEM)
ANY = pl.BlockSpec(memory_space=pl.ANY)
HBM = pl.BlockSpec(memory_space=pltpu.HBM)


def f32(*shape):
    return jax.ShapeDtypeStruct(shape, jnp.float32)


def i32(*shape):
    return jax.ShapeDtypeStruct(shape, jnp.int32)


def b16(*shape):
    return jax.ShapeDtypeStruct(shape, jnp.bfloat16)


def duals_kernel(ro_ref, ov_ref, out_ref):
    count = ro_ref.shape[1]
    out_ref[:, 0:count] = ro_ref[...]
    out_ref[:, count : 2 * count] = ro_ref[...] / ov_ref[...]


def join_kernel(*refs):
    out_ref = refs[-1]
    rows = refs[0].shape[0]
    for place, ref in enumerate(refs[:-1]):
        out_ref[place * rows : (place + 1) * rows, :] = ref[...]


def gather_fields_kernel(cx_ref, cy_ref, rs_ref, after_ref, out_ref):
    levels = cx_ref.shape[0]
    for place, ref in enumerate((cx_ref, cy_ref, rs_ref)):
        out_ref[place * levels : (place + 1) * levels] = ref[...]


def pack_kernel(parts, rs_hbm, rm_hbm, mv_hbm, cx_hbm, cy_hbm, out_hbm, square_hbm, rows_hbm,
                rs_ref, rm_ref, mv_ref, cx_ref, cy_ref, out_ref, square_ref, rows_ref, in_sems, out_sems):
    levels, rows, columns = rs_ref.shape
    per_level = parts // levels
    width = columns // per_level
    fields = ((rs_hbm, rs_ref), (rm_hbm, rm_ref), (mv_hbm, mv_ref))
    loads = [
        [
            pltpu.make_async_copy(a.at[level], b.at[level], in_sems.at[level, place])
            for place, (a, b) in enumerate(fields)
        ]
        for level in range(levels)
    ]
    winds = [
        pltpu.make_async_copy(cx_hbm, cx_ref, in_sems.at[0, 3]),
        pltpu.make_async_copy(cy_hbm, cy_ref, in_sems.at[1, 3]),
    ]
    for copies in loads + [winds]:
        for copy in copies:
            copy.start()
    stores = []
    square = jnp.zeros((rows, columns), jnp.float32)
    for level in range(levels):
        for copy in loads[level]:
            copy.wait()
        for piece in range(per_level):
            part = level * per_level + piece
            cols = slice(piece * width, (piece + 1) * width)
            for place, (_, ref) in enumerate(fields):
                out_ref[part, rows * place : rows * (place + 1), :] = ref[level, :, cols]
        mine = pl.ds(level * per_level, per_level)
        stores.append(pltpu.make_async_copy(out_ref.at[mine], out_hbm.at[mine], out_sems.at[level]))
        stores[-1].start()
        square += rm_ref[level] * rm_ref[level]
    square_ref[...] = jnp.broadcast_to(jnp.sum(square), square_ref.shape)
    stores.append(pltpu.make_async_copy(square_ref, square_hbm, out_sems.at[levels]))
    stores[-1].start()
    for copy in winds:
        copy.wait()
    for place, (ref, pair) in enumerate((
        (cx_ref, (rows - 1, 0)), (cy_ref, (rows - 1, 0)), (cy_ref, (rows - 2, 1)),
    )):
        for half, row in enumerate(pair):
            for level in range(levels):
                at = 8 * place + 4 * half + level
                rows_ref[at : at + 1, :] = ref[level, row : row + 1, :]
    stores.append(pltpu.make_async_copy(rows_ref, rows_hbm, out_sems.at[levels + 1]))
    stores[-1].start()
    for copy in stores:
        copy.wait()


def scan_kernel(in_ref, *rest):
    out_ref = rest[-1]
    steps = in_ref.shape[0]
    rows = in_ref.shape[1] // 3
    later = jnp.zeros((rows, in_ref.shape[2]), jnp.float32)
    for t in reversed(range(steps)):
        out_ref[t, rows : 2 * rows, :] = later
        later = later + in_ref[t, 0:rows, :]
        out_ref[t, 0:rows, :] = (
            in_ref[t, rows : 2 * rows, :] - in_ref[t, 2 * rows : 3 * rows, :] * later
        )
    total = jnp.zeros((rows, in_ref.shape[2]), jnp.float32)
    for t in range(steps):
        total = total + out_ref[t, 0:rows, :]
        out_ref[t, 0:rows, :] = total


def collect_kernel(at_ref, *refs):
    out_ref = refs[-1]
    here = at_ref[0]
    rows = refs[0].shape[0]
    for place, ref in enumerate(refs[:-1]):
        for i in range(rows):
            at = lax.bitwise_xor(jnp.int32(place * rows + i), here)
            out_ref[pl.ds(at, 1), :] = ref[i : i + 1, :]


def edge_kernel(levels, first_row, back_ref, bundle_ref, table_ref, up_ref, down_ref, rows_s):
    parts, both, width = back_ref.shape
    rows = both // 2
    per_level = parts // levels
    for part in range(parts):
        level, piece = part // per_level, part % per_level
        cols = slice(piece * width, (piece + 1) * width)
        for place, row in enumerate((rows - 1, 0, rows - 2, 1)):
            for field in range(2):
                at = 16 * field + 4 * place + level
                row_at = rows * field + row
                rows_s[at : at + 1, cols] = back_ref[part, row_at : row_at + 1, :]
    incr, incr_in, dual, dual_in = (rows_s[8 * i : 8 * i + 8, :] for i in range(4))
    lane_groups = rows_s.shape[1] // LANES
    cx, cy, cy_in = (
        jnp.concatenate(
            [
                table_ref[at : at + 8, :]
                for at in range(first_row + i * lane_groups * 8, first_row + (i + 1) * lane_groups * 8, 8)
            ],
            axis=1,
        )
        for i in range(3)
    )
    middle = bundle_ref[2 * levels]
    own, west, east, south, north = weights_of(cx, cy)
    is_up = lax.broadcasted_iota(jnp.int32, cx.shape, 0) < 4
    inner, outer = jnp.where(is_up, south, north), jnp.where(is_up, north, south)
    one = own * incr + west * west_of(incr) + east * east_of(incr) + inner * incr_in
    from_in = jnp.maximum(jnp.where(is_up, -cy_in, cy_in), 0.0) * dual_in
    kept = middle - (own * dual + east_of(west * dual) + west_of(east * dual) + from_in)
    for place, value in enumerate((incr, one, outer, outer * kept, outer * dual)):
        for half in range(2):
            at = slice(20 * half + 4 * place, 20 * half + 4 * place + 4)
            cols = slice(half * up_ref.shape[1], (half + 1) * up_ref.shape[1])
            up_ref[at, :] = value[0:4, cols]
            down_ref[at, :] = value[4:8, cols]


def slots_held(rank_ref, k, half, first):
    slot = lax.broadcasted_iota(jnp.int32, (SLOTS, BLOCK), 0) + first
    row = rank_ref[pl.ds(k, 1), half * BLOCK : (half + 1) * BLOCK]
    return jnp.broadcast_to(row, (SLOTS, BLOCK)) == slot


def build_slots(rank_ref, code_ref, first, codes_ref, groups_ref):
    eye = (lax.broadcasted_iota(jnp.int32, (LANES, LANES), 0)
           == lax.broadcasted_iota(jnp.int32, (LANES, LANES), 1))

    def one_chunk(k, carry):
        parts = []
        for half in range(CHUNK // BLOCK):
            held = slots_held(rank_ref, k, half, first)
            row = (code_ref[pl.ds(k, 1), half * BLOCK : (half + 1) * BLOCK] + 1).astype(jnp.float32)
            code = jnp.sum(
                jnp.where(held, jnp.broadcast_to(row, (SLOTS, BLOCK)), 0.0), axis=1, keepdims=True
            )
            parts.append(jnp.broadcast_to(code, (SLOTS, LANES)))
        codes = jnp.concatenate(parts, axis=0) - 1.0
        codes_ref[pl.ds(pl.multiple_of(k * LANES, LANES), LANES), :] = codes
        groups_ref[pl.ds(k, 1), :] = jnp.sum(
            jnp.where(eye, codes.astype(jnp.int32) >> 8, 0), axis=0, keepdims=True
        )
        return carry

    lax.fori_loop(0, rank_ref.shape[0], one_chunk, 0, unroll=4)


def sections(chunks, lane_groups):
    tall = CHUNK // LANES
    sizes = dict(
        codes=chunks * LANES, rank=chunks * tall, code=chunks * tall, groups=chunks,
        edges=3 * lane_groups * 8,
    )
    places, at = {}, 0
    for name, size in sizes.items():
        places[name] = at
        at += size
    return places, at


def fold(table_ref, first, lines):
    tall = lines.shape[1] // LANES
    for i in range(lines.shape[0] // 8):
        for j in range(tall):
            at = first + (i * tall + j) * 8
            table_ref[at : at + 8, :] = lines[8 * i : 8 * i + 8, j * LANES : (j + 1) * LANES]


def unfold(table_ref, first, count):
    tall = CHUNK // LANES
    return jnp.concatenate([
        jnp.concatenate(
            [table_ref[first + (i * tall + j) * 8 : first + (i * tall + j) * 8 + 8, :] for j in range(tall)],
            axis=1,
        )
        for i in range(count // 8)
    ], axis=0)


def place_kernel(columns, at_ref, brick_ref, cell_ref, step_ref, rows_ref,
                 table_ref, passes_ref, brick_s, cell_s, step_s, groups_s):
    chunks = brick_s.shape[0]
    rank_ref, code_ref = brick_s, cell_s
    here = at_ref[0]
    lane_groups = columns // LANES
    places, _ = sections(chunks, lane_groups)
    for k in range(chunks):
        cols = slice(k * CHUNK, (k + 1) * CHUNK)
        brick_s[k : k + 1, :] = brick_ref[0:1, cols]
        cell_s[k : k + 1, :] = cell_ref[0:1, cols]
        step_s[k : k + 1, :] = step_ref[0:1, cols]
    brick, cell, step = brick_s[...], cell_s[...], step_s[...]
    line = ((cell >> 10) * 171) >> 9
    level, row = line >> 3, line & 7
    column = cell - line * columns
    group, lane = column >> 7, column & 127
    code_ref[...] = ((level * lane_groups + group) * 8 + row) * 256 + step * LANES + lane
    inside = brick == here
    count = inside.astype(jnp.int32)
    lanes = lax.broadcasted_iota(jnp.int32, count.shape, 1) & (BLOCK - 1)
    shift = 1
    while shift < BLOCK:
        count = count + jnp.where(lanes >= shift, pltpu.roll(count, shift, 1), 0)
        shift *= 2
    rank_ref[...] = jnp.where(inside, count - 1, -1)
    build_slots(rank_ref, code_ref, 0, table_ref, groups_s)
    fold(table_ref, places["rank"], rank_ref[...].astype(jnp.float32))
    fold(table_ref, places["code"], code_ref[...].astype(jnp.float32))
    table_ref[places["groups"] : places["groups"] + chunks, :] = groups_s[...].astype(jnp.float32)
    passes_ref[0] = (jnp.max(count.astype(jnp.float32)).astype(jnp.int32) + SLOTS - 1) // SLOTS
    for place in range(3):
        for g in range(lane_groups):
            at = places["edges"] + (place * lane_groups + g) * 8
            table_ref[at : at + 8, :] = rows_ref[8 * place : 8 * place + 8, g * LANES : (g + 1) * LANES]


def in_column(columns, values, which):
    lane = lax.broadcasted_iota(jnp.int32, columns.shape, 1) + which * LANES
    return jnp.where(columns == lane, values, 0.0)


def split_two(x):
    high = x.astype(jnp.bfloat16)
    low = (x - high.astype(jnp.float32)).astype(jnp.bfloat16)
    return high, low


def spread_kernel(passes_ref, table_ref, lines_ref, rm_hbm, bundle_ref, rm_out,
                  rank_ref, code_ref, again_codes, groups_ref, hot_s, high_s, low_s, total, rm_s, sems):
    rm_in = pltpu.make_async_copy(rm_hbm, rm_s, sems.at[0])
    rm_in.start()
    chunks = rank_ref.shape[0]
    _, rows, columns = bundle_ref.shape
    lane_groups = columns // LANES
    groups = total.shape[0]
    levels = groups // (lane_groups * rows)
    places, _ = sections(chunks, lane_groups)
    rank_ref[...] = unfold(table_ref, places["rank"], chunks).astype(jnp.int32)
    groups_ref[...] = table_ref[places["groups"] : places["groups"] + chunks, :].astype(jnp.int32)
    for k in range(chunks // 8):
        bundle_ref[2 * levels + 1, :, k * CHUNK : (k + 1) * CHUNK] = lines_ref[8 * k : 8 * k + 8, 0:CHUNK]
    rows_ref = bundle_ref.at[2 * levels]
    group_id = lax.broadcasted_iota(jnp.int32, (groups, LANES), 0).astype(jnp.int16)
    one, zero = jnp.ones((), jnp.bfloat16), jnp.zeros((), jnp.bfloat16)

    def add_up(first, codes_ref):
        def one_chunk(k, carry):
            at = pl.ds(pl.multiple_of(k * LANES, LANES), LANES)
            parts = []
            for half in range(CHUNK // BLOCK):
                held = slots_held(rank_ref, k, half, first)
                row = lines_ref[pl.ds(k, 1), CHUNK + half * BLOCK : CHUNK + (half + 1) * BLOCK]
                dual = jnp.sum(
                    jnp.where(held, jnp.broadcast_to(row, (SLOTS, BLOCK)), 0.0),
                    axis=1, keepdims=True,
                )
                parts.append(jnp.broadcast_to(dual, (SLOTS, LANES)))
            dual = jnp.concatenate(parts, axis=0)
            columns = codes_ref[at, :].astype(jnp.int32) & 255
            high = dual.astype(jnp.bfloat16).astype(jnp.float32)
            for which in range(2):
                cols = slice(which * LANES, (which + 1) * LANES)
                high_s[at, cols] = in_column(columns, high, which).astype(jnp.bfloat16)
                low_s[at, cols] = in_column(columns, dual - high, which).astype(jnp.bfloat16)
            row = jnp.broadcast_to(groups_ref[pl.ds(k, 1), :], (16, LANES)).astype(jnp.int16)
            row = jnp.concatenate([row] * (groups // 16), axis=0)
            hot_s[:, at] = jnp.where(row == group_id, one, zero)
            return carry

        lax.fori_loop(0, chunks, one_chunk, 0, unroll=4)
        return jnp.dot(
            hot_s[...], high_s[...], preferred_element_type=jnp.float32
        ) + jnp.dot(hot_s[...], low_s[...], preferred_element_type=jnp.float32)

    rm_in.wait()
    rm_back = pltpu.make_async_copy(rm_s, rm_out, sems.at[1])
    rm_back.start()
    total[...] = add_up(0, table_ref)

    def one_more(number, carry):
        code_ref[...] = unfold(table_ref, places["code"], chunks).astype(jnp.int32)
        build_slots(rank_ref, code_ref, number * SLOTS, again_codes, groups_ref)
        total[...] += add_up(number * SLOTS, again_codes)
        return carry

    lax.fori_loop(1, passes_ref[0], one_more, 0)

    for g in range(lane_groups):
        cols = slice(g * LANES, (g + 1) * LANES)
        for level in range(levels):
            at = (level * lane_groups + g) * 8
            bundle_ref[level, :, cols] = total[at : at + 8, 0:LANES]
            bundle_ref[levels + level, :, cols] = total[at : at + 8, LANES : 2 * LANES]
    for level in range(levels):
        for place, row in enumerate((rows - 1, 0)):
            at = 4 * place + level
            rows_ref[at : at + 1, :] = bundle_ref[levels + level, row : row + 1, :]
    rm_back.wait()


def west_of(v):
    return pltpu.roll(v, 1, 1)


def east_of(v):
    return pltpu.roll(v, v.shape[1] - 1, 1)


def weights_of(cx, cy):
    west, east = jnp.maximum(cx, 0.0), jnp.maximum(-cx, 0.0)
    south, north = jnp.maximum(cy, 0.0), jnp.maximum(-cy, 0.0)
    return 1.0 - jnp.abs(cx) - jnp.abs(cy), west, east, south, north


def forward(v, below, above, coeffs):
    own, west, east, south, north = coeffs
    return own * v + west * west_of(v) + east * east_of(v) + south * below + north * above


def adjoint(v, from_above, from_below, coeffs):
    own, west, east, _, _ = coeffs
    return own * v + east_of(west * v) + west_of(east * v) + from_above + from_below


def row_below(v, edge, first):
    return jnp.where(first, jnp.broadcast_to(edge, v.shape), pltpu.roll(v, 1, 0))


def row_above(v, edge, last):
    return jnp.where(last, jnp.broadcast_to(edge, v.shape), pltpu.roll(v, v.shape[0] - 1, 0))


def image_kernel(windows, bricks, window_ref, at_ref, passes_ref, back_ref, below_ref, above_ref, args_ref,
                 bundle_ref, rm_next_ref, square_ref, table_ref, next_ref, state_ref, sent_ref,
                 fields, rank_ref, code_ref, again_codes, again_groups, hot_s, found):
    levels, rows, columns = rm_next_ref.shape
    parts, _, width = back_ref.shape
    per_level = parts // levels
    chunks = found.shape[0]
    lane_groups = columns // LANES
    places, _ = sections(chunks, lane_groups)
    rank_ref[...] = unfold(table_ref, places["rank"], chunks).astype(jnp.int32)
    window, here = window_ref[0], at_ref[0]
    has_below = jnp.where(here > 0, 1.0, 0.0)
    has_above = jnp.where(here < bricks - 1, 1.0, 0.0)

    row_id = lax.broadcasted_iota(jnp.int32, (rows, columns), 0)
    first, last = row_id == 0, row_id == rows - 1
    projected = jnp.zeros((rows, columns), jnp.float32)
    curvature = jnp.zeros((rows, columns), jnp.float32)
    has_next = jnp.where(window < windows - 1, 1.0, 0.0)
    for level in range(levels):
        pieces = range(level * per_level, (level + 1) * per_level)
        incr = jnp.concatenate([back_ref[p, 0:rows, :] for p in pieces], axis=1)
        next_dual = jnp.concatenate([back_ref[p, rows : 2 * rows, :] for p in pieces], axis=1)
        coeffs = weights_of(args_ref[level], args_ref[levels + level])
        south, north = coeffs[3], coeffs[4]
        low, high = (
            [
                held * jnp.concatenate(
                    [ref[at : at + 1, :] for at in (4 * i + level, 20 + 4 * i + level)], axis=1
                )
                for i in range(5)
            ]
            for ref, held in ((below_ref, has_below), (above_ref, has_above))
        )
        after_one = forward(
            incr,
            row_below(incr, low[0], first),
            row_above(incr, high[0], last),
            coeffs,
        )
        after_two = forward(
            after_one,
            row_below(after_one, low[1] + low[2] * incr[0:1], first),
            row_above(after_one, high[1] + high[2] * incr[rows - 1 :], last),
            coeffs,
        )
        rm_next = rm_next_ref[level]
        image_next = (rm_next + incr - after_two) * has_next
        next_ref[level] = image_next
        south_dual, north_dual = south * next_dual, north * next_dual
        back_one = adjoint(
            next_dual,
            row_above(south_dual, high[4], last),
            row_below(north_dual, low[4], first),
            coeffs,
        )
        kept = bundle_ref[levels + level] - back_one
        rs = args_ref[2 * levels + level]
        image_state = (next_dual + rs) + bundle_ref[level] + adjoint(
            kept,
            row_above(south * kept, high[3] - high[2] * north_dual[rows - 1 :], last),
            row_below(north * kept, low[3] - low[2] * south_dual[0:1], first),
            coeffs,
        )
        state_ref[level] = image_state
        projected += rm_next * image_next + rs * image_state
        curvature += image_next * image_next + image_state * image_state
        for g in range(lane_groups):
            at = (level * lane_groups + g) * 8
            cols = slice(g * LANES, (g + 1) * LANES)
            fields[at : at + 8, 0:LANES] = incr[:, cols]
            fields[at : at + 8, LANES : 2 * LANES] = after_one[:, cols]

    high_fields, low_fields = split_two(fields[...])
    groups = levels * lane_groups * 8
    together = hot_s.shape[0] // LANES
    group_id = lax.broadcasted_iota(jnp.int32, (LANES, groups), 1).astype(jnp.int16)
    one, zero = jnp.ones((), jnp.bfloat16), jnp.zeros((), jnp.bfloat16)

    def look_up(first, fresh, codes_ref):
        def some_chunks(q, carry):
            codes = []
            for j in range(together):
                k = q * together + j
                code = codes_ref[pl.ds(pl.multiple_of(k * LANES, LANES), LANES), :].astype(jnp.int32)
                wide = jnp.concatenate([(code >> 8).astype(jnp.int16)] * (groups // LANES), axis=1)
                hot_s[j * LANES : (j + 1) * LANES, :] = jnp.where(wide == group_id, one, zero)
                codes.append(code & 255)
            picks = hot_s[...]
            picked = jnp.dot(
                picks, high_fields, preferred_element_type=jnp.float32
            ) + jnp.dot(picks, low_fields, preferred_element_type=jnp.float32)
            for j in range(together):
                k = q * together + j
                at = slice(j * LANES, (j + 1) * LANES)
                value = jnp.sum(
                    in_column(codes[j], picked[at, 0:LANES], 0)
                    + in_column(codes[j], picked[at, LANES : 2 * LANES], 1),
                    axis=1, keepdims=True,
                )
                for half in range(CHUNK // BLOCK):
                    held = slots_held(rank_ref, k, half, first)
                    part = value[half * SLOTS : (half + 1) * SLOTS]
                    line = jnp.sum(
                        jnp.where(held, jnp.broadcast_to(part, (SLOTS, BLOCK)), 0.0),
                        axis=0, keepdims=True,
                    )
                    lanes = slice(half * BLOCK, (half + 1) * BLOCK)
                    if fresh:
                        found[pl.ds(k, 1), lanes] = line
                    else:
                        found[pl.ds(k, 1), lanes] += line
            return carry

        lax.fori_loop(0, chunks // together, some_chunks, 0, unroll=fresh)

    look_up(0, True, table_ref)

    def one_more(number, carry):
        code_ref[...] = unfold(table_ref, places["code"], chunks).astype(jnp.int32)
        build_slots(rank_ref, code_ref, number * SLOTS, again_codes, again_groups)
        look_up(number * SLOTS, False, again_codes)
        return carry

    lax.fori_loop(1, passes_ref[0], one_more, 0)

    observed = found[...]
    resid = jnp.concatenate(
        [bundle_ref[2 * levels + 1, :, k * CHUNK : (k + 1) * CHUNK] for k in range(chunks // 8)], axis=0
    )
    image_obs = jnp.where(rank_ref[...] >= 0, resid + observed, 0.0)
    square = jnp.where(window == 0, square_ref[0:1, :], 0.0)
    all_projected = jnp.sum(projected) + jnp.sum(resid * image_obs) + square
    all_curvature = jnp.sum(curvature) + jnp.sum(image_obs * image_obs) + square
    lane = lax.broadcasted_iota(jnp.int32, (1, LANES), 1)
    sums = jnp.where(lane == 0, all_projected, jnp.where(lane == 1, all_curvature, 0.0))
    for k in range(chunks):
        sent_ref[k, :, 0:CHUNK] = found[k : k + 1, :]
        sent_ref[k, :, CHUNK : CHUNK + LANES] = sums


def gather_kernel(got_ref, observed_ref, sums_ref):
    total = got_ref[0]
    for k in range(1, got_ref.shape[0]):
        total = total + got_ref[k]
    observed_ref[...] = total[:, 0:CHUNK]
    for k in range(sums_ref.shape[0]):
        sums_ref[k] = total[:, CHUNK : CHUNK + LANES]


def update_kernel(window_ref, sums_ref, ds_ref, inc_ref, rm_hbm, rs_ref, back_ref, image_ref, state_ref,
                  do_ref, ro_ref, ov_ref, observed_ref,
                  ds_out, do_out, inc_out, rm_out, ro_out, rs_out, ds_s, inc_s, rm_s, rs_s,
                  rm_ref, sems, rm_sem):
    rm_copy = pltpu.make_async_copy(rm_hbm, rm_ref, rm_sem)
    rm_copy.start()
    sums = sums_ref[0]
    for k in range(1, sums_ref.shape[0]):
        sums = sums + sums_ref[k]
    lane = lax.broadcasted_iota(jnp.int32, sums.shape, 1)
    projected = jnp.sum(jnp.where(lane == 0, sums, 0.0), axis=1, keepdims=True)
    curvature = jnp.sum(jnp.where(lane == 1, sums, 0.0), axis=1, keepdims=True)
    step = projected / curvature
    levels, rows, columns = rs_ref.shape
    parts, _, width = back_ref.shape
    per_level = parts // levels
    wide = jnp.broadcast_to(step, (rows, width))
    starts = window_ref[0] == 0
    copies = []

    def store(place, level, held, out):
        copies.append(pltpu.make_async_copy(held.at[level], out.at[level], sems.at[level, place]))
        copies[-1].start()

    for level in range(levels):
        for piece in range(per_level):
            part = level * per_level + piece
            cols = slice(piece * width, (piece + 1) * width)
            rs = rs_ref[level, :, cols]
            dual = back_ref[part, rows : 2 * rows, :] + rs
            ds_s[level, :, cols] = ds_ref[level, :, cols] + wide * dual
            inc_s[level, :, cols] = inc_ref[level, :, cols] + wide * back_ref[part, 0:rows, :]
            rs_s[level, :, cols] = rs - wide * state_ref[level, :, cols]
        store(0, level, ds_s, ds_out)
        store(1, level, inc_s, inc_out)
        store(2, level, rs_s, rs_out)
    rm_copy.wait()
    whole_step = jnp.broadcast_to(step, (rows, columns))
    for level in range(levels):
        rm = rm_ref[level]
        rm_s[level] = rm - whole_step * jnp.where(starts, rm, image_ref[level])
        store(3, level, rm_s, rm_out)
    narrow = jnp.broadcast_to(step, ro_ref.shape)
    ro, ov = ro_ref[...], ov_ref[...]
    dual = ro / ov
    do_out[...] = do_ref[...] + narrow * dual
    ro_out[...] = ro - narrow * (ov * dual + observed_ref[...])
    for copy in copies:
        copy.wait()


def body(windows, bricks, courant_x, courant_y, model_var, obs_var, obs_brick, obs_cell, obs_step,
         dual_state, dual_obs, increment, resid_model, resid_obs, resid_state):
    cx, cy, mv = courant_x[0], courant_y[0], model_var[0]
    ds, inc, rm, rs = dual_state[0], increment[0], resid_model[0], resid_state[0]
    levels, rows, columns = rs.shape
    per_level = windows // levels
    width = columns // per_level
    blocks = bricks
    groups = levels * (columns // LANES) * 8
    field_bytes = 4 * levels * rows * columns
    here = lax.axis_index("space").astype(jnp.int32)
    window = lax.axis_index("tm").astype(jnp.int32)
    at, window_at = here[None], window[None]

    upward = [(i, (i + 1) % bricks) for i in range(bricks)]
    downward = [((i + 1) % bricks, i) for i in range(bricks)]
    later = [(i, (i + 1) % windows) for i in range(windows)]

    packed, square, edge_rows = pl.pallas_call(
        functools.partial(pack_kernel, windows),
        out_shape=(f32(windows, 3 * rows, width), f32(8, LANES), f32(24, columns)),
        in_specs=[HBM] * 5,
        out_specs=(HBM, HBM, HBM),
        scratch_shapes=[
            *[pltpu.VMEM((levels, rows, columns), jnp.float32)] * 5,
            pltpu.VMEM((windows, 3 * rows, width), jnp.float32),
            pltpu.VMEM((8, LANES), jnp.float32),
            pltpu.VMEM((24, columns), jnp.float32),
            pltpu.SemaphoreType.DMA((levels, 4)),
            pltpu.SemaphoreType.DMA((levels + 2,)),
        ],
        compiler_params=params(60),
        cost_estimate=cost(1, 1),
        name="pack",
    )(rs, rm, mv, cx, cy)
    windows_of = lax.all_to_all(packed, "tm", 0, 0)

    near = pl.pallas_call(
        duals_kernel,
        out_shape=f32(1, 2 * CHUNK),
        in_specs=[VMEM] * 2,
        out_specs=VMEM,
        compiler_params=params(2),
        cost_estimate=cost(1, 1),
        name="duals",
    )(resid_obs, obs_var)
    distance = 1
    while 4 * distance < bricks:
        others = [
            lax.ppermute(near, "space", [(i, i ^ (distance * k)) for i in range(bricks)]) for k in (1, 2, 3)
        ]
        near = pl.pallas_call(
            join_kernel,
            out_shape=f32(4 * distance, 2 * CHUNK),
            in_specs=[VMEM] * 4,
            out_specs=VMEM,
            compiler_params=params(2),
            cost_estimate=cost(1, 1),
            name="join",
        )(near, *others)
        distance *= 4
    far = [
        lax.ppermute(near, "space", [(i, i ^ (distance * k)) for i in range(bricks)])
        for k in range(1, bricks // distance)
    ]
    slots = blocks * LANES
    places, table_rows = sections(blocks, columns // LANES)
    field_s = pltpu.VMEM((levels, rows, columns), jnp.float32)
    table_s = pltpu.VMEM((blocks, CHUNK), jnp.int32)
    line_s = pltpu.VMEM((blocks, CHUNK), jnp.float32)
    codes_s = pltpu.VMEM((slots, LANES), jnp.float32)
    groups_s = pltpu.VMEM((blocks, LANES), jnp.int32)
    table, passes = pl.pallas_call(
        functools.partial(place_kernel, columns),
        out_shape=(f32(table_rows, LANES), i32(1)),
        in_specs=[SMEM] + [VMEM] * 4,
        out_specs=(VMEM, SMEM),
        scratch_shapes=[table_s, table_s, table_s, groups_s],
        compiler_params=params(8),
        cost_estimate=cost(1, 1),
        name="places",
    )(at, obs_brick, obs_cell, obs_step, edge_rows)
    lines = pl.pallas_call(
        collect_kernel,
        out_shape=f32(blocks, 2 * CHUNK),
        in_specs=[SMEM] + [VMEM] * (1 + len(far)),
        out_specs=VMEM,
        compiler_params=params(2),
        cost_estimate=cost(1, 1),
        name="collect",
    )(at, near, *far)
    bundle, relayed = pl.pallas_call(
        spread_kernel,
        out_shape=(f32(2 * levels + 2, rows, columns), f32(levels, rows, columns)),
        in_specs=[SMEM] + [VMEM] * 2 + [HBM],
        out_specs=(VMEM, HBM),
        scratch_shapes=[
            table_s, table_s, codes_s, groups_s,
            pltpu.VMEM((groups, slots), jnp.bfloat16),
            pltpu.VMEM((slots, 2 * LANES), jnp.bfloat16),
            pltpu.VMEM((slots, 2 * LANES), jnp.bfloat16),
            pltpu.VMEM((groups, 2 * LANES), jnp.float32),
            pltpu.VMEM((levels, rows, columns), jnp.float32),
            pltpu.SemaphoreType.DMA((2,)),
        ],
        compiler_params=params(24),
        cost_estimate=cost(1, 1),
        name="spread",
    )(passes, table, lines, rm)
    rm_next = lax.ppermute(relayed, "tm", [(i + 1, i) for i in range(windows - 1)])

    summed = pl.pallas_call(
        scan_kernel,
        out_shape=f32(windows, 2 * rows, width),
        in_specs=[VMEM, ANY, ANY],
        out_specs=VMEM,
        compiler_params=params(4),
        cost_estimate=cost(1, 1),
        name="scan",
    )(windows_of, table, lines)
    back = lax.all_to_all(summed, "tm", 0, 0)
    up, down = pl.pallas_call(
        functools.partial(edge_kernel, levels, places["edges"]),
        out_shape=(f32(40, columns // 2), f32(40, columns // 2)),
        in_specs=[VMEM, VMEM, VMEM],
        out_specs=(VMEM, VMEM),
        scratch_shapes=[pltpu.VMEM((32, columns), jnp.float32)],
        compiler_params=params(6),
        cost_estimate=cost(1, 1),
        name="edges",
    )(back, bundle, table)
    below = lax.ppermute(up, "space", upward)
    above = lax.ppermute(down, "space", downward)

    fields = pl.pallas_call(
        gather_fields_kernel,
        out_shape=f32(3 * levels, rows, columns),
        in_specs=[VMEM] * 3 + [ANY],
        out_specs=VMEM,
        compiler_params=params(6),
        cost_estimate=cost(1, 1),
        name="fields",
    )(cx, cy, rs, up)

    image_next, image_state, sent = pl.pallas_call(
        functools.partial(image_kernel, windows, bricks),
        out_shape=(
            f32(levels, rows, columns), f32(levels, rows, columns), f32(blocks, 1, CHUNK + LANES),
        ),
        in_specs=[SMEM, SMEM, SMEM] + [VMEM] * 8,
        out_specs=(VMEM, VMEM, VMEM),
        scratch_shapes=[
            pltpu.VMEM((groups, 2 * LANES), jnp.float32),
            table_s, table_s, codes_s, groups_s,
            pltpu.VMEM((min(4, blocks) * LANES, groups), jnp.bfloat16),
            line_s,
        ],
        compiler_params=params(24),
        cost_estimate=cost(1, 1),
        name="images",
    )(window_at, at, passes, back, below, above, fields, bundle, rm_next, square, table)

    image_model = lax.ppermute(image_next, "tm", later)
    got = lax.all_to_all(sent, "space", 0, 0)
    observed, sums = pl.pallas_call(
        gather_kernel,
        out_shape=(f32(1, CHUNK), f32(windows, 1, LANES)),
        in_specs=[VMEM],
        out_specs=(VMEM, VMEM),
        compiler_params=params(4),
        cost_estimate=cost(1, 1),
        name="first_sums",
    )(got)
    all_sums = lax.all_to_all(sums, "tm", 0, 0)

    count = resid_obs.shape[1]
    new_ds, new_do, new_inc, new_rm, new_ro, new_rs = pl.pallas_call(
        update_kernel,
        out_shape=(
            f32(levels, rows, columns), f32(1, count), f32(levels, rows, columns),
            f32(levels, rows, columns), f32(1, count), f32(levels, rows, columns),
        ),
        in_specs=[SMEM] + [VMEM] * 3 + [HBM] + [VMEM] * 8,
        out_specs=(HBM, VMEM, HBM, HBM, VMEM, HBM),
        scratch_shapes=[field_s] * 5
        + [pltpu.SemaphoreType.DMA((levels, 4)), pltpu.SemaphoreType.DMA(())],
        compiler_params=params(8),
        cost_estimate=cost(1, 1),
        name="updates",
    )(window_at, all_sums, ds, inc, rm, rs, back, image_model, image_state,
      dual_obs, resid_obs, obs_var, observed)
    return new_ds[None], new_do, new_inc[None], new_rm[None], new_ro, new_rs[None]


def solution(mesh):
    field = P("tm", None, "space", None)
    obs = P("tm", "space")
    shared = P("tm", None)
    return jax.shard_map(
        functools.partial(body, mesh.shape["tm"], mesh.shape["space"]),
        mesh=mesh,
        in_specs=(
            field, field, field, obs, shared, shared, shared,
            field, obs, field, field, obs, field,
        ),
        out_specs=(field, obs, field, field, obs, field),
        check_vma=False,
    )
```

```python
import functools

import jax
import jax.numpy as jnp
from jax import lax
from jax.experimental import pallas as pl
from jax.experimental.pallas import tpu as pltpu
from jax.sharding import PartitionSpec as P

LANES = 128
SLOTS = 64
BLOCK = 512
CHUNK = 1024
MIB = 1024 * 1024


def params(mib):
    return pltpu.CompilerParams(vmem_limit_bytes=mib * MIB)


def cost(flops, touched):
    return pl.CostEstimate(flops=flops, bytes_accessed=touched, transcendentals=0)


VMEM = pl.BlockSpec(memory_space=pltpu.VMEM)
SMEM = pl.BlockSpec(memory_space=pltpu.SMEM)
ANY = pl.BlockSpec(memory_space=pl.ANY)
HBM = pl.BlockSpec(memory_space=pltpu.HBM)


def f32(*shape):
    return jax.ShapeDtypeStruct(shape, jnp.float32)


def i32(*shape):
    return jax.ShapeDtypeStruct(shape, jnp.int32)


def b16(*shape):
    return jax.ShapeDtypeStruct(shape, jnp.bfloat16)


def duals_kernel(ro_ref, ov_ref, out_ref):
    count = ro_ref.shape[1]
    out_ref[:, 0:count] = ro_ref[...]
    out_ref[:, count : 2 * count] = ro_ref[...] / ov_ref[...]


def join_kernel(*refs):
    out_ref = refs[-1]
    rows = refs[0].shape[0]
    for place, ref in enumerate(refs[:-1]):
        out_ref[place * rows : (place + 1) * rows, :] = ref[...]


def gather_fields_kernel(cx_ref, cy_ref, rs_ref, after_ref, out_ref):
    levels = cx_ref.shape[0]
    for place, ref in enumerate((cx_ref, cy_ref, rs_ref)):
        out_ref[place * levels : (place + 1) * levels] = ref[...]


def pack_kernel(parts, rs_hbm, rm_hbm, mv_hbm, cx_hbm, cy_hbm, out_hbm, square_hbm, rows_hbm,
                rs_ref, rm_ref, mv_ref, cx_ref, cy_ref, out_ref, square_ref, rows_ref, in_sems, out_sems):
    levels, rows, columns = rs_ref.shape
    per_level = parts // levels
    width = columns // per_level
    fields = ((rs_hbm, rs_ref), (rm_hbm, rm_ref), (mv_hbm, mv_ref))
    loads = [
        [
            pltpu.make_async_copy(a.at[level], b.at[level], in_sems.at[level, place])
            for place, (a, b) in enumerate(fields)
        ]
        for level in range(levels)
    ]
    winds = [
        pltpu.make_async_copy(cx_hbm, cx_ref, in_sems.at[0, 3]),
        pltpu.make_async_copy(cy_hbm, cy_ref, in_sems.at[1, 3]),
    ]
    for copies in loads + [winds]:
        for copy in copies:
            copy.start()
    stores = []
    square = jnp.zeros((rows, columns), jnp.float32)
    for level in range(levels):
        for copy in loads[level]:
            copy.wait()
        for piece in range(per_level):
            part = level * per_level + piece
            cols = slice(piece * width, (piece + 1) * width)
            for place, (_, ref) in enumerate(fields):
                out_ref[part, rows * place : rows * (place + 1), :] = ref[level, :, cols]
        mine = pl.ds(level * per_level, per_level)
        stores.append(pltpu.make_async_copy(out_ref.at[mine], out_hbm.at[mine], out_sems.at[level]))
        stores[-1].start()
        square += rm_ref[level] * rm_ref[level]
    square_ref[...] = jnp.broadcast_to(jnp.sum(square), square_ref.shape)
    stores.append(pltpu.make_async_copy(square_ref, square_hbm, out_sems.at[levels]))
    stores[-1].start()
    for copy in winds:
        copy.wait()
    for place, (ref, pair) in enumerate((
        (cx_ref, (rows - 1, 0)), (cy_ref, (rows - 1, 0)), (cy_ref, (rows - 2, 1)),
    )):
        for half, row in enumerate(pair):
            for level in range(levels):
                at = 8 * place + 4 * half + level
                rows_ref[at : at + 1, :] = ref[level, row : row + 1, :]
    stores.append(pltpu.make_async_copy(rows_ref, rows_hbm, out_sems.at[levels + 1]))
    stores[-1].start()
    for copy in stores:
        copy.wait()


def scan_kernel(in_ref, *rest):
    out_ref = rest[-1]
    steps = in_ref.shape[0]
    rows = in_ref.shape[1] // 3
    later = jnp.zeros((rows, in_ref.shape[2]), jnp.float32)
    for t in reversed(range(steps)):
        out_ref[t, rows : 2 * rows, :] = later
        later = later + in_ref[t, 0:rows, :]
        out_ref[t, 0:rows, :] = (
            in_ref[t, rows : 2 * rows, :] - in_ref[t, 2 * rows : 3 * rows, :] * later
        )
    total = jnp.zeros((rows, in_ref.shape[2]), jnp.float32)
    for t in range(steps):
        total = total + out_ref[t, 0:rows, :]
        out_ref[t, 0:rows, :] = total


def collect_kernel(at_ref, *refs):
    out_ref = refs[-1]
    here = at_ref[0]
    rows = refs[0].shape[0]
    for place, ref in enumerate(refs[:-1]):
        for i in range(rows):
            at = lax.bitwise_xor(jnp.int32(place * rows + i), here)
            out_ref[pl.ds(at, 1), :] = ref[i : i + 1, :]


def edge_kernel(levels, first_row, back_ref, bundle_ref, table_ref, up_ref, down_ref, rows_s):
    parts, both, width = back_ref.shape
    rows = both // 2
    per_level = parts // levels
    for part in range(parts):
        level, piece = part // per_level, part % per_level
        cols = slice(piece * width, (piece + 1) * width)
        for place, row in enumerate((rows - 1, 0, rows - 2, 1)):
            for field in range(2):
                at = 16 * field + 4 * place + level
                row_at = rows * field + row
                rows_s[at : at + 1, cols] = back_ref[part, row_at : row_at + 1, :]
    incr, incr_in, dual, dual_in = (rows_s[8 * i : 8 * i + 8, :] for i in range(4))
    lane_groups = rows_s.shape[1] // LANES
    cx, cy, cy_in = (
        jnp.concatenate(
            [
                table_ref[at : at + 8, :]
                for at in range(first_row + i * lane_groups * 8, first_row + (i + 1) * lane_groups * 8, 8)
            ],
            axis=1,
        )
        for i in range(3)
    )
    middle = bundle_ref[2 * levels]
    own, west, east, south, north = weights_of(cx, cy)
    is_up = lax.broadcasted_iota(jnp.int32, cx.shape, 0) < 4
    inner, outer = jnp.where(is_up, south, north), jnp.where(is_up, north, south)
    one = own * incr + west * west_of(incr) + east * east_of(incr) + inner * incr_in
    from_in = jnp.maximum(jnp.where(is_up, -cy_in, cy_in), 0.0) * dual_in
    kept = middle - (own * dual + east_of(west * dual) + west_of(east * dual) + from_in)
    for place, value in enumerate((incr, one, outer, outer * kept, outer * dual)):
        for half in range(2):
            at = slice(20 * half + 4 * place, 20 * half + 4 * place + 4)
            cols = slice(half * up_ref.shape[1], (half + 1) * up_ref.shape[1])
            up_ref[at, :] = value[0:4, cols]
            down_ref[at, :] = value[4:8, cols]


def slots_held(rank_ref, k, half, first):
    slot = lax.broadcasted_iota(jnp.int32, (SLOTS, BLOCK), 0) + first
    row = rank_ref[pl.ds(k, 1), half * BLOCK : (half + 1) * BLOCK]
    return jnp.broadcast_to(row, (SLOTS, BLOCK)) == slot


def build_slots(rank_ref, code_ref, first, codes_ref, groups_ref):
    eye = (lax.broadcasted_iota(jnp.int32, (LANES, LANES), 0)
           == lax.broadcasted_iota(jnp.int32, (LANES, LANES), 1))

    def one_chunk(k, carry):
        parts = []
        for half in range(CHUNK // BLOCK):
            held = slots_held(rank_ref, k, half, first)
            row = (code_ref[pl.ds(k, 1), half * BLOCK : (half + 1) * BLOCK] + 1).astype(jnp.float32)
            code = jnp.sum(
                jnp.where(held, jnp.broadcast_to(row, (SLOTS, BLOCK)), 0.0), axis=1, keepdims=True
            )
            parts.append(jnp.broadcast_to(code, (SLOTS, LANES)))
        codes = jnp.concatenate(parts, axis=0) - 1.0
        codes_ref[pl.ds(pl.multiple_of(k * LANES, LANES), LANES), :] = codes
        groups_ref[pl.ds(k, 1), :] = jnp.sum(
            jnp.where(eye, codes.astype(jnp.int32) >> 8, 0), axis=0, keepdims=True
        )
        return carry

    lax.fori_loop(0, rank_ref.shape[0], one_chunk, 0, unroll=8)


def sections(chunks, lane_groups):
    tall = CHUNK // LANES
    sizes = dict(
        codes=chunks * LANES, rank=chunks * tall, code=chunks * tall, groups=chunks,
        edges=3 * lane_groups * 8,
    )
    places, at = {}, 0
    for name, size in sizes.items():
        places[name] = at
        at += size
    return places, at


def fold(table_ref, first, lines):
    tall = lines.shape[1] // LANES
    for i in range(lines.shape[0] // 8):
        for j in range(tall):
            at = first + (i * tall + j) * 8
            table_ref[at : at + 8, :] = lines[8 * i : 8 * i + 8, j * LANES : (j + 1) * LANES]


def unfold(table_ref, first, count):
    tall = CHUNK // LANES
    return jnp.concatenate([
        jnp.concatenate(
            [table_ref[first + (i * tall + j) * 8 : first + (i * tall + j) * 8 + 8, :] for j in range(tall)],
            axis=1,
        )
        for i in range(count // 8)
    ], axis=0)


def place_kernel(columns, at_ref, brick_ref, cell_ref, step_ref, rows_ref,
                 table_ref, passes_ref, brick_s, cell_s, step_s, groups_s):
    chunks = brick_s.shape[0]
    rank_ref, code_ref = brick_s, cell_s
    here = at_ref[0]
    lane_groups = columns // LANES
    places, _ = sections(chunks, lane_groups)
    for k in range(chunks):
        cols = slice(k * CHUNK, (k + 1) * CHUNK)
        brick_s[k : k + 1, :] = brick_ref[0:1, cols]
        cell_s[k : k + 1, :] = cell_ref[0:1, cols]
        step_s[k : k + 1, :] = step_ref[0:1, cols]
    brick, cell, step = brick_s[...], cell_s[...], step_s[...]
    line = ((cell >> 10) * 171) >> 9
    level, row = line >> 3, line & 7
    column = cell - line * columns
    group, lane = column >> 7, column & 127
    code_ref[...] = ((level * lane_groups + group) * 8 + row) * 256 + step * LANES + lane
    inside = brick == here
    count = inside.astype(jnp.int32)
    lanes = lax.broadcasted_iota(jnp.int32, count.shape, 1) & (BLOCK - 1)
    shift = 1
    while shift < BLOCK:
        count = count + jnp.where(lanes >= shift, pltpu.roll(count, shift, 1), 0)
        shift *= 2
    rank_ref[...] = jnp.where(inside, count - 1, -1)
    build_slots(rank_ref, code_ref, 0, table_ref, groups_s)
    fold(table_ref, places["rank"], rank_ref[...].astype(jnp.float32))
    fold(table_ref, places["code"], code_ref[...].astype(jnp.float32))
    table_ref[places["groups"] : places["groups"] + chunks, :] = groups_s[...].astype(jnp.float32)
    passes_ref[0] = (jnp.max(count.astype(jnp.float32)).astype(jnp.int32) + SLOTS - 1) // SLOTS
    for place in range(3):
        for g in range(lane_groups):
            at = places["edges"] + (place * lane_groups + g) * 8
            table_ref[at : at + 8, :] = rows_ref[8 * place : 8 * place + 8, g * LANES : (g + 1) * LANES]


def in_column(columns, values, which):
    lane = lax.broadcasted_iota(jnp.int32, columns.shape, 1) + which * LANES
    return jnp.where(columns == lane, values, 0.0)


def split_two(x):
    high = x.astype(jnp.bfloat16)
    low = (x - high.astype(jnp.float32)).astype(jnp.bfloat16)
    return high, low


def spread_kernel(passes_ref, table_ref, lines_ref, rm_hbm, bundle_ref, rm_out,
                  rank_ref, code_ref, again_codes, groups_ref, hot_s, high_s, low_s, total, rm_s, sems):
    rm_in = pltpu.make_async_copy(rm_hbm, rm_s, sems.at[0])
    rm_in.start()
    chunks = rank_ref.shape[0]
    _, rows, columns = bundle_ref.shape
    lane_groups = columns // LANES
    groups = total.shape[0]
    levels = groups // (lane_groups * rows)
    places, _ = sections(chunks, lane_groups)
    rank_ref[...] = unfold(table_ref, places["rank"], chunks).astype(jnp.int32)
    groups_ref[...] = table_ref[places["groups"] : places["groups"] + chunks, :].astype(jnp.int32)
    for k in range(chunks // 8):
        bundle_ref[2 * levels + 1, :, k * CHUNK : (k + 1) * CHUNK] = lines_ref[8 * k : 8 * k + 8, 0:CHUNK]
    rows_ref = bundle_ref.at[2 * levels]
    group_id = lax.broadcasted_iota(jnp.int32, (groups, LANES), 0).astype(jnp.int16)
    one, zero = jnp.ones((), jnp.bfloat16), jnp.zeros((), jnp.bfloat16)

    def add_up(first, codes_ref):
        def one_chunk(k, carry):
            at = pl.ds(pl.multiple_of(k * LANES, LANES), LANES)
            parts = []
            for half in range(CHUNK // BLOCK):
                held = slots_held(rank_ref, k, half, first)
                row = lines_ref[pl.ds(k, 1), CHUNK + half * BLOCK : CHUNK + (half + 1) * BLOCK]
                dual = jnp.sum(
                    jnp.where(held, jnp.broadcast_to(row, (SLOTS, BLOCK)), 0.0),
                    axis=1, keepdims=True,
                )
                parts.append(jnp.broadcast_to(dual, (SLOTS, LANES)))
            dual = jnp.concatenate(parts, axis=0)
            columns = codes_ref[at, :].astype(jnp.int32) & 255
            high = dual.astype(jnp.bfloat16).astype(jnp.float32)
            for which in range(2):
                cols = slice(which * LANES, (which + 1) * LANES)
                high_s[at, cols] = in_column(columns, high, which).astype(jnp.bfloat16)
                low_s[at, cols] = in_column(columns, dual - high, which).astype(jnp.bfloat16)
            row = jnp.broadcast_to(groups_ref[pl.ds(k, 1), :], (16, LANES)).astype(jnp.int16)
            row = jnp.concatenate([row] * (groups // 16), axis=0)
            hot_s[:, at] = jnp.where(row == group_id, one, zero)
            return carry

        lax.fori_loop(0, chunks, one_chunk, 0, unroll=8)
        return jnp.dot(
            hot_s[...], high_s[...], preferred_element_type=jnp.float32
        ) + jnp.dot(hot_s[...], low_s[...], preferred_element_type=jnp.float32)

    rm_in.wait()
    rm_back = pltpu.make_async_copy(rm_s, rm_out, sems.at[1])
    rm_back.start()
    total[...] = add_up(0, table_ref)

    def one_more(number, carry):
        code_ref[...] = unfold(table_ref, places["code"], chunks).astype(jnp.int32)
        build_slots(rank_ref, code_ref, number * SLOTS, again_codes, groups_ref)
        total[...] += add_up(number * SLOTS, again_codes)
        return carry

    lax.fori_loop(1, passes_ref[0], one_more, 0)

    for g in range(lane_groups):
        cols = slice(g * LANES, (g + 1) * LANES)
        for level in range(levels):
            at = (level * lane_groups + g) * 8
            bundle_ref[level, :, cols] = total[at : at + 8, 0:LANES]
            bundle_ref[levels + level, :, cols] = total[at : at + 8, LANES : 2 * LANES]
    for level in range(levels):
        for place, row in enumerate((rows - 1, 0)):
            at = 4 * place + level
            rows_ref[at : at + 1, :] = bundle_ref[levels + level, row : row + 1, :]
    rm_back.wait()


def west_of(v):
    return pltpu.roll(v, 1, 1)


def east_of(v):
    return pltpu.roll(v, v.shape[1] - 1, 1)


def weights_of(cx, cy):
    west, east = jnp.maximum(cx, 0.0), jnp.maximum(-cx, 0.0)
    south, north = jnp.maximum(cy, 0.0), jnp.maximum(-cy, 0.0)
    return 1.0 - jnp.abs(cx) - jnp.abs(cy), west, east, south, north


def forward(v, below, above, coeffs):
    own, west, east, south, north = coeffs
    return own * v + west * west_of(v) + east * east_of(v) + south * below + north * above


def adjoint(v, from_above, from_below, coeffs):
    own, west, east, _, _ = coeffs
    return own * v + east_of(west * v) + west_of(east * v) + from_above + from_below


def row_below(v, edge, first):
    return jnp.where(first, jnp.broadcast_to(edge, v.shape), pltpu.roll(v, 1, 0))


def row_above(v, edge, last):
    return jnp.where(last, jnp.broadcast_to(edge, v.shape), pltpu.roll(v, v.shape[0] - 1, 0))


def image_kernel(windows, bricks, window_ref, at_ref, passes_ref, back_ref, below_hbm, above_hbm, args_ref,
                 bundle_ref, rm_next_hbm, square_ref, table_ref, next_ref, state_ref, sent_ref,
                 fields, rank_ref, code_ref, again_codes, again_groups, hot_s, found,
                 below_ref, above_ref, rm_next_ref, sems):
    arrivals = [
        pltpu.make_async_copy(a, b, sems.at[i])
        for i, (a, b) in enumerate(
            ((below_hbm, below_ref), (above_hbm, above_ref), (rm_next_hbm, rm_next_ref))
        )
    ]
    for copy in arrivals:
        copy.start()
    levels, rows, columns = rm_next_ref.shape
    parts, _, width = back_ref.shape
    per_level = parts // levels
    chunks = found.shape[0]
    lane_groups = columns // LANES
    places, _ = sections(chunks, lane_groups)
    rank_ref[...] = unfold(table_ref, places["rank"], chunks).astype(jnp.int32)
    window, here = window_ref[0], at_ref[0]
    has_below = jnp.where(here > 0, 1.0, 0.0)
    has_above = jnp.where(here < bricks - 1, 1.0, 0.0)

    groups = levels * lane_groups * 8
    group_id = lax.broadcasted_iota(jnp.int32, (LANES, groups), 1).astype(jnp.int16)
    one, zero = jnp.ones((), jnp.bfloat16), jnp.zeros((), jnp.bfloat16)

    def make_hot(codes_ref):
        def one_chunk(k, carry):
            at = pl.ds(pl.multiple_of(k * LANES, LANES), LANES)
            group = (codes_ref[at, :].astype(jnp.int32) >> 8).astype(jnp.int16)
            wide = jnp.concatenate([group] * (groups // LANES), axis=1)
            hot_s[at, :] = jnp.where(wide == group_id, one, zero)
            return carry

        lax.fori_loop(0, chunks, one_chunk, 0, unroll=8)

    make_hot(table_ref)
    for copy in arrivals:
        copy.wait()

    row_id = lax.broadcasted_iota(jnp.int32, (rows, columns), 0)
    first, last = row_id == 0, row_id == rows - 1
    projected = jnp.zeros((rows, columns), jnp.float32)
    curvature = jnp.zeros((rows, columns), jnp.float32)
    has_next = jnp.where(window < windows - 1, 1.0, 0.0)
    for level in range(levels):
        pieces = range(level * per_level, (level + 1) * per_level)
        incr = jnp.concatenate([back_ref[p, 0:rows, :] for p in pieces], axis=1)
        next_dual = jnp.concatenate([back_ref[p, rows : 2 * rows, :] for p in pieces], axis=1)
        coeffs = weights_of(args_ref[level], args_ref[levels + level])
        south, north = coeffs[3], coeffs[4]
        low, high = (
            [
                held * jnp.concatenate(
                    [ref[at : at + 1, :] for at in (4 * i + level, 20 + 4 * i + level)], axis=1
                )
                for i in range(5)
            ]
            for ref, held in ((below_ref, has_below), (above_ref, has_above))
        )
        after_one = forward(
            incr,
            row_below(incr, low[0], first),
            row_above(incr, high[0], last),
            coeffs,
        )
        after_two = forward(
            after_one,
            row_below(after_one, low[1] + low[2] * incr[0:1], first),
            row_above(after_one, high[1] + high[2] * incr[rows - 1 :], last),
            coeffs,
        )
        rm_next = rm_next_ref[level]
        image_next = (rm_next + incr - after_two) * has_next
        next_ref[level] = image_next
        south_dual, north_dual = south * next_dual, north * next_dual
        back_one = adjoint(
            next_dual,
            row_above(south_dual, high[4], last),
            row_below(north_dual, low[4], first),
            coeffs,
        )
        kept = bundle_ref[levels + level] - back_one
        rs = args_ref[2 * levels + level]
        image_state = (next_dual + rs) + bundle_ref[level] + adjoint(
            kept,
            row_above(south * kept, high[3] - high[2] * north_dual[rows - 1 :], last),
            row_below(north * kept, low[3] - low[2] * south_dual[0:1], first),
            coeffs,
        )
        state_ref[level] = image_state
        projected += rm_next * image_next + rs * image_state
        curvature += image_next * image_next + image_state * image_state
        for g in range(lane_groups):
            at = (level * lane_groups + g) * 8
            cols = slice(g * LANES, (g + 1) * LANES)
            fields[at : at + 8, 0:LANES] = incr[:, cols]
            fields[at : at + 8, LANES : 2 * LANES] = after_one[:, cols]

    high_fields, low_fields = split_two(fields[...])
    together = min(4, chunks)

    def look_up(first, fresh, codes_ref):
        def some_chunks(q, carry):
            codes = [
                codes_ref[pl.ds(pl.multiple_of((q * together + j) * LANES, LANES), LANES), :].astype(jnp.int32) & 255
                for j in range(together)
            ]
            picks = hot_s[pl.ds(pl.multiple_of(q * together * LANES, together * LANES), together * LANES), :]
            picked = jnp.dot(
                picks, high_fields, preferred_element_type=jnp.float32
            ) + jnp.dot(picks, low_fields, preferred_element_type=jnp.float32)
            for j in range(together):
                k = q * together + j
                at = slice(j * LANES, (j + 1) * LANES)
                value = jnp.sum(
                    in_column(codes[j], picked[at, 0:LANES], 0)
                    + in_column(codes[j], picked[at, LANES : 2 * LANES], 1),
                    axis=1, keepdims=True,
                )
                for half in range(CHUNK // BLOCK):
                    held = slots_held(rank_ref, k, half, first)
                    part = value[half * SLOTS : (half + 1) * SLOTS]
                    line = jnp.sum(
                        jnp.where(held, jnp.broadcast_to(part, (SLOTS, BLOCK)), 0.0),
                        axis=0, keepdims=True,
                    )
                    lanes = slice(half * BLOCK, (half + 1) * BLOCK)
                    if fresh:
                        found[pl.ds(k, 1), lanes] = line
                    else:
                        found[pl.ds(k, 1), lanes] += line
            return carry

        lax.fori_loop(0, chunks // together, some_chunks, 0, unroll=fresh)

    look_up(0, True, table_ref)

    def one_more(number, carry):
        code_ref[...] = unfold(table_ref, places["code"], chunks).astype(jnp.int32)
        build_slots(rank_ref, code_ref, number * SLOTS, again_codes, again_groups)
        make_hot(again_codes)
        look_up(number * SLOTS, False, again_codes)
        return carry

    lax.fori_loop(1, passes_ref[0], one_more, 0)

    observed = found[...]
    resid = jnp.concatenate(
        [bundle_ref[2 * levels + 1, :, k * CHUNK : (k + 1) * CHUNK] for k in range(chunks // 8)], axis=0
    )
    image_obs = jnp.where(rank_ref[...] >= 0, resid + observed, 0.0)
    square = jnp.where(window == 0, square_ref[0:1, :], 0.0)
    all_projected = jnp.sum(projected) + jnp.sum(resid * image_obs) + square
    all_curvature = jnp.sum(curvature) + jnp.sum(image_obs * image_obs) + square
    lane = lax.broadcasted_iota(jnp.int32, (1, LANES), 1)
    sums = jnp.where(lane == 0, all_projected, jnp.where(lane == 1, all_curvature, 0.0))
    for k in range(chunks):
        sent_ref[k, :, 0:CHUNK] = found[k : k + 1, :]
        sent_ref[k, :, CHUNK : CHUNK + LANES] = sums


def gather_kernel(got_ref, observed_ref, sums_ref):
    total = got_ref[0]
    for k in range(1, got_ref.shape[0]):
        total = total + got_ref[k]
    observed_ref[...] = total[:, 0:CHUNK]
    for k in range(sums_ref.shape[0]):
        sums_ref[k] = total[:, CHUNK : CHUNK + LANES]


def update_kernel(window_ref, sums_ref, ds_ref, inc_ref, rm_hbm, rs_ref, back_ref, image_ref, state_ref,
                  do_ref, ro_ref, ov_ref, observed_ref,
                  ds_out, do_out, inc_out, rm_out, ro_out, rs_out, ds_s, inc_s, rm_s, rs_s,
                  rm_ref, sems, rm_sem):
    rm_copy = pltpu.make_async_copy(rm_hbm, rm_ref, rm_sem)
    rm_copy.start()
    sums = sums_ref[0]
    for k in range(1, sums_ref.shape[0]):
        sums = sums + sums_ref[k]
    lane = lax.broadcasted_iota(jnp.int32, sums.shape, 1)
    projected = jnp.sum(jnp.where(lane == 0, sums, 0.0), axis=1, keepdims=True)
    curvature = jnp.sum(jnp.where(lane == 1, sums, 0.0), axis=1, keepdims=True)
    step = projected / curvature
    levels, rows, columns = rs_ref.shape
    parts, _, width = back_ref.shape
    per_level = parts // levels
    wide = jnp.broadcast_to(step, (rows, width))
    starts = window_ref[0] == 0
    copies = []

    def store(place, level, held, out):
        copies.append(pltpu.make_async_copy(held.at[level], out.at[level], sems.at[level, place]))
        copies[-1].start()

    for level in range(levels):
        for piece in range(per_level):
            part = level * per_level + piece
            cols = slice(piece * width, (piece + 1) * width)
            rs = rs_ref[level, :, cols]
            dual = back_ref[part, rows : 2 * rows, :] + rs
            ds_s[level, :, cols] = ds_ref[level, :, cols] + wide * dual
            inc_s[level, :, cols] = inc_ref[level, :, cols] + wide * back_ref[part, 0:rows, :]
            rs_s[level, :, cols] = rs - wide * state_ref[level, :, cols]
        store(0, level, ds_s, ds_out)
        store(1, level, inc_s, inc_out)
        store(2, level, rs_s, rs_out)
    rm_copy.wait()
    whole_step = jnp.broadcast_to(step, (rows, columns))
    for level in range(levels):
        rm = rm_ref[level]
        rm_s[level] = rm - whole_step * jnp.where(starts, rm, image_ref[level])
        store(3, level, rm_s, rm_out)
    narrow = jnp.broadcast_to(step, ro_ref.shape)
    ro, ov = ro_ref[...], ov_ref[...]
    dual = ro / ov
    do_out[...] = do_ref[...] + narrow * dual
    ro_out[...] = ro - narrow * (ov * dual + observed_ref[...])
    for copy in copies:
        copy.wait()


def body(windows, bricks, courant_x, courant_y, model_var, obs_var, obs_brick, obs_cell, obs_step,
         dual_state, dual_obs, increment, resid_model, resid_obs, resid_state):
    cx, cy, mv = courant_x[0], courant_y[0], model_var[0]
    ds, inc, rm, rs = dual_state[0], increment[0], resid_model[0], resid_state[0]
    levels, rows, columns = rs.shape
    per_level = windows // levels
    width = columns // per_level
    blocks = bricks
    groups = levels * (columns // LANES) * 8
    field_bytes = 4 * levels * rows * columns
    here = lax.axis_index("space").astype(jnp.int32)
    window = lax.axis_index("tm").astype(jnp.int32)
    at, window_at = here[None], window[None]

    upward = [(i, (i + 1) % bricks) for i in range(bricks)]
    downward = [((i + 1) % bricks, i) for i in range(bricks)]
    later = [(i, (i + 1) % windows) for i in range(windows)]

    packed, square, edge_rows = pl.pallas_call(
        functools.partial(pack_kernel, windows),
        out_shape=(f32(windows, 3 * rows, width), f32(8, LANES), f32(24, columns)),
        in_specs=[HBM] * 5,
        out_specs=(HBM, HBM, HBM),
        scratch_shapes=[
            *[pltpu.VMEM((levels, rows, columns), jnp.float32)] * 5,
            pltpu.VMEM((windows, 3 * rows, width), jnp.float32),
            pltpu.VMEM((8, LANES), jnp.float32),
            pltpu.VMEM((24, columns), jnp.float32),
            pltpu.SemaphoreType.DMA((levels, 4)),
            pltpu.SemaphoreType.DMA((levels + 2,)),
        ],
        compiler_params=params(60),
        cost_estimate=cost(1, 1),
        name="pack",
    )(rs, rm, mv, cx, cy)
    windows_of = lax.all_to_all(packed, "tm", 0, 0)

    near = pl.pallas_call(
        duals_kernel,
        out_shape=f32(1, 2 * CHUNK),
        in_specs=[VMEM] * 2,
        out_specs=VMEM,
        compiler_params=params(2),
        cost_estimate=cost(1, 1),
        name="duals",
    )(resid_obs, obs_var)
    distance = 1
    while 4 * distance < bricks:
        others = [
            lax.ppermute(near, "space", [(i, i ^ (distance * k)) for i in range(bricks)]) for k in (1, 2, 3)
        ]
        near = pl.pallas_call(
            join_kernel,
            out_shape=f32(4 * distance, 2 * CHUNK),
            in_specs=[VMEM] * 4,
            out_specs=VMEM,
            compiler_params=params(2),
            cost_estimate=cost(1, 1),
            name="join",
        )(near, *others)
        distance *= 4
    far = [
        lax.ppermute(near, "space", [(i, i ^ (distance * k)) for i in range(bricks)])
        for k in range(1, bricks // distance)
    ]
    slots = blocks * LANES
    places, table_rows = sections(blocks, columns // LANES)
    field_s = pltpu.VMEM((levels, rows, columns), jnp.float32)
    table_s = pltpu.VMEM((blocks, CHUNK), jnp.int32)
    line_s = pltpu.VMEM((blocks, CHUNK), jnp.float32)
    codes_s = pltpu.VMEM((slots, LANES), jnp.float32)
    groups_s = pltpu.VMEM((blocks, LANES), jnp.int32)
    table, passes = pl.pallas_call(
        functools.partial(place_kernel, columns),
        out_shape=(f32(table_rows, LANES), i32(1)),
        in_specs=[SMEM] + [VMEM] * 4,
        out_specs=(VMEM, SMEM),
        scratch_shapes=[table_s, table_s, table_s, groups_s],
        compiler_params=params(8),
        cost_estimate=cost(1, 1),
        name="places",
    )(at, obs_brick, obs_cell, obs_step, edge_rows)
    lines = pl.pallas_call(
        collect_kernel,
        out_shape=f32(blocks, 2 * CHUNK),
        in_specs=[SMEM] + [VMEM] * (1 + len(far)),
        out_specs=VMEM,
        compiler_params=params(2),
        cost_estimate=cost(1, 1),
        name="collect",
    )(at, near, *far)
    bundle, relayed = pl.pallas_call(
        spread_kernel,
        out_shape=(f32(2 * levels + 2, rows, columns), f32(levels, rows, columns)),
        in_specs=[SMEM] + [VMEM] * 2 + [HBM],
        out_specs=(VMEM, HBM),
        scratch_shapes=[
            table_s, table_s, codes_s, groups_s,
            pltpu.VMEM((groups, slots), jnp.bfloat16),
            pltpu.VMEM((slots, 2 * LANES), jnp.bfloat16),
            pltpu.VMEM((slots, 2 * LANES), jnp.bfloat16),
            pltpu.VMEM((groups, 2 * LANES), jnp.float32),
            pltpu.VMEM((levels, rows, columns), jnp.float32),
            pltpu.SemaphoreType.DMA((2,)),
        ],
        compiler_params=params(24),
        cost_estimate=cost(1, 1),
        name="spread",
    )(passes, table, lines, rm)
    rm_next = lax.ppermute(relayed, "tm", [(i + 1, i) for i in range(windows - 1)])

    summed = pl.pallas_call(
        scan_kernel,
        out_shape=f32(windows, 2 * rows, width),
        in_specs=[VMEM, ANY, ANY],
        out_specs=VMEM,
        compiler_params=params(4),
        cost_estimate=cost(1, 1),
        name="scan",
    )(windows_of, table, lines)
    back = lax.all_to_all(summed, "tm", 0, 0)
    up, down = pl.pallas_call(
        functools.partial(edge_kernel, levels, places["edges"]),
        out_shape=(f32(40, columns // 2), f32(40, columns // 2)),
        in_specs=[VMEM, VMEM, VMEM],
        out_specs=(VMEM, VMEM),
        scratch_shapes=[pltpu.VMEM((32, columns), jnp.float32)],
        compiler_params=params(6),
        cost_estimate=cost(1, 1),
        name="edges",
    )(back, bundle, table)
    below = lax.ppermute(up, "space", upward)
    above = lax.ppermute(down, "space", downward)

    fields = pl.pallas_call(
        gather_fields_kernel,
        out_shape=f32(3 * levels, rows, columns),
        in_specs=[VMEM] * 3 + [ANY],
        out_specs=VMEM,
        compiler_params=params(6),
        cost_estimate=cost(1, 1),
        name="fields",
    )(cx, cy, rs, up)

    image_next, image_state, sent = pl.pallas_call(
        functools.partial(image_kernel, windows, bricks),
        out_shape=(
            f32(levels, rows, columns), f32(levels, rows, columns), f32(blocks, 1, CHUNK + LANES),
        ),
        in_specs=[SMEM] * 3 + [VMEM, HBM, HBM, VMEM, VMEM, HBM, VMEM, VMEM],
        out_specs=(VMEM, VMEM, VMEM),
        scratch_shapes=[
            pltpu.VMEM((groups, 2 * LANES), jnp.float32),
            table_s, table_s, codes_s, groups_s,
            pltpu.VMEM((slots, groups), jnp.bfloat16),
            line_s,
            pltpu.VMEM((40, columns // 2), jnp.float32), pltpu.VMEM((40, columns // 2), jnp.float32),
            pltpu.VMEM((levels, rows, columns), jnp.float32),
            pltpu.SemaphoreType.DMA((3,)),
        ],
        compiler_params=params(24),
        cost_estimate=cost(1, 1),
        name="images",
    )(window_at, at, passes, back, below, above, fields, bundle, rm_next, square, table)

    image_model = lax.ppermute(image_next, "tm", later)
    got = lax.all_to_all(sent, "space", 0, 0)
    observed, sums = pl.pallas_call(
        gather_kernel,
        out_shape=(f32(1, CHUNK), f32(windows, 1, LANES)),
        in_specs=[VMEM],
        out_specs=(VMEM, VMEM),
        compiler_params=params(4),
        cost_estimate=cost(1, 1),
        name="first_sums",
    )(got)
    all_sums = lax.all_to_all(sums, "tm", 0, 0)

    count = resid_obs.shape[1]
    new_ds, new_do, new_inc, new_rm, new_ro, new_rs = pl.pallas_call(
        update_kernel,
        out_shape=(
            f32(levels, rows, columns), f32(1, count), f32(levels, rows, columns),
            f32(levels, rows, columns), f32(1, count), f32(levels, rows, columns),
        ),
        in_specs=[SMEM] + [VMEM] * 3 + [HBM] + [VMEM] * 8,
        out_specs=(HBM, VMEM, HBM, HBM, VMEM, HBM),
        scratch_shapes=[field_s] * 5
        + [pltpu.SemaphoreType.DMA((levels, 4)), pltpu.SemaphoreType.DMA(())],
        compiler_params=params(8),
        cost_estimate=cost(1, 1),
        name="updates",
    )(window_at, all_sums, ds, inc, rm, rs, back, image_model, image_state,
      dual_obs, resid_obs, obs_var, observed)
    return new_ds[None], new_do, new_inc[None], new_rm[None], new_ro, new_rs[None]


def solution(mesh):
    field = P("tm", None, "space", None)
    obs = P("tm", "space")
    shared = P("tm", None)
    return jax.shard_map(
        functools.partial(body, mesh.shape["tm"], mesh.shape["space"]),
        mesh=mesh,
        in_specs=(
            field, field, field, obs, shared, shared, shared,
            field, obs, field, field, obs, field,
        ),
        out_specs=(field, obs, field, field, obs, field),
        check_vma=False,
    )
```
